32 devices in a mesh: groups: 1, tp: 8 (over z, core), dp: 4 (over y, x).
Axes of the slice: x: 2, y: 2, z: 4, core: 2. Of those that a mesh axis runs over, the one named last changes fastest.
Arguments:
- inputs: bfloat16 [512, 12288], P('groups', ('dp', 'tp')), may hold values from -6 to 6
- cotangent: bfloat16 [512, 12288], P('groups', ('dp', 'tp')), may hold values from -6 to 6
- gate_code: bfloat16 [12288, 16384], P('dp', 'tp'), may hold values from -0.0546875 to 0.0546875
- gate_scale: float32 [96, 128], P('dp', 'tp'), may hold values from 0.4 to 2.5
- up_code: bfloat16 [12288, 16384], P('dp', 'tp'), may hold values from -0.0546875 to 0.0546875
- up_scale: float32 [96, 128], P('dp', 'tp'), may hold values from 0.4 to 2.5
- down_code: bfloat16 [16384, 12288], P('tp', 'dp'), may hold values from -0.046875 to 0.046875
- down_scale: float32 [128, 96], P('tp', 'dp'), may hold values from 0.4 to 2.5
Outputs:
- input_grad: bfloat16 [512, 12288], P('groups', ('dp', 'tp'))
The draws below stay inside these ranges and needn't reach their ends.
All inputs are finite; a program needn't handle non-finite values.
Results may differ from the reference program's by a relative error of at most 0.02.
Values may be sent and summed in bfloat16 or wider, within the bound.
No kernel may reach another device: no remote copies, remote signals or barrier semaphores. Data moves between devices by JAX's collectives and lax.ppermute only.
A program may use at most 256 MiB of HBM per device.

```python
import math
import jax
import jax.numpy as jnp
from jax import lax

D = 12288
FF = 16384
BLOCK = 128
SEQ = 512
N_TP = 8
N_DP = 4


def levels(rng, extent, shards, low, largest):
    gain, own = 1.0, jax.random.fold_in(rng, 6)
    for dim, parts in shards:
        draws = jnp.exp(jax.random.uniform(jax.random.fold_in(own, dim), (parts,), jnp.float32, low / len(shards), largest / len(shards)))
        gain = gain * jnp.repeat(draws, extent[dim] // parts).reshape([-1 if axis == dim else 1 for axis in range(len(extent))])
    return gain


def normal_values(own_key, dims, deviation, most, pieces=(), dtype=jnp.bfloat16):
    drawn = jax.random.normal(own_key, dims, jnp.float32) * deviation
    if len(pieces) > 0:
        drawn = levels(own_key, dims, pieces, -0.22, 0.18) * drawn
    return jnp.clip(drawn, min=-most, max=most).astype(dtype)


def setup_inputs(seed: int = 0, part: int = 0) -> dict:
    splits = jax.random.split(jax.random.key(seed), 9)
    part_splits = jax.random.split(jax.random.fold_in(splits[8], part), 9)
    return {
        "inputs": normal_values(part_splits[0], (SEQ, D), 1.0, 6.0, ((1, 32),)),
        "cotangent": normal_values(part_splits[1], (SEQ, D), 1.0, 6.0, ((1, 32),)),
        "gate_code": normal_values(splits[2], (D, FF), D ** -0.5, 0.0546875, ((0, 4), (1, 8))),
        "gate_scale": jnp.clip(jnp.exp(math.log(2.5) - 1.8325814 * jax.random.uniform(splits[3], (D // BLOCK, FF // BLOCK), jnp.float32) ** levels(splits[3], (D // BLOCK, FF // BLOCK), ((0, 4), (1, 8)), -0.2, 0.2)), 0.4, 2.5),
        "up_code": normal_values(splits[4], (D, FF), D ** -0.5, 0.0546875, ((0, 4), (1, 8))),
        "up_scale": jnp.clip(jnp.exp(math.log(2.5) - 1.8325814 * jax.random.uniform(splits[5], (D // BLOCK, FF // BLOCK), jnp.float32) ** levels(splits[5], (D // BLOCK, FF // BLOCK), ((0, 4), (1, 8)), -0.2, 0.2)), 0.4, 2.5),
        "down_code": normal_values(splits[6], (FF, D), FF ** -0.5, 0.046875, ((0, 8), (1, 4))),
        "down_scale": jnp.clip(jnp.exp(math.log(2.5) - 1.8325814 * jax.random.uniform(splits[7], (FF // BLOCK, D // BLOCK), jnp.float32) ** levels(splits[7], (FF // BLOCK, D // BLOCK), ((0, 8), (1, 4)), -0.2, 0.2)), 0.4, 2.5),
    }


def dequantize(code, scale):
    spread = jnp.repeat(jnp.repeat(scale, BLOCK, axis=0), BLOCK, axis=1)
    return (code.astype(jnp.float32) * spread).astype(jnp.bfloat16)


def rounded(value):
    return lax.optimization_barrier(value.astype(jnp.bfloat16)).astype(jnp.float32)


def reference(inputs, cotangent, gate_code, gate_scale, up_code, up_scale, down_code, down_scale):
    gate_weight = dequantize(gate_code, gate_scale)
    up_weight = dequantize(up_code, up_scale)
    down_weight = dequantize(down_code, down_scale)
    width = D // N_DP
    gate_pre = jnp.zeros((SEQ, FF), jnp.float32)
    up_pre = jnp.zeros((SEQ, FF), jnp.float32)
    hidden_grad = jnp.zeros((SEQ, FF), jnp.float32)
    for block_index in range(N_DP):
        lower = block_index * width
        input_slice = inputs[:, lower:lower + width]
        cotan_slice = cotangent[:, lower:lower + width]
        gate_pre = gate_pre + rounded(jnp.dot(input_slice, gate_weight[lower:lower + width], preferred_element_type=jnp.float32))
        up_pre = up_pre + rounded(jnp.dot(input_slice, up_weight[lower:lower + width], preferred_element_type=jnp.float32))
        hidden_grad = hidden_grad + rounded(jnp.dot(cotan_slice, down_weight[:, lower:lower + width].T, preferred_element_type=jnp.float32))
    gate_sig = jax.nn.sigmoid(gate_pre)
    gate_grad = (hidden_grad * up_pre * gate_sig * (1.0 + gate_pre * (1.0 - gate_sig))).astype(jnp.bfloat16)
    up_grad = (hidden_grad * gate_pre * gate_sig).astype(jnp.bfloat16)
    hidden_width = FF // N_TP
    summed = jnp.zeros((SEQ, D), jnp.float32)
    for block_index in range(N_TP):
        lower = block_index * hidden_width
        term = jnp.dot(gate_grad[:, lower:lower + hidden_width], gate_weight[:, lower:lower + hidden_width].T, preferred_element_type=jnp.float32)
        term = term + jnp.dot(up_grad[:, lower:lower + hidden_width], up_weight[:, lower:lower + hidden_width].T, preferred_element_type=jnp.float32)
        summed = summed + rounded(term)
    return summed.astype(jnp.bfloat16)
```

```python
import functools

import jax
import jax.numpy as jnp
from jax import lax
from jax.experimental import pallas as pl
from jax.experimental.pallas import tpu as pltpu
from jax.sharding import PartitionSpec as P

BLOCK = 128
CORES = 2
CHUNKS = 2
BF16 = jnp.bfloat16
F32 = jnp.float32
PARAMS = pltpu.CompilerParams(vmem_limit_bytes=40 << 20)


def tile_of(extent, most):
    best = BLOCK
    for size in range(BLOCK, most + 1, BLOCK):
        if extent % size == 0:
            best = size
    return best


def weight_tile(code, scale_ref, row, column):
    rows = []
    for r in range(code.shape[0] // BLOCK):
        line = [
            (
                code[r * BLOCK : (r + 1) * BLOCK, c * BLOCK : (c + 1) * BLOCK].astype(F32)
                * scale_ref[row + r, column + c]
            ).astype(BF16)
            for c in range(code.shape[1] // BLOCK)
        ]
        rows.append(jnp.concatenate(line, axis=1))
    return jnp.concatenate(rows, axis=0)


def dot(left, right, contract):
    return lax.dot_general(
        left, right, (((1,), (contract,)), ((), ())), preferred_element_type=F32
    )


def prep_kernel(rows, where_ref, inputs_ref, cotangent_ref, *out_refs):
    count = inputs_ref.shape[0] // CHUNKS // rows
    for chunk in range(CHUNKS):
        for q in range(count):
            start = pl.multiple_of((chunk * count + (where_ref[0] ^ q)) * rows, rows)
            out_refs[2 * chunk][q * rows : (q + 1) * rows] = inputs_ref[pl.ds(start, rows)]
            out_refs[2 * chunk + 1][q * rows : (q + 1) * rows] = cotangent_ref[
                pl.ds(start, rows)
            ]


def prepare(where, inputs, cotangent, n_dp):
    seq, width = inputs.shape
    part = jax.ShapeDtypeStruct((seq // CHUNKS, width), inputs.dtype)
    return pl.pallas_call(
        functools.partial(prep_kernel, seq // CHUNKS // n_dp),
        grid_spec=pltpu.PrefetchScalarGridSpec(
            num_scalar_prefetch=1,
            grid=(),
            in_specs=[pl.BlockSpec(memory_space=pltpu.VMEM)] * 2,
            out_specs=[pl.BlockSpec(memory_space=pltpu.VMEM)] * (2 * CHUNKS),
        ),
        out_shape=[part] * (2 * CHUNKS),
        compiler_params=PARAMS,
        name="order_rows",
    )(where, inputs, cotangent)


def forward_kernel(groups, transposed, first, width, where_ref, scale_ref, *refs):
    *x_refs, code_ref, out_refs, x_all = refs[: len(refs) - len(groups) - 1] + (
        refs[len(refs) - len(groups) - 1 : -1],
        refs[-1],
    )
    n = pl.program_id(0)
    x = x_all
    if len(x_refs) == 2:

        @pl.when(n == 0)
        def _():
            count = x_all.shape[1] // (CORES * width)
            for j in range(count):
                for core, x_ref in enumerate(x_refs):
                    place = lax.rem(where_ref[1] + j, count) * CORES + (where_ref[2] ^ core)
                    x_all[:, pl.ds(pl.multiple_of(place * width, width), width)] = x_ref[
                        :, j * width : (j + 1) * width
                    ]
    else:
        x = x_refs[0]
    depth = x_all.shape[1]
    tile = code_ref.shape[0 if transposed else 1]
    step = tile_of(depth, 1024)
    block = (first + n * tile) // BLOCK
    total = None
    for k in range(0, depth, step):
        if transposed:
            weight = weight_tile(code_ref[:, k : k + step], scale_ref, block, k // BLOCK)
        else:
            weight = weight_tile(code_ref[k : k + step, :], scale_ref, k // BLOCK, block)
        term = dot(x[:, k : k + step], weight, 1 if transposed else 0)
        total = term if total is None else total + term
    rows = total.shape[0] // sum(len(group) for group in groups)
    for out_ref, group in zip(out_refs, groups):
        for place, q in enumerate(group):
            out_ref[place * rows : (place + 1) * rows] = total[
                q * rows : (q + 1) * rows
            ].astype(BF16)


def forward(where, scale, x, code, groups, transposed, first, count, width):
    rows = x[0].shape[0]
    depth = code.shape[1 if transposed else 0]
    blocks = sum(len(group) for group in groups)
    tile = tile_of(count, 512)
    base = first // tile
    code_spec = (
        pl.BlockSpec((tile, depth), lambda n, *_: (base + n, 0))
        if transposed
        else pl.BlockSpec((depth, tile), lambda n, *_: (0, base + n))
    )
    heights = [rows * len(group) // blocks for group in groups]
    return pl.pallas_call(
        functools.partial(forward_kernel, groups, transposed, first, width),
        grid_spec=pltpu.PrefetchScalarGridSpec(
            num_scalar_prefetch=2,
            grid=(count // tile,),
            in_specs=[pl.BlockSpec(part.shape, lambda n, *_: (0, 0)) for part in x] + [code_spec],
            out_specs=[pl.BlockSpec((height, tile), lambda n, *_: (0, n)) for height in heights],
            scratch_shapes=[pltpu.VMEM((rows, depth), BF16)],
        ),
        out_shape=[jax.ShapeDtypeStruct((height, count), BF16) for height in heights],
        compiler_params=PARAMS,
        cost_estimate=pl.CostEstimate(
            flops=2 * rows * depth * count, bytes_accessed=2 * depth * count, transcendentals=0
        ),
        name="forward_product",
    )(where, scale, *x, code)


def grads_kernel(pieces, *refs):
    *in_refs, gate_ref, up_ref = refs
    rows, width = gate_ref.shape
    at, sums = 0, []
    for piece in pieces:
        columns = []
        for terms in piece:
            total = None
            for term in in_refs[at : at + terms]:
                value = term[term.shape[0] - rows :].astype(F32)
                total = value if total is None else total + value
            at += terms
            columns.append(total)
        sums.append(columns[0] if len(columns) == 1 else jnp.concatenate(columns, axis=1))
    gate_pre, up_pre, hidden_grad = sums
    gate_sig = jax.nn.sigmoid(gate_pre)
    gate_ref[...] = (
        hidden_grad * up_pre * gate_sig * (1.0 + gate_pre * (1.0 - gate_sig))
    ).astype(BF16)
    up_ref[...] = (hidden_grad * gate_pre * gate_sig).astype(BF16)


def grads(pieces, rows, width):
    flat = [term for piece in pieces for part in piece for term in part]
    out = jax.ShapeDtypeStruct((rows, width), BF16)
    return pl.pallas_call(
        functools.partial(grads_kernel, [[len(part) for part in piece] for piece in pieces]),
        in_specs=[pl.BlockSpec(memory_space=pltpu.VMEM)] * len(flat),
        out_specs=[pl.BlockSpec(memory_space=pltpu.VMEM)] * 2,
        out_shape=[out, out],
        compiler_params=PARAMS,
        name="hidden_grads",
    )(*flat)


def backward_kernel(blocks, relative, where_ref, gate_scale_ref, up_scale_ref, *refs):
    gate_refs, up_refs = refs[:blocks], refs[blocks : 2 * blocks]
    gate_code_ref, up_code_ref = refs[2 * blocks : 2 * blocks + 2]
    *out_refs, gate_all, up_all, total_ref = refs[2 * blocks + 2 :]
    rows = gate_refs[0].shape[0]
    n = pl.program_id(0)

    @pl.when(n == 0)
    def _():
        for q in range(blocks):
            gate_all[q * rows : (q + 1) * rows] = gate_refs[q][...]
            up_all[q * rows : (q + 1) * rows] = up_refs[q][...]

    tile, depth = gate_code_ref.shape
    place = lax.rem(where_ref[1] + n, pl.num_programs(0)) if relative else n
    block = place * (tile // BLOCK)
    step = tile_of(depth, 1024)
    total = None
    for k in range(0, depth, step):
        for left, code_ref, scale_ref in (
            (gate_all, gate_code_ref, gate_scale_ref),
            (up_all, up_code_ref, up_scale_ref),
        ):
            weight = weight_tile(code_ref[:, k : k + step], scale_ref, block, k // BLOCK)
            term = dot(left[:, k : k + step], weight, 1)
            total = term if total is None else total + term
    if relative:
        width = tile // CORES
        total_ref[...] = total.astype(BF16)
        for out_ref, core in zip(out_refs, (where_ref[2], 1 - where_ref[2])):
            out_ref[...] = total_ref[:, pl.ds(pl.multiple_of(core * width, width), width)]
    else:
        out_refs[0][...] = total.astype(BF16)


def backward(where, gate_scale, up_scale, gate, up, gate_code, up_code, tiles):
    depth_rows, depth = gate_code.shape
    blocks, rows = len(gate), gate[0].shape[0] * len(gate)
    relative = tiles is not None
    tile = depth_rows // tiles if relative else tile_of(depth_rows, 512)
    steps = depth_rows // tile
    outs = CORES if relative else 1

    def code_place(n, where_ref, *_):
        return (lax.rem(where_ref[1] + n, steps) if relative else n, 0)

    return pl.pallas_call(
        functools.partial(backward_kernel, blocks, relative),
        grid_spec=pltpu.PrefetchScalarGridSpec(
            num_scalar_prefetch=3,
            grid=(steps,),
            in_specs=[pl.BlockSpec(part.shape, lambda n, *_: (0, 0)) for part in (*gate, *up)]
            + [pl.BlockSpec((tile, depth), code_place)] * 2,
            out_specs=[pl.BlockSpec((rows, tile // outs), lambda n, *_: (0, n))] * outs,
            scratch_shapes=[pltpu.VMEM((rows, depth), BF16)] * 2 + [pltpu.VMEM((rows, tile), BF16)],
        ),
        out_shape=[jax.ShapeDtypeStruct((rows, depth_rows // outs), BF16)] * outs,
        compiler_params=PARAMS,
        cost_estimate=pl.CostEstimate(
            flops=4 * rows * depth * depth_rows,
            bytes_accessed=4 * depth * depth_rows,
            transcendentals=0,
        ),
        name="backward_product",
    )(where, gate_scale, up_scale, *gate, *up, gate_code, up_code)


def pair_kernel(own_ref, other_ref, *out_refs):
    width = out_refs[0].shape[1]
    for j, out_ref in enumerate(out_refs):
        columns = slice((j + 1) * width, (j + 2) * width)
        out_ref[...] = (own_ref[:, columns].astype(F32) + other_ref[:, columns].astype(F32)).astype(BF16)


def pair_sums(own, other, count):
    rows, width = own.shape[0], own.shape[1] // count
    return pl.pallas_call(
        pair_kernel,
        in_specs=[pl.BlockSpec(memory_space=pltpu.VMEM)] * 2,
        out_specs=[pl.BlockSpec(memory_space=pltpu.VMEM)] * (count - 1),
        out_shape=[jax.ShapeDtypeStruct((rows, width), BF16)] * (count - 1),
        compiler_params=PARAMS,
        name="pair_sums",
    )(own, other)


def final_kernel(blocks, where_ref, *refs):
    *in_refs, out_ref = refs
    rows = in_refs[0].shape[0] // blocks
    width = out_ref.shape[1]
    for q in range(blocks):
        total = None
        for ref in in_refs:
            value = ref[q * rows : (q + 1) * rows, :width].astype(F32)
            total = value if total is None else total + value
        start = pl.multiple_of((where_ref[0] ^ q) * rows, rows)
        out_ref[pl.ds(start, rows)] = total.astype(BF16)


def final_sum(where, terms, blocks, width):
    rows = terms[0].shape[0]
    first = pl.BlockSpec((rows, width), lambda *_: (0, 0))
    return pl.pallas_call(
        functools.partial(final_kernel, blocks),
        grid_spec=pltpu.PrefetchScalarGridSpec(
            num_scalar_prefetch=1,
            grid=(1,),
            in_specs=[first] * len(terms),
            out_specs=first,
        ),
        out_shape=jax.ShapeDtypeStruct((rows, width), BF16),
        compiler_params=PARAMS,
        name="final_sum",
    )(where, *terms)


def local(
    n_tp, n_dp, inputs, cotangent, gate_code, gate_scale, up_code, up_scale, down_code, down_scale
):
    n_z = n_tp // CORES
    width = inputs.shape[1]
    hidden = gate_code.shape[1]
    bits = [1 << i for i in range(n_dp.bit_length() - 1)]
    by_blocks = width % BLOCK == 0 and n_tp % CORES == 0
    dp, tp = lax.axis_index("dp"), lax.axis_index("tp")
    place, core = tp // CORES, tp % CORES
    where = jnp.stack([dp, place, core]).astype(jnp.int32)

    def exchange(value, bit):
        return lax.ppermute(value, "dp", [(i, i ^ bit) for i in range(n_dp)])

    def swap_cores(value):
        return lax.ppermute(value, "tp", [(i, i ^ 1) for i in range(n_tp)])

    def gather(piece):
        if not by_blocks:
            return [lax.all_gather(piece, "tp", axis=1, tiled=True)]
        below, above = [piece], [piece]
        for s in range(1, n_z):
            ups = [z for z in range(n_z - 1) if z >= s - 1]
            downs = [z for z in range(1, n_z) if z <= n_z - s]
            pairs = lambda froms, by: [
                ((z * CORES + c), ((z + by) * CORES + c)) for z in froms for c in range(CORES)
            ]
            below.append(lax.ppermute(below[-1], "tp", pairs(ups, 1)))
            above.append(lax.ppermute(above[-1], "tp", pairs(downs, -1)))
        own = [piece] + [
            jnp.where(place + j < n_z, above[j], below[n_z - j]) for j in range(1, n_z)
        ]
        own = jnp.concatenate(own, axis=1)
        return [own, swap_cores(own)]

    def order_groups(order):
        rest, groups = list(range(n_dp)), []
        for bit in order:
            keep = [q for q in rest if not q & bit]
            groups.append((bit, keep))
            rest = keep
        stays, sends = [0], []
        for bit, _ in reversed(groups):
            sends.append([q | bit for q in stays])
            stays = sends[-1] + stays
        return sends[::-1] + [[0]]

    def reduce(parts, order):
        terms = []
        parts = list(parts)
        rows = parts[-1].shape[0]
        for step, bit in enumerate(order):
            got = exchange(parts[step], bit)
            at = 0
            for later in range(step + 1, len(parts) - 1):
                height = parts[later].shape[0]
                parts[later] = (
                    parts[later].astype(F32) + got[at : at + height].astype(F32)
                ).astype(BF16)
                at += height
            terms.append(got)
        return [parts[-1]] + terms

    def gather_rows(value, order):
        have = {0: value}
        for bit in order:
            for q in list(have):
                have[q | bit] = exchange(have[q], bit)
        return [have[q] for q in range(n_dp)]

    one, two = bits, bits[::-1]
    half = hidden // 2
    pieces = prepare(where, inputs, cotangent, n_dp)
    outs = []
    for chunk in range(CHUNKS):
        x_inputs = gather(pieces[2 * chunk])
        x_cotan = gather(pieces[2 * chunk + 1])
        product = lambda x, code, scale, order, transposed, first, count: reduce(
            forward(where, scale, x, code, order_groups(order), transposed, first, count, width),
            order,
        )
        gate_terms = [product(x_inputs, gate_code, gate_scale, one, False, 0, hidden)]
        up_terms = [product(x_inputs, up_code, up_scale, two, False, 0, hidden)]
        hidden_terms = [
            product(x_cotan, down_code, down_scale, one, True, 0, half),
            product(x_cotan, down_code, down_scale, two, True, half, half),
        ]
        rows = inputs.shape[0] // CHUNKS // n_dp
        gate_grad, up_grad = grads([gate_terms, up_terms, hidden_terms], rows, hidden)
        gate_all, up_all = gather_rows(gate_grad, one), gather_rows(up_grad, two)
        partial = backward(
            where, gate_scale, up_scale, gate_all, up_all, gate_code, up_code,
            n_z if by_blocks else None,
        )
        if by_blocks:
            own, other = partial
            other = swap_cores(other)
            sums = pair_sums(own, other, n_z)
            terms = [own, other] + [
                lax.ppermute(
                    part,
                    "tp",
                    [(i, (i + (j + 1) * CORES) % n_tp) for i in range(n_tp)],
                )
                for j, part in enumerate(sums)
            ]
            outs.append(final_sum(where, terms, n_dp, width))
        else:
            summed = lax.psum_scatter(partial[0], "tp", scatter_dimension=1, tiled=True)
            outs.append(final_sum(where, [summed], n_dp, width))
    return jnp.concatenate(outs, axis=0)


def solution(mesh):
    placed = (
        P("groups", ("dp", "tp")),
        P("groups", ("dp", "tp")),
        P("dp", "tp"),
        P("dp", "tp"),
        P("dp", "tp"),
        P("dp", "tp"),
        P("tp", "dp"),
        P("tp", "dp"),
    )
    return jax.shard_map(
        functools.partial(local, mesh.shape["tp"], mesh.shape["dp"]),
        mesh=mesh,
        in_specs=placed,
        out_specs=P("groups", ("dp", "tp")),
        check_vma=False,
    )
```

```python
import functools

import jax
import jax.numpy as jnp
from jax import lax
from jax.experimental import pallas as pl
from jax.experimental.pallas import tpu as pltpu
from jax.sharding import PartitionSpec as P

BLOCK = 128
CORES = 2
CHUNKS = 2
BF16 = jnp.bfloat16
F32 = jnp.float32
PARAMS = pltpu.CompilerParams(vmem_limit_bytes=8 << 20)
VMEM = pl.BlockSpec(memory_space=pltpu.VMEM)
SMEM = pl.BlockSpec(memory_space=pltpu.SMEM)


def tile_of(extent, most):
    best = BLOCK
    for size in range(BLOCK, most + 1, BLOCK):
        if extent % size == 0:
            best = size
    return best


def dot(left, right, contract):
    return lax.dot_general(
        left, right, (((1,), (contract,)), ((), ())), preferred_element_type=F32
    )


def cost(rows, depth, columns):
    return pl.CostEstimate(
        flops=1024, bytes_accessed=1024, transcendentals=0
    )


def array(rows, columns):
    return jax.ShapeDtypeStruct((rows, columns), BF16)


def reversed_bits(q, count):
    width = count.bit_length() - 1
    return sum(((q >> i) & 1) << (width - 1 - i) for i in range(width))


def block_of(q, count, core):
    return q + core * (reversed_bits(q, count) - q)


def weight_kernel(turned, code_ref, scale_ref, weight_ref, buffer, sems):
    slots, rows = buffer.shape[:2]
    count = code_ref.shape[0] // rows

    def fetch(i):
        slot = lax.rem(i, slots)
        return pltpu.make_async_copy(
            code_ref.at[pl.ds(pl.multiple_of(i * rows, rows), rows)], buffer.at[slot], sems.at[slot]
        )

    for i in range(min(slots, count)):
        fetch(i).start()

    def body(i, carry):
        fetch(i).wait()
        slot = lax.rem(i, slots)
        start = pl.multiple_of(i * rows, rows)
        for c in range(code_ref.shape[1] // BLOCK):
            columns = slice(c * BLOCK, (c + 1) * BLOCK)
            weight_ref[pl.ds(start, rows), columns] = (
                buffer[slot, :, columns].astype(F32) * (scale_ref[c, i] if turned else scale_ref[i, c])
            ).astype(BF16)

        @pl.when(i + slots < count)
        def _():
            fetch(i + slots).start()

        return carry

    lax.fori_loop(0, count, body, 0)


def weight(code, scale, turned):
    slots = 6
    scale = scale.T if turned else scale
    return pl.pallas_call(
        functools.partial(weight_kernel, turned),
        in_specs=[pl.BlockSpec(memory_space=pltpu.HBM), SMEM],
        out_specs=VMEM,
        out_shape=pltpu.VMEM(code.shape, BF16),
        scratch_shapes=[
            pltpu.VMEM((slots, BLOCK, code.shape[1]), BF16),
            pltpu.SemaphoreType.DMA((slots,)),
        ],
        compiler_params=pltpu.CompilerParams(vmem_limit_bytes=10 << 20),
        cost_estimate=pl.CostEstimate(
            flops=0, bytes_accessed=code.size // 4096, transcendentals=0
        ),
        name="scaled_weight",
    )(pltpu.with_memory_space_constraint(code, pltpu.HBM), scale)


def prep_kernel(rows, where_ref, inputs_ref, cotangent_ref, *refs):
    *out_refs, sem = refs
    count = inputs_ref.shape[0] // CHUNKS // rows
    copies = []
    for at, out_ref in enumerate(out_refs):
        for q in range(count):
            start = pl.multiple_of((at // 2 * count + (where_ref[0] ^ q)) * rows, rows)
            copies.append(
                pltpu.make_async_copy(
                    (inputs_ref, cotangent_ref)[at % 2].at[pl.ds(start, rows)],
                    out_ref.at[pl.ds(q * rows, rows)],
                    sem.at[len(copies)],
                )
            )
            copies[-1].start()
    for copy in copies:
        copy.wait()


def prepare(where, inputs, cotangent, n_dp):
    seq, width = inputs.shape
    return pl.pallas_call(
        functools.partial(prep_kernel, seq // CHUNKS // n_dp),
        in_specs=[SMEM] + [pl.BlockSpec(memory_space=pltpu.HBM)] * 2,
        out_specs=[VMEM] * (2 * CHUNKS),
        out_shape=[array(seq // CHUNKS, width)] * (2 * CHUNKS),
        scratch_shapes=[pltpu.SemaphoreType.DMA((2 * CHUNKS * n_dp,))],
        compiler_params=PARAMS,
        name="order_rows",
    )(
        where,
        pltpu.with_memory_space_constraint(inputs, pltpu.HBM),
        pltpu.with_memory_space_constraint(cotangent, pltpu.HBM),
    )


def join_kernel(*refs):
    *part_refs, out_ref = refs
    width = part_refs[0].shape[1]
    for j, part_ref in enumerate(part_refs):
        out_ref[:, j * width : (j + 1) * width] = part_ref[...]


def join(parts):
    rows, width = parts[0].shape
    return pl.pallas_call(
        join_kernel,
        in_specs=[VMEM] * len(parts),
        out_specs=VMEM,
        out_shape=array(rows, width * len(parts)),
        compiler_params=PARAMS,
        name="join",
    )(*parts)


def join_four_kernel(where_ref, own_ref, two_ref, near_ref, middle_ref, passed_ref, out_ref):
    width = own_ref.shape[1]
    place = where_ref[1]
    out_ref[:, :width] = own_ref[...]
    out_ref[:, 2 * width : 3 * width] = two_ref[...]
    odd = lax.rem(place, 2)
    out_ref[:, pl.ds(pl.multiple_of((1 + 2 * odd) * width, width), width)] = near_ref[...]
    rest = pl.ds(pl.multiple_of((3 - 2 * odd) * width, width), width)
    inner = jnp.logical_or(place == 1, place == 2)

    @pl.when(inner)
    def _():
        out_ref[:, rest] = middle_ref[...]

    @pl.when(jnp.logical_not(inner))
    def _():
        out_ref[:, rest] = passed_ref[...]


def join_four(where, parts):
    rows, width = parts[0].shape
    return pl.pallas_call(
        join_four_kernel,
        in_specs=[SMEM] + [VMEM] * len(parts),
        out_specs=VMEM,
        out_shape=array(rows, 4 * width),
        compiler_params=PARAMS,
        name="join",
    )(where, *parts)


def assemble(width, blocks, where_ref, x_refs, x_all):
    rows = x_all.shape[0] // blocks
    for q in range(blocks):
        start = pl.multiple_of(block_of(q, blocks, where_ref[2]) * rows, rows)
        own = slice(q * rows, (q + 1) * rows)
        if len(x_refs) == 1:
            x_all[own] = x_refs[0][pl.ds(start, rows)]
            continue
        count = x_all.shape[1] // (CORES * width)
        for j in range(count):
            for core, x_ref in enumerate(x_refs):
                place = lax.rem(where_ref[1] + j, count) * CORES + (where_ref[2] ^ core)
                x_all[own, pl.ds(pl.multiple_of(place * width, width), width)] = x_ref[
                    pl.ds(start, rows), j * width : (j + 1) * width
                ]


def forward_kernel(groups, contract, width, count, where_ref, *refs):
    outs = len(groups)
    x_refs, weight_refs = refs[: -outs - 1 - count], refs[-outs - 1 - count : -outs - 1]
    out_refs, x_all = refs[-outs - 1 : -1], refs[-1]
    blocks = sum(len(group) for group in groups)
    assemble(width, blocks, where_ref, x_refs, x_all)
    columns = out_refs[0].shape[1] // count
    rows = x_all.shape[0] // blocks
    tile = tile_of(columns, 512)
    for at, weight_ref in enumerate(weight_refs):
        for n in range(0, columns, tile):
            part = weight_ref[n : n + tile, :] if contract else weight_ref[:, n : n + tile]
            total = dot(x_all[...], part, contract).astype(BF16)
            place = slice(at * columns + n, at * columns + n + tile)
            for out_ref, group in zip(out_refs, groups):
                for i, q in enumerate(group):
                    out_ref[i * rows : (i + 1) * rows, place] = total[q * rows : (q + 1) * rows]


def forward(where, x, weights, groups, contract, width):
    rows, blocks = x[0].shape[0], sum(len(group) for group in groups)
    depth, columns = weights[0].shape[contract], weights[0].shape[1 - contract]
    outs = [array(rows * len(group) // blocks, columns * len(weights)) for group in groups]
    return pl.pallas_call(
        functools.partial(forward_kernel, groups, contract, width, len(weights)),
        in_specs=[SMEM] + [VMEM] * (len(x) + len(weights)),
        out_specs=[VMEM] * len(outs),
        out_shape=outs,
        scratch_shapes=[pltpu.VMEM((rows, depth), BF16)],
        compiler_params=PARAMS,
        cost_estimate=cost(rows, depth, columns),
        name="forward_product",
    )(where, *x, *(pltpu.with_memory_space_constraint(part, pltpu.VMEM) for part in weights))


def streamed_kernel(groups, width, where_ref, scale_ref, *refs):
    outs = len(groups)
    x_refs, code_ref = refs[: -outs - 4], refs[-outs - 4]
    out_refs, (x_all, buffer, sems) = refs[-outs - 3 : -3], refs[-3:]
    slots, tile, depth = buffer.shape
    count = code_ref.shape[0] // tile
    blocks = sum(len(group) for group in groups)
    rows = x_all.shape[0] // blocks
    step = tile_of(depth, 512)

    def fetch(i):
        slot = lax.rem(i, slots)
        return pltpu.make_async_copy(
            code_ref.at[pl.ds(pl.multiple_of(i * tile, tile), tile)], buffer.at[slot], sems.at[slot]
        )

    for i in range(min(slots, count)):
        fetch(i).start()
    assemble(width, blocks, where_ref, x_refs, x_all)

    def body(i, carry):
        fetch(i).wait()
        slot = lax.rem(i, slots)
        total = None
        for k in range(0, depth, step):
            lines = []
            for r in range(tile // BLOCK):
                lines.append(
                    jnp.concatenate(
                        [
                            (
                                buffer[slot, r * BLOCK : (r + 1) * BLOCK, c : c + BLOCK].astype(F32)
                                * scale_ref[i * (tile // BLOCK) + r, c // BLOCK]
                            ).astype(BF16)
                            for c in range(k, k + step, BLOCK)
                        ],
                        axis=1,
                    )
                )
            term = dot(x_all[:, k : k + step], jnp.concatenate(lines, axis=0), 1)
            total = term if total is None else total + term
        total = total.astype(BF16)
        columns = pl.ds(pl.multiple_of(i * tile, tile), tile)
        for out_ref, group in zip(out_refs, groups):
            for at, q in enumerate(group):
                out_ref[at * rows : (at + 1) * rows, columns] = total[q * rows : (q + 1) * rows]

        @pl.when(i + slots < count)
        def _():
            fetch(i + slots).start()

        return carry

    lax.fori_loop(0, count, body, 0)


def forward_streamed(where, x, code, scale, groups, width):
    rows, blocks = x[0].shape[0], sum(len(group) for group in groups)
    columns, depth = code.shape
    tile, slots = tile_of(columns, 256), 3
    return pl.pallas_call(
        functools.partial(streamed_kernel, groups, width),
        in_specs=[SMEM] * 2 + [VMEM] * len(x) + [pl.BlockSpec(memory_space=pltpu.HBM)],
        out_specs=[VMEM] * len(groups),
        out_shape=[array(rows * len(group) // blocks, columns) for group in groups],
        scratch_shapes=[
            pltpu.VMEM((rows, depth), BF16),
            pltpu.VMEM((slots, tile, depth), BF16),
            pltpu.SemaphoreType.DMA((slots,)),
        ],
        compiler_params=pltpu.CompilerParams(vmem_limit_bytes=14 << 20),
        cost_estimate=cost(rows, depth, columns),
        name="forward_streamed",
    )(where, scale, *x, pltpu.with_memory_space_constraint(code, pltpu.HBM))


def grads_kernel(both, where_ref, *refs):
    *in_refs, out_ref = refs
    rows, width = out_ref.shape[0], out_ref.shape[1] // 2
    tile = tile_of(width, 512)

    def total(terms, n):
        values = [term[term.shape[0] - rows :, n : n + tile].astype(F32) for term in terms]
        return functools.reduce(lambda left, right: left + right, values)

    for n in range(0, width, tile):
        gate_pre = total(in_refs[:both], n)
        up_pre = total(in_refs[:both], width + n)
        hidden_grad = total(in_refs[both:], n)
        gate_sig = jax.nn.sigmoid(gate_pre)
        out_ref[:, n : n + tile] = (
            hidden_grad * up_pre * gate_sig * (1.0 + gate_pre * (1.0 - gate_sig))
        ).astype(BF16)
        out_ref[:, width + n : width + n + tile] = (hidden_grad * gate_pre * gate_sig).astype(BF16)


def grads(where, gate_up, hidden_terms, rows, width):
    return pl.pallas_call(
        functools.partial(grads_kernel, len(gate_up)),
        in_specs=[SMEM] + [VMEM] * (len(gate_up) + len(hidden_terms)),
        out_specs=VMEM,
        out_shape=array(rows, 2 * width),
        compiler_params=PARAMS,
        name="hidden_grads",
    )(where, *gate_up, *hidden_terms)


def backward_kernel(places, total_places, where_ref, *refs):
    outs = CORES if total_places else 1
    *grad_refs, gate_ref, up_ref = refs[: -3 - outs]
    *out_refs, gate_all, up_all, total_ref = refs[-3 - outs :]
    blocks, rows = len(grad_refs), grad_refs[0].shape[0]
    depth = gate_all.shape[1]
    for q, grad_ref in enumerate(grad_refs):
        start = pl.multiple_of(block_of(q, blocks, where_ref[2]) * rows, rows)
        gate_all[pl.ds(start, rows)] = grad_ref[:, :depth]
        up_all[pl.ds(start, rows)] = grad_ref[:, depth:]
    tile = total_ref.shape[1]
    for at, j in enumerate(places):
        place = lax.rem(where_ref[1] + j, total_places) if total_places else j
        part = pl.ds(pl.multiple_of(place * tile, tile), tile)
        total = dot(gate_all[...], gate_ref[part, :], 1) + dot(up_all[...], up_ref[part, :], 1)
        if total_places:
            width = tile // CORES
            total_ref[...] = total.astype(BF16)
            for out_ref, core in zip(out_refs, (where_ref[2], 1 - where_ref[2])):
                out_ref[:, at * width : (at + 1) * width] = total_ref[
                    :, pl.ds(pl.multiple_of(core * width, width), width)
                ]
        else:
            out_refs[0][:, at * tile : (at + 1) * tile] = total.astype(BF16)


def backward(where, grad_parts, gate_weight, up_weight, places, total_places):
    columns, depth = gate_weight.shape
    rows = grad_parts[0].shape[0] * len(grad_parts)
    outs = CORES if total_places else 1
    tile = columns // total_places if total_places else tile_of(columns, 512)
    places = places if total_places else range(columns // tile)
    return pl.pallas_call(
        functools.partial(backward_kernel, places, total_places),
        in_specs=[SMEM] + [VMEM] * (len(grad_parts) + 2),
        out_specs=[VMEM] * outs,
        out_shape=[array(rows, tile * len(places) // outs)] * outs,
        scratch_shapes=[pltpu.VMEM((rows, depth), BF16)] * 2 + [pltpu.VMEM((rows, tile), BF16)],
        compiler_params=PARAMS,
        cost_estimate=cost(rows, 2 * depth, tile * len(places)),
        name="backward_product",
    )(
        where,
        *grad_parts,
        pltpu.with_memory_space_constraint(gate_weight, pltpu.VMEM),
        pltpu.with_memory_space_constraint(up_weight, pltpu.VMEM),
    )


def pair_kernel(own_ref, other_ref, *out_refs):
    width = out_refs[0].shape[1]
    for j, out_ref in enumerate(out_refs):
        columns = slice(j * width, (j + 1) * width)
        out_ref[...] = (own_ref[:, columns].astype(F32) + other_ref[:, columns].astype(F32)).astype(
            BF16
        )


def pair_sums(own, other, count, width):
    rows = own.shape[0]
    return pl.pallas_call(
        pair_kernel,
        in_specs=[VMEM] * 2,
        out_specs=[VMEM] * count,
        out_shape=[array(rows, width)] * count,
        compiler_params=PARAMS,
        name="pair_sums",
    )(own, other)


def final_kernel(blocks, done, where_ref, *refs):
    done_refs, in_refs, out_ref = refs[:done], refs[done:-1], refs[-1]
    rows = in_refs[0].shape[0] // blocks
    width = out_ref.shape[1]
    at = 0
    for done_ref in done_refs:
        out_ref[at : at + done_ref.shape[0]] = done_ref[...]
        at += done_ref.shape[0]
    for q in range(blocks):
        total = None
        for ref in in_refs:
            value = ref[q * rows : (q + 1) * rows, ref.shape[1] - width :].astype(F32)
            total = value if total is None else total + value
        start = pl.multiple_of(at + (where_ref[0] ^ q) * rows, rows)
        out_ref[pl.ds(start, rows)] = total.astype(BF16)


def final_sum(where, done, terms, blocks, width):
    rows = terms[0].shape[0] + sum(part.shape[0] for part in done)
    return pl.pallas_call(
        functools.partial(final_kernel, blocks, len(done)),
        in_specs=[SMEM] + [VMEM] * (len(done) + len(terms)),
        out_specs=VMEM,
        out_shape=array(rows, width),
        compiler_params=PARAMS,
        name="final_sum",
    )(where, *done, *terms)


def local(
    n_tp, n_dp, inputs, cotangent, gate_code, gate_scale, up_code, up_scale, down_code, down_scale
):
    n_z = n_tp // CORES
    width = inputs.shape[1]
    hidden = gate_code.shape[1]
    steps = n_dp.bit_length() - 1
    by_blocks = width % BLOCK == 0
    tp = lax.axis_index("tp")
    where = jnp.stack([lax.axis_index("dp"), tp // CORES, tp % CORES]).astype(jnp.int32)

    def exchange(value, step):
        pairs = []
        for i in range(n_tp):
            bit = 1 << (step if i % CORES == 0 else steps - 1 - step)
            pairs += [(i * n_dp + k, i * n_dp + (k ^ bit)) for k in range(n_dp)]
        return lax.ppermute(value, ("tp", "dp"), pairs)

    def swap_cores(value):
        return lax.ppermute(value, "tp", [(i, i ^ 1) for i in range(n_tp)])

    def along(value, places):
        return lax.ppermute(
            value, "tp", [(i, (i + places * CORES) % n_tp) for i in range(n_tp)]
        )

    def between(value, pairs):
        return lax.ppermute(
            value,
            "tp",
            [(i * CORES + c, k * CORES + c) for i, k in pairs for c in range(CORES)],
        )

    hops = by_blocks and n_z == 4

    def set_out(piece):
        if not by_blocks:
            return [lax.all_gather(piece, "tp", axis=1, tiled=True)]
        if hops:
            return [along(piece, 2)]
        return [along(piece, n_z - j) for j in range(1, n_z)]

    def near(piece, got):
        return [*got, between(piece, [(0, 1), (1, 0), (2, 3), (3, 2)])] if hops else got

    def pass_on(piece, got):
        if not hops:
            return got
        return [*got, between(piece, [(1, 2), (2, 1)]), between(got[0], [(1, 0), (2, 3)])]

    def arrive(piece, got):
        if not by_blocks:
            return got
        own = join_four(where, (piece, *got)) if hops else join([piece, *got])
        return [own, swap_cores(own)]

    groups, stays = [[0]], [0]
    for step in reversed(range(steps)):
        groups.insert(0, [q | 1 << step for q in stays])
        stays = groups[0] + stays

    def send(parts, step=0):
        return [*parts, exchange(parts[step], step)]

    def take(parts, step=0):
        parts, at = list(parts), 0
        for later in range(step + 1, steps):
            height = parts[later].shape[0]
            came = parts[-1][at : at + height].astype(F32)
            parts[later] = (parts[later].astype(F32) + came).astype(BF16)
            at += height
        return parts

    def settle(parts):
        for step in range(1, steps):
            parts = send(take(parts, step - 1), step)
        return parts

    def terms_of(parts):
        return parts[steps:]

    def start_rows(value):
        return (
            {0: value, 1: exchange(value, 0)},
            {1 << step: exchange(value, step) for step in range(1, steps)},
        )

    def finish_rows(have, late):
        have = dict(have)
        for step in range(1, steps):
            for q in list(have):
                have[q | 1 << step] = exchange(have[q], step) if q else late[1 << step]
        return [have[q] for q in range(n_dp)]

    whole = [[*range(1, n_z), 0]]
    parts_of_z = [[2], [1, 3], [0]] if hops else whole

    def products(grad_parts, places):
        return backward(
            where, grad_parts, gate_weight, up_weight, places, n_z if by_blocks else 0
        )

    def swapped(partial):
        return [partial[0], swap_cores(partial[1])] if by_blocks else partial

    def scatter(partial, places):
        if not by_blocks:
            return [lax.psum_scatter(partial[0], "tp", scatter_dimension=1, tiled=True)]
        away = [j for j in places if j]
        if not away:
            return list(partial)
        sums = pair_sums(*partial, len(away), width)
        terms = [along(part, j) for j, part in zip(away, sums)]
        return terms + (list(partial) if 0 in places else [])

    rows = inputs.shape[0] // CHUNKS // n_dp

    def hold(values):
        nonlocal where
        values, where = lax.optimization_barrier((values, where))
        return values

    in_1, co_1, in_2, co_2 = prepare(where, inputs, cotangent, n_dp)
    got_in_1 = near(in_1, set_out(in_1))
    gate_weight = weight(gate_code, gate_scale, True)
    gate_weight, got_in_1, co_1 = hold((gate_weight, got_in_1, co_1))

    got_in_1 = pass_on(in_1, got_in_1)
    got_co_1 = near(co_1, set_out(co_1))
    up_weight = weight(up_code, up_scale, True)
    up_weight, got_in_1, got_co_1 = hold((up_weight, got_in_1, got_co_1))

    x = arrive(in_1, got_in_1)
    got_co_1 = pass_on(co_1, got_co_1)
    gate_up_1 = forward(where, x, [gate_weight, up_weight], groups, 0, width)
    gate_up_1, got_co_1, in_2 = hold((gate_up_1, got_co_1, in_2))

    gate_up_1 = send(gate_up_1)
    x = arrive(co_1, got_co_1)
    got_in_2 = near(in_2, set_out(in_2))
    hidden_1 = forward_streamed(where, x, down_code, down_scale, groups, width)
    hidden_1, gate_up_1, got_in_2 = hold((hidden_1, gate_up_1, got_in_2))

    hidden_1 = send(hidden_1)
    gate_up_1 = settle(gate_up_1)
    got_in_2 = hold(pass_on(in_2, got_in_2))

    x = arrive(in_2, got_in_2)
    x, co_2, hidden_1 = hold((x, co_2, hidden_1))

    hidden_1 = settle(hidden_1)
    got_co_2 = near(co_2, set_out(co_2))
    gate_up_2 = forward(where, x, [gate_weight, up_weight], groups, 0, width)
    gate_up_2, got_co_2, gate_up_1, hidden_1 = hold((gate_up_2, got_co_2, gate_up_1, hidden_1))

    got_co_2 = pass_on(co_2, got_co_2)
    gate_up_2 = send(gate_up_2)
    grad_1 = grads(where, terms_of(gate_up_1), terms_of(hidden_1), rows, hidden)
    got_co_2, grad_1 = hold((got_co_2, grad_1))

    early_1, late_1 = start_rows(grad_1)
    x = hold(arrive(co_2, got_co_2))

    hidden_2 = forward_streamed(where, x, down_code, down_scale, groups, width)
    hidden_2, gate_up_2 = hold((hidden_2, gate_up_2))

    hidden_2 = send(hidden_2)
    gate_up_2 = settle(gate_up_2)
    early_1 = hold(early_1)

    parts_1 = finish_rows(early_1, late_1)
    parts_1, hidden_2, gate_up_2 = hold((parts_1, hidden_2, gate_up_2))

    hidden_2 = settle(hidden_2)
    partial_1 = products(parts_1, whole[0])
    hidden_2, partial_1 = hold((hidden_2, partial_1))

    partial_1 = swapped(partial_1)
    grad_2 = grads(where, terms_of(gate_up_2), terms_of(hidden_2), rows, hidden)
    early_2, late_2 = start_rows(grad_2)
    terms_1 = scatter(partial_1, whole[0])
    early_2, early = hold((early_2, terms_1[:1]))
    parts_2 = finish_rows(early_2, late_2)
    parts_2, terms_1 = hold((parts_2, [*early, *terms_1[1:]]))

    terms_2 = []
    partial, before = products(parts_2, parts_of_z[0]), parts_of_z[0]
    for places in parts_of_z[1:]:
        following = products(parts_2, places)
        partial, following = hold((swapped(partial), following))
        terms_2 += scatter(partial, before)
        partial, before = following, places
    terms_2 += scatter(swapped(partial), before)
    done = [final_sum(where, [], terms_1, n_dp, width)]
    return final_sum(where, done, terms_2, n_dp, width)


def solution(mesh):
    placed = (
        P("groups", ("dp", "tp")),
        P("groups", ("dp", "tp")),
        P("dp", "tp"),
        P("dp", "tp"),
        P("dp", "tp"),
        P("dp", "tp"),
        P("tp", "dp"),
        P("tp", "dp"),
    )
    return jax.shard_map(
        functools.partial(local, mesh.shape["tp"], mesh.shape["dp"]),
        mesh=mesh,
        in_specs=placed,
        out_specs=P("groups", ("dp", "tp")),
        check_vma=False,
    )
```

```python
import functools

import jax
import jax.numpy as jnp
from jax import lax
from jax.experimental import pallas as pl
from jax.experimental.pallas import tpu as pltpu
from jax.sharding import PartitionSpec as P

BLOCK = 128
CORES = 2
CHUNKS = 2
BF16 = jnp.bfloat16
F32 = jnp.float32
PARAMS = pltpu.CompilerParams(vmem_limit_bytes=8 << 20)
VMEM = pl.BlockSpec(memory_space=pltpu.VMEM)
SMEM = pl.BlockSpec(memory_space=pltpu.SMEM)


def tile_of(extent, most):
    best = BLOCK
    for size in range(BLOCK, most + 1, BLOCK):
        if extent % size == 0:
            best = size
    return best


def dot(left, right, contract):
    return lax.dot_general(
        left, right, (((1,), (contract,)), ((), ())), preferred_element_type=F32
    )


def cost(rows, depth, columns):
    return pl.CostEstimate(
        flops=1024, bytes_accessed=1024, transcendentals=0
    )


def array(rows, columns):
    return jax.ShapeDtypeStruct((rows, columns), BF16)


def reversed_bits(q, count):
    width = count.bit_length() - 1
    return sum(((q >> i) & 1) << (width - 1 - i) for i in range(width))


def block_of(q, count, core):
    return q + core * (reversed_bits(q, count) - q)


def weight_kernel(turned, code_ref, scale_ref, weight_ref, buffer, sems):
    slots, rows = buffer.shape[:2]
    count = code_ref.shape[0] // rows

    def fetch(i):
        slot = lax.rem(i, slots)
        return pltpu.make_async_copy(
            code_ref.at[pl.ds(pl.multiple_of(i * rows, rows), rows)], buffer.at[slot], sems.at[slot]
        )

    for i in range(min(slots, count)):
        fetch(i).start()

    def body(i, carry):
        fetch(i).wait()
        slot = lax.rem(i, slots)
        start = pl.multiple_of(i * rows, rows)
        for c in range(code_ref.shape[1] // BLOCK):
            columns = slice(c * BLOCK, (c + 1) * BLOCK)
            weight_ref[pl.ds(start, rows), columns] = (
                buffer[slot, :, columns].astype(F32) * (scale_ref[c, i] if turned else scale_ref[i, c])
            ).astype(BF16)

        @pl.when(i + slots < count)
        def _():
            fetch(i + slots).start()

        return carry

    lax.fori_loop(0, count, body, 0)


def weight(code, scale, turned):
    slots = 6
    scale = scale.T if turned else scale
    return pl.pallas_call(
        functools.partial(weight_kernel, turned),
        in_specs=[pl.BlockSpec(memory_space=pltpu.HBM), SMEM],
        out_specs=VMEM,
        out_shape=pltpu.VMEM(code.shape, BF16),
        scratch_shapes=[
            pltpu.VMEM((slots, BLOCK, code.shape[1]), BF16),
            pltpu.SemaphoreType.DMA((slots,)),
        ],
        compiler_params=pltpu.CompilerParams(vmem_limit_bytes=10 << 20),
        cost_estimate=pl.CostEstimate(
            flops=0, bytes_accessed=code.size // 4096, transcendentals=0
        ),
        name="scaled_weight",
    )(pltpu.with_memory_space_constraint(code, pltpu.HBM), scale)


def prep_kernel(rows, where_ref, inputs_ref, cotangent_ref, *refs):
    *out_refs, sem = refs
    count = inputs_ref.shape[0] // CHUNKS // rows
    copies = []
    for at, out_ref in enumerate(out_refs):
        for q in range(count):
            start = pl.multiple_of((at // 2 * count + (where_ref[0] ^ q)) * rows, rows)
            copies.append(
                pltpu.make_async_copy(
                    (inputs_ref, cotangent_ref)[at % 2].at[pl.ds(start, rows)],
                    out_ref.at[pl.ds(q * rows, rows)],
                    sem.at[len(copies)],
                )
            )
            copies[-1].start()
    for copy in copies:
        copy.wait()


def prepare(where, inputs, cotangent, n_dp):
    seq, width = inputs.shape
    return pl.pallas_call(
        functools.partial(prep_kernel, seq // CHUNKS // n_dp),
        in_specs=[SMEM] + [pl.BlockSpec(memory_space=pltpu.HBM)] * 2,
        out_specs=[VMEM] * (2 * CHUNKS),
        out_shape=[array(seq // CHUNKS, width)] * (2 * CHUNKS),
        scratch_shapes=[pltpu.SemaphoreType.DMA((2 * CHUNKS * n_dp,))],
        compiler_params=PARAMS,
        name="order_rows",
    )(
        where,
        pltpu.with_memory_space_constraint(inputs, pltpu.HBM),
        pltpu.with_memory_space_constraint(cotangent, pltpu.HBM),
    )


def join_kernel(*refs):
    *part_refs, out_ref = refs
    width = part_refs[0].shape[1]
    for j, part_ref in enumerate(part_refs):
        out_ref[:, j * width : (j + 1) * width] = part_ref[...]


def join(parts):
    rows, width = parts[0].shape
    return pl.pallas_call(
        join_kernel,
        in_specs=[VMEM] * len(parts),
        out_specs=VMEM,
        out_shape=array(rows, width * len(parts)),
        compiler_params=PARAMS,
        name="join",
    )(*parts)


def join_four_kernel(where_ref, own_ref, two_ref, near_ref, middle_ref, passed_ref, out_ref):
    width = own_ref.shape[1]
    place = where_ref[1]
    out_ref[:, :width] = own_ref[...]
    out_ref[:, 2 * width : 3 * width] = two_ref[...]
    odd = lax.rem(place, 2)
    out_ref[:, pl.ds(pl.multiple_of((1 + 2 * odd) * width, width), width)] = near_ref[...]
    rest = pl.ds(pl.multiple_of((3 - 2 * odd) * width, width), width)
    inner = jnp.logical_or(place == 1, place == 2)

    @pl.when(inner)
    def _():
        out_ref[:, rest] = middle_ref[...]

    @pl.when(jnp.logical_not(inner))
    def _():
        out_ref[:, rest] = passed_ref[...]


def join_four(where, parts):
    rows, width = parts[0].shape
    return pl.pallas_call(
        join_four_kernel,
        in_specs=[SMEM] + [VMEM] * len(parts),
        out_specs=VMEM,
        out_shape=array(rows, 4 * width),
        compiler_params=PARAMS,
        name="join",
    )(where, *parts)


def assemble(width, blocks, where_ref, x_refs, x_all):
    rows = x_all.shape[0] // blocks
    for q in range(blocks):
        start = pl.multiple_of(block_of(q, blocks, where_ref[2]) * rows, rows)
        own = slice(q * rows, (q + 1) * rows)
        if len(x_refs) == 1:
            x_all[own] = x_refs[0][pl.ds(start, rows)]
            continue
        count = x_all.shape[1] // (CORES * width)
        for j in range(count):
            for core, x_ref in enumerate(x_refs):
                place = lax.rem(where_ref[1] + j, count) * CORES + (where_ref[2] ^ core)
                x_all[own, pl.ds(pl.multiple_of(place * width, width), width)] = x_ref[
                    pl.ds(start, rows), j * width : (j + 1) * width
                ]


def forward_kernel(groups, contract, width, count, where_ref, *refs):
    outs = len(groups)
    x_refs, weight_refs = refs[: -outs - 1 - count], refs[-outs - 1 - count : -outs - 1]
    out_refs, x_all = refs[-outs - 1 : -1], refs[-1]
    blocks = sum(len(group) for group in groups)
    assemble(width, blocks, where_ref, x_refs, x_all)
    columns = out_refs[0].shape[1] // count
    rows = x_all.shape[0] // blocks
    tile = tile_of(columns, 512)
    for at, weight_ref in enumerate(weight_refs):
        for n in range(0, columns, tile):
            part = weight_ref[n : n + tile, :] if contract else weight_ref[:, n : n + tile]
            total = dot(x_all[...], part, contract).astype(BF16)
            place = slice(at * columns + n, at * columns + n + tile)
            for out_ref, group in zip(out_refs, groups):
                for i, q in enumerate(group):
                    out_ref[i * rows : (i + 1) * rows, place] = total[q * rows : (q + 1) * rows]


def forward(where, x, weights, groups, contract, width):
    rows, blocks = x[0].shape[0], sum(len(group) for group in groups)
    depth, columns = weights[0].shape[contract], weights[0].shape[1 - contract]
    outs = [array(rows * len(group) // blocks, columns * len(weights)) for group in groups]
    return pl.pallas_call(
        functools.partial(forward_kernel, groups, contract, width, len(weights)),
        in_specs=[SMEM] + [VMEM] * (len(x) + len(weights)),
        out_specs=[VMEM] * len(outs),
        out_shape=outs,
        scratch_shapes=[pltpu.VMEM((rows, depth), BF16)],
        compiler_params=PARAMS,
        cost_estimate=cost(rows, depth, columns),
        name="forward_product",
    )(where, *x, *(pltpu.with_memory_space_constraint(part, pltpu.VMEM) for part in weights))


def streamed_kernel(groups, width, where_ref, scale_ref, *refs):
    outs = len(groups)
    x_refs, code_ref = refs[: -outs - 4], refs[-outs - 4]
    out_refs, (x_all, buffer, sems) = refs[-outs - 3 : -3], refs[-3:]
    slots, tile, depth = buffer.shape
    count = code_ref.shape[0] // tile
    blocks = sum(len(group) for group in groups)
    rows = x_all.shape[0] // blocks
    step = tile_of(depth, 512)

    def fetch(i):
        slot = lax.rem(i, slots)
        return pltpu.make_async_copy(
            code_ref.at[pl.ds(pl.multiple_of(i * tile, tile), tile)], buffer.at[slot], sems.at[slot]
        )

    for i in range(min(slots, count)):
        fetch(i).start()
    assemble(width, blocks, where_ref, x_refs, x_all)

    def body(i, carry):
        fetch(i).wait()
        slot = lax.rem(i, slots)
        total = None
        for k in range(0, depth, step):
            lines = []
            for r in range(tile // BLOCK):
                lines.append(
                    jnp.concatenate(
                        [
                            (
                                buffer[slot, r * BLOCK : (r + 1) * BLOCK, c : c + BLOCK].astype(F32)
                                * scale_ref[i * (tile // BLOCK) + r, c // BLOCK]
                            ).astype(BF16)
                            for c in range(k, k + step, BLOCK)
                        ],
                        axis=1,
                    )
                )
            term = dot(x_all[:, k : k + step], jnp.concatenate(lines, axis=0), 1)
            total = term if total is None else total + term
        total = total.astype(BF16)
        columns = pl.ds(pl.multiple_of(i * tile, tile), tile)
        for out_ref, group in zip(out_refs, groups):
            for at, q in enumerate(group):
                out_ref[at * rows : (at + 1) * rows, columns] = total[q * rows : (q + 1) * rows]

        @pl.when(i + slots < count)
        def _():
            fetch(i + slots).start()

        return carry

    lax.fori_loop(0, count, body, 0)


def forward_streamed(where, x, code, scale, groups, width):
    rows, blocks = x[0].shape[0], sum(len(group) for group in groups)
    columns, depth = code.shape
    tile, slots = tile_of(columns, 256), 3
    return pl.pallas_call(
        functools.partial(streamed_kernel, groups, width),
        in_specs=[SMEM] * 2 + [VMEM] * len(x) + [pl.BlockSpec(memory_space=pltpu.HBM)],
        out_specs=[VMEM] * len(groups),
        out_shape=[array(rows * len(group) // blocks, columns) for group in groups],
        scratch_shapes=[
            pltpu.VMEM((rows, depth), BF16),
            pltpu.VMEM((slots, tile, depth), BF16),
            pltpu.SemaphoreType.DMA((slots,)),
        ],
        compiler_params=pltpu.CompilerParams(vmem_limit_bytes=14 << 20),
        cost_estimate=cost(rows, depth, columns),
        name="forward_streamed",
    )(where, scale, *x, pltpu.with_memory_space_constraint(code, pltpu.HBM))


def grads_kernel(both, where_ref, *refs):
    *in_refs, out_ref = refs
    rows, width = out_ref.shape[0], out_ref.shape[1] // 2
    tile = tile_of(width, 512)

    def total(terms, n):
        values = [term[term.shape[0] - rows :, n : n + tile].astype(F32) for term in terms]
        return functools.reduce(lambda left, right: left + right, values)

    for n in range(0, width, tile):
        gate_pre = total(in_refs[:both], n)
        up_pre = total(in_refs[:both], width + n)
        hidden_grad = total(in_refs[both:], n)
        gate_sig = jax.nn.sigmoid(gate_pre)
        out_ref[:, n : n + tile] = (
            hidden_grad * up_pre * gate_sig * (1.0 + gate_pre * (1.0 - gate_sig))
        ).astype(BF16)
        out_ref[:, width + n : width + n + tile] = (hidden_grad * gate_pre * gate_sig).astype(BF16)


def grads(where, gate_up, hidden_terms, rows, width):
    return pl.pallas_call(
        functools.partial(grads_kernel, len(gate_up)),
        in_specs=[SMEM] + [VMEM] * (len(gate_up) + len(hidden_terms)),
        out_specs=VMEM,
        out_shape=array(rows, 2 * width),
        compiler_params=PARAMS,
        name="hidden_grads",
    )(where, *gate_up, *hidden_terms)


def backward_kernel(places, total_places, where_ref, *refs):
    outs = CORES if total_places else 1
    *grad_refs, gate_ref, up_ref = refs[: -3 - outs]
    *out_refs, gate_all, up_all, total_ref = refs[-3 - outs :]
    blocks, rows = len(grad_refs), grad_refs[0].shape[0]
    depth = gate_all.shape[1]
    for q, grad_ref in enumerate(grad_refs):
        start = pl.multiple_of(block_of(q, blocks, where_ref[2]) * rows, rows)
        gate_all[pl.ds(start, rows)] = grad_ref[:, :depth]
        up_all[pl.ds(start, rows)] = grad_ref[:, depth:]
    tile = total_ref.shape[1]
    for at, j in enumerate(places):
        place = lax.rem(where_ref[1] + j, total_places) if total_places else j
        part = pl.ds(pl.multiple_of(place * tile, tile), tile)
        total = dot(gate_all[...], gate_ref[part, :], 1) + dot(up_all[...], up_ref[part, :], 1)
        if total_places:
            width = tile // CORES
            total_ref[...] = total.astype(BF16)
            for out_ref, core in zip(out_refs, (where_ref[2], 1 - where_ref[2])):
                out_ref[:, at * width : (at + 1) * width] = total_ref[
                    :, pl.ds(pl.multiple_of(core * width, width), width)
                ]
        else:
            out_refs[0][:, at * tile : (at + 1) * tile] = total.astype(BF16)


def backward(where, grad_parts, gate_weight, up_weight, places, total_places):
    columns, depth = gate_weight.shape
    rows = grad_parts[0].shape[0] * len(grad_parts)
    outs = CORES if total_places else 1
    tile = columns // total_places if total_places else tile_of(columns, 512)
    places = places if total_places else range(columns // tile)
    return pl.pallas_call(
        functools.partial(backward_kernel, places, total_places),
        in_specs=[SMEM] + [VMEM] * (len(grad_parts) + 2),
        out_specs=[VMEM] * outs,
        out_shape=[array(rows, tile * len(places) // outs)] * outs,
        scratch_shapes=[pltpu.VMEM((rows, depth), BF16)] * 2 + [pltpu.VMEM((rows, tile), BF16)],
        compiler_params=PARAMS,
        cost_estimate=cost(rows, 2 * depth, tile * len(places)),
        name="backward_product",
    )(
        where,
        *grad_parts,
        pltpu.with_memory_space_constraint(gate_weight, pltpu.VMEM),
        pltpu.with_memory_space_constraint(up_weight, pltpu.VMEM),
    )


def pair_kernel(own_ref, other_ref, *out_refs):
    width = out_refs[0].shape[1]
    for j, out_ref in enumerate(out_refs):
        columns = slice(j * width, (j + 1) * width)
        out_ref[...] = (own_ref[:, columns].astype(F32) + other_ref[:, columns].astype(F32)).astype(
            BF16
        )


def pair_sums(own, other, count, width):
    rows = own.shape[0]
    return pl.pallas_call(
        pair_kernel,
        in_specs=[VMEM] * 2,
        out_specs=[VMEM] * count,
        out_shape=[array(rows, width)] * count,
        compiler_params=PARAMS,
        name="pair_sums",
    )(own, other)


def final_kernel(blocks, done, where_ref, *refs):
    done_refs, in_refs, out_ref = refs[:done], refs[done:-1], refs[-1]
    rows = in_refs[0].shape[0] // blocks
    width = out_ref.shape[1]
    at = 0
    for done_ref in done_refs:
        out_ref[at : at + done_ref.shape[0]] = done_ref[...]
        at += done_ref.shape[0]
    for q in range(blocks):
        total = None
        for ref in in_refs:
            value = ref[q * rows : (q + 1) * rows, ref.shape[1] - width :].astype(F32)
            total = value if total is None else total + value
        start = pl.multiple_of(at + (where_ref[0] ^ q) * rows, rows)
        out_ref[pl.ds(start, rows)] = total.astype(BF16)


def final_sum(where, done, terms, blocks, width):
    rows = terms[0].shape[0] + sum(part.shape[0] for part in done)
    return pl.pallas_call(
        functools.partial(final_kernel, blocks, len(done)),
        in_specs=[SMEM] + [VMEM] * (len(done) + len(terms)),
        out_specs=VMEM,
        out_shape=array(rows, width),
        compiler_params=PARAMS,
        name="final_sum",
    )(where, *done, *terms)


def local(
    n_tp, n_dp, inputs, cotangent, gate_code, gate_scale, up_code, up_scale, down_code, down_scale
):
    n_z = n_tp // CORES
    width = inputs.shape[1]
    hidden = gate_code.shape[1]
    steps = n_dp.bit_length() - 1
    by_blocks = width % BLOCK == 0
    tp = lax.axis_index("tp")
    where = jnp.stack([lax.axis_index("dp"), tp // CORES, tp % CORES]).astype(jnp.int32)

    def exchange(value, step):
        pairs = []
        for i in range(n_tp):
            bit = 1 << (step if i % CORES == 0 else steps - 1 - step)
            pairs += [(i * n_dp + k, i * n_dp + (k ^ bit)) for k in range(n_dp)]
        return lax.ppermute(value, ("tp", "dp"), pairs)

    def swap_cores(value):
        return lax.ppermute(value, "tp", [(i, i ^ 1) for i in range(n_tp)])

    def along(value, places):
        return lax.ppermute(
            value, "tp", [(i, (i + places * CORES) % n_tp) for i in range(n_tp)]
        )

    def between(value, pairs):
        return lax.ppermute(
            value,
            "tp",
            [(i * CORES + c, k * CORES + c) for i, k in pairs for c in range(CORES)],
        )

    hops = by_blocks and n_z == 4

    def set_out(piece):
        if not by_blocks:
            return [lax.all_gather(piece, "tp", axis=1, tiled=True)]
        if hops:
            return [along(piece, 2)]
        return [along(piece, n_z - j) for j in range(1, n_z)]

    def near(piece, got):
        return [*got, between(piece, [(0, 1), (1, 0), (2, 3), (3, 2)])] if hops else got

    def pass_on(piece, got):
        if not hops:
            return got
        return [*got, between(piece, [(1, 2), (2, 1)]), between(got[0], [(1, 0), (2, 3)])]

    def arrive(piece, got):
        if not by_blocks:
            return got
        own = join_four(where, (piece, *got)) if hops else join([piece, *got])
        return [own, swap_cores(own)]

    groups, stays = [[0]], [0]
    for step in reversed(range(steps)):
        groups.insert(0, [q | 1 << step for q in stays])
        stays = groups[0] + stays

    def send(parts, step=0):
        return [*parts, exchange(parts[step], step)]

    def take(parts, step=0):
        parts, at = list(parts), 0
        for later in range(step + 1, steps):
            height = parts[later].shape[0]
            came = parts[-1][at : at + height].astype(F32)
            parts[later] = (parts[later].astype(F32) + came).astype(BF16)
            at += height
        return parts

    def settle(parts):
        for step in range(1, steps):
            parts = send(take(parts, step - 1), step)
        return parts

    def terms_of(parts):
        return parts[steps:]

    def start_rows(value):
        return (
            {0: value, 1: exchange(value, 0)},
            {1 << step: exchange(value, step) for step in range(1, steps)},
        )

    def finish_rows(have, late):
        have = dict(have)
        for step in range(1, steps):
            for q in list(have):
                have[q | 1 << step] = exchange(have[q], step) if q else late[1 << step]
        return [have[q] for q in range(n_dp)]

    whole = [[2, 1, 3, 0] if hops else [*range(1, n_z), 0]]
    parts_of_z = [[2], [1, 3], [0]] if hops else whole

    def products(grad_parts, places):
        return backward(
            where, grad_parts, gate_weight, up_weight, places, n_z if by_blocks else 0
        )

    def swapped(partial):
        return [partial[0], swap_cores(partial[1])] if by_blocks else partial

    def sums_of(partial, places):
        away = [j for j in places if j]
        return pair_sums(*partial, len(away), width) if by_blocks and away else []

    def spread(sums, partial, places):
        if not by_blocks:
            return [lax.psum_scatter(partial[0], "tp", scatter_dimension=1, tiled=True)]
        terms = [along(part, j) for j, part in zip([j for j in places if j], sums)]
        return terms + (list(partial) if 0 in places else [])

    def scatter(partial, places):
        return spread(sums_of(partial, places), partial, places)

    rows = inputs.shape[0] // CHUNKS // n_dp

    def hold(values):
        nonlocal where
        values, where = lax.optimization_barrier((values, where))
        return values

    in_1, co_1, in_2, co_2 = prepare(where, inputs, cotangent, n_dp)
    got_in_1 = near(in_1, set_out(in_1))
    gate_weight = weight(gate_code, gate_scale, True)
    gate_weight, got_in_1, co_1 = hold((gate_weight, got_in_1, co_1))

    got_in_1 = pass_on(in_1, got_in_1)
    got_co_1 = near(co_1, set_out(co_1))
    up_weight = weight(up_code, up_scale, True)
    up_weight, got_in_1, got_co_1 = hold((up_weight, got_in_1, got_co_1))

    x = arrive(in_1, got_in_1)
    got_co_1 = pass_on(co_1, got_co_1)
    gate_up_1 = forward(where, x, [gate_weight, up_weight], groups, 0, width)
    gate_up_1, got_co_1, in_2 = hold((gate_up_1, got_co_1, in_2))

    gate_up_1 = send(gate_up_1)
    x = arrive(co_1, got_co_1)
    got_in_2 = near(in_2, set_out(in_2))
    hidden_1 = forward_streamed(where, x, down_code, down_scale, groups, width)
    hidden_1, gate_up_1, got_in_2 = hold((hidden_1, gate_up_1, got_in_2))

    hidden_1 = send(hidden_1)
    gate_up_1 = settle(gate_up_1)
    got_in_2 = hold(pass_on(in_2, got_in_2))

    x = arrive(in_2, got_in_2)
    x, co_2, hidden_1 = hold((x, co_2, hidden_1))

    hidden_1 = settle(hidden_1)
    got_co_2 = near(co_2, set_out(co_2))
    gate_up_2 = forward(where, x, [gate_weight, up_weight], groups, 0, width)
    gate_up_2, got_co_2, gate_up_1, hidden_1 = hold((gate_up_2, got_co_2, gate_up_1, hidden_1))

    got_co_2 = pass_on(co_2, got_co_2)
    gate_up_2 = send(gate_up_2)
    grad_1 = grads(where, terms_of(gate_up_1), terms_of(hidden_1), rows, hidden)
    got_co_2, grad_1 = hold((got_co_2, grad_1))

    early_1, late_1 = start_rows(grad_1)
    x = hold(arrive(co_2, got_co_2))

    hidden_2 = forward_streamed(where, x, down_code, down_scale, groups, width)
    hidden_2, gate_up_2 = hold((hidden_2, gate_up_2))

    hidden_2 = send(hidden_2)
    early_1 = hold(early_1)

    parts_1 = finish_rows(early_1, late_1)
    parts_1, hidden_2 = hold((parts_1, hidden_2))

    hidden_2 = settle(hidden_2)
    gate_up_2 = settle(gate_up_2)
    partial_1 = products(parts_1, whole[0])
    hidden_2, gate_up_2, partial_1 = hold((hidden_2, gate_up_2, partial_1))

    partial_1 = swapped(partial_1)
    grad_2 = grads(where, terms_of(gate_up_2), terms_of(hidden_2), rows, hidden)
    early_2, late_2 = start_rows(grad_2)
    terms_1 = scatter(partial_1, whole[0])
    early_2, early = hold((early_2, terms_1[:1]))
    parts_2 = finish_rows(early_2, late_2)
    parts_2, later = hold((parts_2, terms_1[1:2]))
    terms_1 = [*early, *later, *terms_1[2:]]

    terms_2 = []
    partial, before = products(parts_2, parts_of_z[0]), parts_of_z[0]
    for places in parts_of_z[1:]:
        following = products(parts_2, places) if len(places) > 1 else None
        partial, following, terms_1 = hold((swapped(partial), following, terms_1))
        sums = hold(sums_of(partial, before))
        terms_2 += spread(sums, partial, before)
        partial = following or products(parts_2, places)
        before = places
    partial = swapped(partial)
    terms_2 += spread(sums_of(partial, before), partial, before)
    done = [final_sum(where, [], terms_1, n_dp, width)]
    return final_sum(where, done, terms_2, n_dp, width)


def solution(mesh):
    placed = (
        P("groups", ("dp", "tp")),
        P("groups", ("dp", "tp")),
        P("dp", "tp"),
        P("dp", "tp"),
        P("dp", "tp"),
        P("dp", "tp"),
        P("tp", "dp"),
        P("tp", "dp"),
    )
    return jax.shard_map(
        functools.partial(local, mesh.shape["tp"], mesh.shape["dp"]),
        mesh=mesh,
        in_specs=placed,
        out_specs=P("groups", ("dp", "tp")),
        check_vma=False,
    )
```

```python
import functools

import jax
import jax.numpy as jnp
from jax import lax
from jax.experimental import pallas as pl
from jax.experimental.pallas import tpu as pltpu
from jax.sharding import PartitionSpec as P

BLOCK = 128
CORES = 2
CHUNKS = 2
BF16 = jnp.bfloat16
F32 = jnp.float32
PARAMS = pltpu.CompilerParams(vmem_limit_bytes=8 << 20)
VMEM = pl.BlockSpec(memory_space=pltpu.VMEM)
SMEM = pl.BlockSpec(memory_space=pltpu.SMEM)


def tile_of(extent, most):
    best = BLOCK
    for size in range(BLOCK, most + 1, BLOCK):
        if extent % size == 0:
            best = size
    return best


def dot(left, right, contract):
    return lax.dot_general(
        left, right, (((1,), (contract,)), ((), ())), preferred_element_type=F32
    )


def cost(rows, depth, columns):
    return pl.CostEstimate(
        flops=1024, bytes_accessed=1024, transcendentals=0
    )


def array(rows, columns):
    return jax.ShapeDtypeStruct((rows, columns), BF16)


def reversed_bits(q, count):
    width = count.bit_length() - 1
    return sum(((q >> i) & 1) << (width - 1 - i) for i in range(width))


def block_of(q, count, core):
    return q + core * (reversed_bits(q, count) - q)


def weight_kernel(turned, code_ref, scale_ref, weight_ref, buffer, sems):
    slots, rows = buffer.shape[:2]
    count = code_ref.shape[0] // rows

    def fetch(i):
        slot = lax.rem(i, slots)
        return pltpu.make_async_copy(
            code_ref.at[pl.ds(pl.multiple_of(i * rows, rows), rows)], buffer.at[slot], sems.at[slot]
        )

    for i in range(min(slots, count)):
        fetch(i).start()

    def body(i, carry):
        fetch(i).wait()
        slot = lax.rem(i, slots)
        start = pl.multiple_of(i * rows, rows)
        for c in range(code_ref.shape[1] // BLOCK):
            columns = slice(c * BLOCK, (c + 1) * BLOCK)
            weight_ref[pl.ds(start, rows), columns] = (
                buffer[slot, :, columns].astype(F32) * (scale_ref[c, i] if turned else scale_ref[i, c])
            ).astype(BF16)

        @pl.when(i + slots < count)
        def _():
            fetch(i + slots).start()

        return carry

    lax.fori_loop(0, count, body, 0)


def weight(code, scale, turned):
    slots = 6
    scale = scale.T if turned else scale
    return pl.pallas_call(
        functools.partial(weight_kernel, turned),
        in_specs=[pl.BlockSpec(memory_space=pltpu.HBM), SMEM],
        out_specs=VMEM,
        out_shape=pltpu.VMEM(code.shape, BF16),
        scratch_shapes=[
            pltpu.VMEM((slots, BLOCK, code.shape[1]), BF16),
            pltpu.SemaphoreType.DMA((slots,)),
        ],
        compiler_params=pltpu.CompilerParams(vmem_limit_bytes=10 << 20),
        cost_estimate=pl.CostEstimate(
            flops=0, bytes_accessed=code.size // 4096, transcendentals=0
        ),
        name="scaled_weight",
    )(pltpu.with_memory_space_constraint(code, pltpu.HBM), scale)


def prep_kernel(rows, where_ref, inputs_ref, cotangent_ref, *refs):
    *out_refs, sem = refs
    count = inputs_ref.shape[0] // CHUNKS // rows
    copies = []
    for at, out_ref in enumerate(out_refs):
        for q in range(count):
            start = pl.multiple_of((at // 2 * count + (where_ref[0] ^ q)) * rows, rows)
            copies.append(
                pltpu.make_async_copy(
                    (inputs_ref, cotangent_ref)[at % 2].at[pl.ds(start, rows)],
                    out_ref.at[pl.ds(q * rows, rows)],
                    sem.at[len(copies)],
                )
            )
            copies[-1].start()
    for copy in copies:
        copy.wait()


def prepare(where, inputs, cotangent, n_dp):
    seq, width = inputs.shape
    return pl.pallas_call(
        functools.partial(prep_kernel, seq // CHUNKS // n_dp),
        in_specs=[SMEM] + [pl.BlockSpec(memory_space=pltpu.HBM)] * 2,
        out_specs=[VMEM] * (2 * CHUNKS),
        out_shape=[array(seq // CHUNKS, width)] * (2 * CHUNKS),
        scratch_shapes=[pltpu.SemaphoreType.DMA((2 * CHUNKS * n_dp,))],
        compiler_params=PARAMS,
        name="order_rows",
    )(
        where,
        pltpu.with_memory_space_constraint(inputs, pltpu.HBM),
        pltpu.with_memory_space_constraint(cotangent, pltpu.HBM),
    )


def join_kernel(*refs):
    *part_refs, out_ref = refs
    width = part_refs[0].shape[1]
    for j, part_ref in enumerate(part_refs):
        out_ref[:, j * width : (j + 1) * width] = part_ref[...]


def join(parts):
    rows, width = parts[0].shape
    return pl.pallas_call(
        join_kernel,
        in_specs=[VMEM] * len(parts),
        out_specs=VMEM,
        out_shape=array(rows, width * len(parts)),
        compiler_params=PARAMS,
        name="join",
    )(*parts)


def join_four_kernel(where_ref, own_ref, two_ref, near_ref, middle_ref, passed_ref, out_ref):
    width = own_ref.shape[1]
    place = where_ref[1]
    out_ref[:, :width] = own_ref[...]
    out_ref[:, 2 * width : 3 * width] = two_ref[...]
    odd = lax.rem(place, 2)
    out_ref[:, pl.ds(pl.multiple_of((1 + 2 * odd) * width, width), width)] = near_ref[...]
    rest = pl.ds(pl.multiple_of((3 - 2 * odd) * width, width), width)
    inner = jnp.logical_or(place == 1, place == 2)

    @pl.when(inner)
    def _():
        out_ref[:, rest] = middle_ref[...]

    @pl.when(jnp.logical_not(inner))
    def _():
        out_ref[:, rest] = passed_ref[...]


def join_four(where, parts):
    rows, width = parts[0].shape
    return pl.pallas_call(
        join_four_kernel,
        in_specs=[SMEM] + [VMEM] * len(parts),
        out_specs=VMEM,
        out_shape=array(rows, 4 * width),
        compiler_params=PARAMS,
        name="join",
    )(where, *parts)


def assemble(width, blocks, where_ref, x_refs, x_all):
    rows = x_all.shape[0] // blocks
    for q in range(blocks):
        start = pl.multiple_of(block_of(q, blocks, where_ref[2]) * rows, rows)
        own = slice(q * rows, (q + 1) * rows)
        if len(x_refs) == 1:
            x_all[own] = x_refs[0][pl.ds(start, rows)]
            continue
        count = x_all.shape[1] // (CORES * width)
        for j in range(count):
            for core, x_ref in enumerate(x_refs):
                place = lax.rem(where_ref[1] + j, count) * CORES + (where_ref[2] ^ core)
                x_all[own, pl.ds(pl.multiple_of(place * width, width), width)] = x_ref[
                    pl.ds(start, rows), j * width : (j + 1) * width
                ]


def forward_kernel(groups, contract, width, count, where_ref, *refs):
    outs = len(groups)
    x_refs, weight_refs = refs[: -outs - 1 - count], refs[-outs - 1 - count : -outs - 1]
    out_refs, x_all = refs[-outs - 1 : -1], refs[-1]
    blocks = sum(len(group) for group in groups)
    assemble(width, blocks, where_ref, x_refs, x_all)
    columns = out_refs[0].shape[1] // count
    rows = x_all.shape[0] // blocks
    tile = tile_of(columns, 512)
    for at, weight_ref in enumerate(weight_refs):
        for n in range(0, columns, tile):
            part = weight_ref[n : n + tile, :] if contract else weight_ref[:, n : n + tile]
            total = dot(x_all[...], part, contract).astype(BF16)
            place = slice(at * columns + n, at * columns + n + tile)
            for out_ref, group in zip(out_refs, groups):
                for i, q in enumerate(group):
                    out_ref[i * rows : (i + 1) * rows, place] = total[q * rows : (q + 1) * rows]


def forward(where, x, weights, groups, contract, width):
    rows, blocks = x[0].shape[0], sum(len(group) for group in groups)
    depth, columns = weights[0].shape[contract], weights[0].shape[1 - contract]
    outs = [array(rows * len(group) // blocks, columns * len(weights)) for group in groups]
    return pl.pallas_call(
        functools.partial(forward_kernel, groups, contract, width, len(weights)),
        in_specs=[SMEM] + [VMEM] * (len(x) + len(weights)),
        out_specs=[VMEM] * len(outs),
        out_shape=outs,
        scratch_shapes=[pltpu.VMEM((rows, depth), BF16)],
        compiler_params=PARAMS,
        cost_estimate=cost(rows, depth, columns),
        name="forward_product",
    )(where, *x, *(pltpu.with_memory_space_constraint(part, pltpu.VMEM) for part in weights))


def streamed_kernel(groups, width, where_ref, scale_ref, *refs):
    outs = len(groups)
    x_refs, code_ref = refs[: -outs - 4], refs[-outs - 4]
    out_refs, (x_all, buffer, sems) = refs[-outs - 3 : -3], refs[-3:]
    slots, tile, depth = buffer.shape
    count = code_ref.shape[0] // tile
    blocks = sum(len(group) for group in groups)
    rows = x_all.shape[0] // blocks
    step = tile_of(depth, 512)

    def fetch(i):
        slot = lax.rem(i, slots)
        return pltpu.make_async_copy(
            code_ref.at[pl.ds(pl.multiple_of(i * tile, tile), tile)], buffer.at[slot], sems.at[slot]
        )

    for i in range(min(slots, count)):
        fetch(i).start()
    assemble(width, blocks, where_ref, x_refs, x_all)

    def body(i, carry):
        fetch(i).wait()
        slot = lax.rem(i, slots)
        total = None
        for k in range(0, depth, step):
            lines = []
            for r in range(tile // BLOCK):
                lines.append(
                    jnp.concatenate(
                        [
                            (
                                buffer[slot, r * BLOCK : (r + 1) * BLOCK, c : c + BLOCK].astype(F32)
                                * scale_ref[i * (tile // BLOCK) + r, c // BLOCK]
                            ).astype(BF16)
                            for c in range(k, k + step, BLOCK)
                        ],
                        axis=1,
                    )
                )
            term = dot(x_all[:, k : k + step], jnp.concatenate(lines, axis=0), 1)
            total = term if total is None else total + term
        total = total.astype(BF16)
        columns = pl.ds(pl.multiple_of(i * tile, tile), tile)
        for out_ref, group in zip(out_refs, groups):
            for at, q in enumerate(group):
                out_ref[at * rows : (at + 1) * rows, columns] = total[q * rows : (q + 1) * rows]

        @pl.when(i + slots < count)
        def _():
            fetch(i + slots).start()

        return carry

    lax.fori_loop(0, count, body, 0)


def forward_streamed(where, x, code, scale, groups, width):
    rows, blocks = x[0].shape[0], sum(len(group) for group in groups)
    columns, depth = code.shape
    tile, slots = tile_of(columns, 256), 3
    return pl.pallas_call(
        functools.partial(streamed_kernel, groups, width),
        in_specs=[SMEM] * 2 + [VMEM] * len(x) + [pl.BlockSpec(memory_space=pltpu.HBM)],
        out_specs=[VMEM] * len(groups),
        out_shape=[array(rows * len(group) // blocks, columns) for group in groups],
        scratch_shapes=[
            pltpu.VMEM((rows, depth), BF16),
            pltpu.VMEM((slots, tile, depth), BF16),
            pltpu.SemaphoreType.DMA((slots,)),
        ],
        compiler_params=pltpu.CompilerParams(vmem_limit_bytes=14 << 20),
        cost_estimate=cost(rows, depth, columns),
        name="forward_streamed",
    )(where, scale, *x, pltpu.with_memory_space_constraint(code, pltpu.HBM))


def grads_kernel(both, where_ref, *refs):
    *in_refs, out_ref = refs
    rows, width = out_ref.shape[0], out_ref.shape[1] // 2
    tile = tile_of(width, 512)

    def total(terms, n):
        values = [term[term.shape[0] - rows :, n : n + tile].astype(F32) for term in terms]
        return functools.reduce(lambda left, right: left + right, values)

    for n in range(0, width, tile):
        gate_pre = total(in_refs[:both], n)
        up_pre = total(in_refs[:both], width + n)
        hidden_grad = total(in_refs[both:], n)
        gate_sig = jax.nn.sigmoid(gate_pre)
        out_ref[:, n : n + tile] = (
            hidden_grad * up_pre * gate_sig * (1.0 + gate_pre * (1.0 - gate_sig))
        ).astype(BF16)
        out_ref[:, width + n : width + n + tile] = (hidden_grad * gate_pre * gate_sig).astype(BF16)


def grads(where, gate_up, hidden_terms, rows, width):
    return pl.pallas_call(
        functools.partial(grads_kernel, len(gate_up)),
        in_specs=[SMEM] + [VMEM] * (len(gate_up) + len(hidden_terms)),
        out_specs=VMEM,
        out_shape=array(rows, 2 * width),
        compiler_params=PARAMS,
        name="hidden_grads",
    )(where, *gate_up, *hidden_terms)


def backward_kernel(places, total_places, where_ref, *refs):
    outs = CORES if total_places else 1
    *grad_refs, gate_ref, up_ref = refs[: -3 - outs]
    *out_refs, gate_all, up_all, total_ref = refs[-3 - outs :]
    blocks, rows = len(grad_refs), grad_refs[0].shape[0]
    depth = gate_all.shape[1]
    for q, grad_ref in enumerate(grad_refs):
        start = pl.multiple_of(block_of(q, blocks, where_ref[2]) * rows, rows)
        gate_all[pl.ds(start, rows)] = grad_ref[:, :depth]
        up_all[pl.ds(start, rows)] = grad_ref[:, depth:]
    tile = total_ref.shape[1]
    for at, j in enumerate(places):
        place = lax.rem(where_ref[1] + j, total_places) if total_places else j
        part = pl.ds(pl.multiple_of(place * tile, tile), tile)
        total = dot(gate_all[...], gate_ref[part, :], 1) + dot(up_all[...], up_ref[part, :], 1)
        if total_places:
            width = tile // CORES
            total_ref[...] = total.astype(BF16)
            for out_ref, core in zip(out_refs, (where_ref[2], 1 - where_ref[2])):
                out_ref[:, at * width : (at + 1) * width] = total_ref[
                    :, pl.ds(pl.multiple_of(core * width, width), width)
                ]
        else:
            out_refs[0][:, at * tile : (at + 1) * tile] = total.astype(BF16)


def backward(where, grad_parts, gate_weight, up_weight, places, total_places):
    columns, depth = gate_weight.shape
    rows = grad_parts[0].shape[0] * len(grad_parts)
    outs = CORES if total_places else 1
    tile = columns // total_places if total_places else tile_of(columns, 512)
    places = places if total_places else range(columns // tile)
    return pl.pallas_call(
        functools.partial(backward_kernel, places, total_places),
        in_specs=[SMEM] + [VMEM] * (len(grad_parts) + 2),
        out_specs=[VMEM] * outs,
        out_shape=[array(rows, tile * len(places) // outs)] * outs,
        scratch_shapes=[pltpu.VMEM((rows, depth), BF16)] * 2 + [pltpu.VMEM((rows, tile), BF16)],
        compiler_params=PARAMS,
        cost_estimate=cost(rows, 2 * depth, tile * len(places)),
        name="backward_product",
    )(
        where,
        *grad_parts,
        pltpu.with_memory_space_constraint(gate_weight, pltpu.VMEM),
        pltpu.with_memory_space_constraint(up_weight, pltpu.VMEM),
    )


def pair_kernel(own_ref, other_ref, *out_refs):
    width = out_refs[0].shape[1]
    for j, out_ref in enumerate(out_refs):
        columns = slice(j * width, (j + 1) * width)
        out_ref[...] = (own_ref[:, columns].astype(F32) + other_ref[:, columns].astype(F32)).astype(
            BF16
        )


def pair_sums(own, other, count, width):
    rows = own.shape[0]
    return pl.pallas_call(
        pair_kernel,
        in_specs=[VMEM] * 2,
        out_specs=[VMEM] * count,
        out_shape=[array(rows, width)] * count,
        compiler_params=PARAMS,
        name="pair_sums",
    )(own, other)


def final_kernel(blocks, done, where_ref, *refs):
    done_refs, in_refs, out_ref = refs[:done], refs[done:-1], refs[-1]
    rows = in_refs[0].shape[0] // blocks
    width = out_ref.shape[1]
    at = 0
    for done_ref in done_refs:
        out_ref[at : at + done_ref.shape[0]] = done_ref[...]
        at += done_ref.shape[0]
    for q in range(blocks):
        total = None
        for ref in in_refs:
            value = ref[q * rows : (q + 1) * rows, ref.shape[1] - width :].astype(F32)
            total = value if total is None else total + value
        start = pl.multiple_of(at + (where_ref[0] ^ q) * rows, rows)
        out_ref[pl.ds(start, rows)] = total.astype(BF16)


def final_sum(where, done, terms, blocks, width):
    rows = terms[0].shape[0] + sum(part.shape[0] for part in done)
    return pl.pallas_call(
        functools.partial(final_kernel, blocks, len(done)),
        in_specs=[SMEM] + [VMEM] * (len(done) + len(terms)),
        out_specs=VMEM,
        out_shape=array(rows, width),
        compiler_params=PARAMS,
        name="final_sum",
    )(where, *done, *terms)


def local(
    n_tp, n_dp, inputs, cotangent, gate_code, gate_scale, up_code, up_scale, down_code, down_scale
):
    n_z = n_tp // CORES
    width = inputs.shape[1]
    hidden = gate_code.shape[1]
    steps = n_dp.bit_length() - 1
    by_blocks = width % BLOCK == 0
    tp = lax.axis_index("tp")
    where = jnp.stack([lax.axis_index("dp"), tp // CORES, tp % CORES]).astype(jnp.int32)

    def exchange(value, step):
        pairs = []
        for i in range(n_tp):
            bit = 1 << (step if i % CORES == 0 else steps - 1 - step)
            pairs += [(i * n_dp + k, i * n_dp + (k ^ bit)) for k in range(n_dp)]
        return lax.ppermute(value, ("tp", "dp"), pairs)

    def swap_cores(value):
        return lax.ppermute(value, "tp", [(i, i ^ 1) for i in range(n_tp)])

    def along(value, places):
        return lax.ppermute(
            value, "tp", [(i, (i + places * CORES) % n_tp) for i in range(n_tp)]
        )

    def between(value, pairs):
        return lax.ppermute(
            value,
            "tp",
            [(i * CORES + c, k * CORES + c) for i, k in pairs for c in range(CORES)],
        )

    hops = by_blocks and n_z == 4

    def set_out(piece):
        if not by_blocks:
            return [lax.all_gather(piece, "tp", axis=1, tiled=True)]
        if hops:
            return [along(piece, 2)]
        return [along(piece, n_z - j) for j in range(1, n_z)]

    def near(piece, got):
        return [*got, between(piece, [(0, 1), (1, 0), (2, 3), (3, 2)])] if hops else got

    def pass_on(piece, got):
        if not hops:
            return got
        return [*got, between(piece, [(1, 2), (2, 1)]), between(got[0], [(1, 0), (2, 3)])]

    def arrive(piece, got):
        if not by_blocks:
            return got
        own = join_four(where, (piece, *got)) if hops else join([piece, *got])
        return [own, swap_cores(own)]

    groups, stays = [[0]], [0]
    for step in reversed(range(steps)):
        groups.insert(0, [q | 1 << step for q in stays])
        stays = groups[0] + stays

    def send(parts, step=0):
        return [*parts, exchange(parts[step], step)]

    def take(parts, step=0):
        parts, at = list(parts), 0
        for later in range(step + 1, steps):
            height = parts[later].shape[0]
            came = parts[-1][at : at + height].astype(F32)
            parts[later] = (parts[later].astype(F32) + came).astype(BF16)
            at += height
        return parts

    def settle(parts):
        for step in range(1, steps):
            parts = send(take(parts, step - 1), step)
        return parts

    def terms_of(parts):
        return parts[steps:]

    def start_rows(value):
        return (
            {0: value, 1: exchange(value, 0)},
            {1 << step: exchange(value, step) for step in range(1, steps)},
        )

    def finish_rows(have, late):
        have = dict(have)
        for step in range(1, steps):
            for q in list(have):
                have[q | 1 << step] = exchange(have[q], step) if q else late[1 << step]
        return [have[q] for q in range(n_dp)]

    whole = [[2, 1, 3, 0] if hops else [*range(1, n_z), 0]]
    parts_of_z = [[2], [1, 3], [0]] if hops else whole

    def products(grad_parts, places):
        return backward(
            where, grad_parts, gate_weight, up_weight, places, n_z if by_blocks else 0
        )

    def swapped(partial):
        return [partial[0], swap_cores(partial[1])] if by_blocks else partial

    def sums_of(partial, places):
        away = [j for j in places if j]
        return pair_sums(*partial, len(away), width) if by_blocks and away else []

    def spread(sums, partial, places):
        if not by_blocks:
            return [lax.psum_scatter(partial[0], "tp", scatter_dimension=1, tiled=True)]
        terms = [along(part, j) for j, part in zip([j for j in places if j], sums)]
        return terms + (list(partial) if 0 in places else [])

    def scatter(partial, places):
        return spread(sums_of(partial, places), partial, places)

    rows = inputs.shape[0] // CHUNKS // n_dp

    def hold(values):
        nonlocal where
        values, where = lax.optimization_barrier((values, where))
        return values

    in_1, co_1, in_2, co_2 = prepare(where, inputs, cotangent, n_dp)
    got_in_1 = near(in_1, set_out(in_1))
    gate_weight = weight(gate_code, gate_scale, True)
    gate_weight, got_in_1, co_1 = hold((gate_weight, got_in_1, co_1))

    got_in_1 = pass_on(in_1, got_in_1)
    got_co_1 = near(co_1, set_out(co_1))
    up_weight = weight(up_code, up_scale, True)
    up_weight, got_in_1, got_co_1 = hold((up_weight, got_in_1, got_co_1))

    x = arrive(in_1, got_in_1)
    got_co_1 = pass_on(co_1, got_co_1)
    gate_up_1 = forward(where, x, [gate_weight, up_weight], groups, 0, width)
    gate_up_1, got_co_1, in_2 = hold((gate_up_1, got_co_1, in_2))

    gate_up_1 = send(gate_up_1)
    x = arrive(co_1, got_co_1)
    got_in_2 = near(in_2, set_out(in_2))
    hidden_1 = forward_streamed(where, x, down_code, down_scale, groups, width)
    hidden_1, gate_up_1, got_in_2, co_2 = hold((hidden_1, gate_up_1, got_in_2, co_2))

    hidden_1 = send(hidden_1)
    got_co_2 = near(co_2, set_out(co_2))
    got_in_2 = hold(pass_on(in_2, got_in_2))

    gate_up_1 = settle(gate_up_1)
    x = arrive(in_2, got_in_2)
    x, hidden_1, got_co_2 = hold((x, hidden_1, got_co_2))

    hidden_1 = settle(hidden_1)
    got_co_2 = pass_on(co_2, got_co_2)
    gate_up_2 = forward(where, x, [gate_weight, up_weight], groups, 0, width)
    gate_up_2, got_co_2, gate_up_1, hidden_1 = hold((gate_up_2, got_co_2, gate_up_1, hidden_1))

    gate_up_2 = send(gate_up_2)
    grad_1 = grads(where, terms_of(gate_up_1), terms_of(hidden_1), rows, hidden)
    x, grad_1 = hold((arrive(co_2, got_co_2), grad_1))

    early_1, late_1 = start_rows(grad_1)
    hidden_2 = forward_streamed(where, x, down_code, down_scale, groups, width)
    hidden_2, gate_up_2 = hold((hidden_2, gate_up_2))

    hidden_2 = send(hidden_2)
    early_1 = hold(early_1)

    parts_1 = finish_rows(early_1, late_1)
    parts_1, hidden_2 = hold((parts_1, hidden_2))

    hidden_2 = settle(hidden_2)
    gate_up_2 = settle(gate_up_2)
    partial_1 = products(parts_1, whole[0])
    hidden_2, gate_up_2, partial_1 = hold((hidden_2, gate_up_2, partial_1))

    partial_1 = swapped(partial_1)
    grad_2 = grads(where, terms_of(gate_up_2), terms_of(hidden_2), rows, hidden)
    early_2, late_2 = start_rows(grad_2)
    terms_1 = scatter(partial_1, whole[0])
    early_2 = hold(early_2)
    parts_2 = finish_rows(early_2, late_2)
    parts_2, early = hold((parts_2, terms_1[:1]))
    terms_1 = [*early, *terms_1[1:]]

    terms_2 = []
    partial, before = products(parts_2, parts_of_z[0]), parts_of_z[0]
    for places in parts_of_z[1:]:
        following = products(parts_2, places) if len(places) > 1 else None
        partial, following, terms_1 = hold((swapped(partial), following, terms_1))
        sums = hold(sums_of(partial, before))
        terms_2 += spread(sums, partial, before)
        partial = following or products(parts_2, places)
        before = places
    partial = swapped(partial)
    terms_2 += spread(sums_of(partial, before), partial, before)
    done = [final_sum(where, [], terms_1, n_dp, width)]
    return final_sum(where, done, terms_2, n_dp, width)


def solution(mesh):
    placed = (
        P("groups", ("dp", "tp")),
        P("groups", ("dp", "tp")),
        P("dp", "tp"),
        P("dp", "tp"),
        P("dp", "tp"),
        P("dp", "tp"),
        P("tp", "dp"),
        P("tp", "dp"),
    )
    return jax.shard_map(
        functools.partial(local, mesh.shape["tp"], mesh.shape["dp"]),
        mesh=mesh,
        in_specs=placed,
        out_specs=P("groups", ("dp", "tp")),
        check_vma=False,
    )
```

```python
import functools

import jax
import jax.numpy as jnp
from jax import lax
from jax.experimental import pallas as pl
from jax.experimental.pallas import tpu as pltpu
from jax.sharding import PartitionSpec as P

BLOCK = 128
CORES = 2
CHUNKS = 2
BF16 = jnp.bfloat16
F32 = jnp.float32
PARAMS = pltpu.CompilerParams(vmem_limit_bytes=8 << 20)
VMEM = pl.BlockSpec(memory_space=pltpu.VMEM)
SMEM = pl.BlockSpec(memory_space=pltpu.SMEM)


def tile_of(extent, most):
    best = BLOCK
    for size in range(BLOCK, most + 1, BLOCK):
        if extent % size == 0:
            best = size
    return best


def dot(left, right, contract):
    return lax.dot_general(
        left, right, (((1,), (contract,)), ((), ())), preferred_element_type=F32
    )


def cost(rows, depth, columns):
    return pl.CostEstimate(
        flops=1024, bytes_accessed=1024, transcendentals=0
    )


def array(rows, columns):
    return jax.ShapeDtypeStruct((rows, columns), BF16)


def reversed_bits(q, count):
    width = count.bit_length() - 1
    return sum(((q >> i) & 1) << (width - 1 - i) for i in range(width))


def block_of(q, count, core):
    return q + core * (reversed_bits(q, count) - q)


def weight_kernel(turned, code_ref, scale_ref, weight_ref, buffer, sems):
    slots, rows = buffer.shape[:2]
    count = code_ref.shape[0] // rows

    def fetch(i):
        slot = lax.rem(i, slots)
        return pltpu.make_async_copy(
            code_ref.at[pl.ds(pl.multiple_of(i * rows, rows), rows)], buffer.at[slot], sems.at[slot]
        )

    for i in range(min(slots, count)):
        fetch(i).start()

    def body(i, carry):
        fetch(i).wait()
        slot = lax.rem(i, slots)
        start = pl.multiple_of(i * rows, rows)
        for c in range(code_ref.shape[1] // BLOCK):
            columns = slice(c * BLOCK, (c + 1) * BLOCK)
            weight_ref[pl.ds(start, rows), columns] = (
                buffer[slot, :, columns].astype(F32) * (scale_ref[c, i] if turned else scale_ref[i, c])
            ).astype(BF16)

        @pl.when(i + slots < count)
        def _():
            fetch(i + slots).start()

        return carry

    lax.fori_loop(0, count, body, 0)


def weight(code, scale, turned):
    slots = 6
    scale = scale.T if turned else scale
    return pl.pallas_call(
        functools.partial(weight_kernel, turned),
        in_specs=[pl.BlockSpec(memory_space=pltpu.HBM), SMEM],
        out_specs=VMEM,
        out_shape=pltpu.VMEM(code.shape, BF16),
        scratch_shapes=[
            pltpu.VMEM((slots, BLOCK, code.shape[1]), BF16),
            pltpu.SemaphoreType.DMA((slots,)),
        ],
        compiler_params=pltpu.CompilerParams(vmem_limit_bytes=10 << 20),
        cost_estimate=pl.CostEstimate(
            flops=0, bytes_accessed=code.size // 4096, transcendentals=0
        ),
        name="scaled_weight",
    )(pltpu.with_memory_space_constraint(code, pltpu.HBM), scale)


def prep_kernel(rows, where_ref, inputs_ref, cotangent_ref, *refs):
    *out_refs, sem = refs
    count = inputs_ref.shape[0] // CHUNKS // rows
    copies = []
    for at, out_ref in enumerate(out_refs):
        for q in range(count):
            start = pl.multiple_of((at // 2 * count + (where_ref[0] ^ q)) * rows, rows)
            copies.append(
                pltpu.make_async_copy(
                    (inputs_ref, cotangent_ref)[at % 2].at[pl.ds(start, rows)],
                    out_ref.at[pl.ds(q * rows, rows)],
                    sem.at[len(copies)],
                )
            )
            copies[-1].start()
    for copy in copies:
        copy.wait()


def prepare(where, inputs, cotangent, n_dp):
    seq, width = inputs.shape
    return pl.pallas_call(
        functools.partial(prep_kernel, seq // CHUNKS // n_dp),
        in_specs=[SMEM] + [pl.BlockSpec(memory_space=pltpu.HBM)] * 2,
        out_specs=[VMEM] * (2 * CHUNKS),
        out_shape=[array(seq // CHUNKS, width)] * (2 * CHUNKS),
        scratch_shapes=[pltpu.SemaphoreType.DMA((2 * CHUNKS * n_dp,))],
        compiler_params=PARAMS,
        name="order_rows",
    )(
        where,
        pltpu.with_memory_space_constraint(inputs, pltpu.HBM),
        pltpu.with_memory_space_constraint(cotangent, pltpu.HBM),
    )


def join_kernel(*refs):
    *part_refs, out_ref = refs
    width = part_refs[0].shape[1]
    for j, part_ref in enumerate(part_refs):
        out_ref[:, j * width : (j + 1) * width] = part_ref[...]


def join(parts):
    rows, width = parts[0].shape
    return pl.pallas_call(
        join_kernel,
        in_specs=[VMEM] * len(parts),
        out_specs=VMEM,
        out_shape=array(rows, width * len(parts)),
        compiler_params=PARAMS,
        name="join",
    )(*parts)


def join_four_kernel(where_ref, own_ref, two_ref, near_ref, middle_ref, passed_ref, out_ref):
    width = own_ref.shape[1]
    place = where_ref[1]
    out_ref[:, :width] = own_ref[...]
    out_ref[:, 2 * width : 3 * width] = two_ref[...]
    odd = lax.rem(place, 2)
    out_ref[:, pl.ds(pl.multiple_of((1 + 2 * odd) * width, width), width)] = near_ref[...]
    rest = pl.ds(pl.multiple_of((3 - 2 * odd) * width, width), width)
    inner = jnp.logical_or(place == 1, place == 2)

    @pl.when(inner)
    def _():
        out_ref[:, rest] = middle_ref[...]

    @pl.when(jnp.logical_not(inner))
    def _():
        out_ref[:, rest] = passed_ref[...]


def join_four(where, parts):
    rows, width = parts[0].shape
    return pl.pallas_call(
        join_four_kernel,
        in_specs=[SMEM] + [VMEM] * len(parts),
        out_specs=VMEM,
        out_shape=array(rows, 4 * width),
        compiler_params=PARAMS,
        name="join",
    )(where, *parts)


def assemble(width, blocks, where_ref, x_refs, x_all):
    rows = x_all.shape[0] // blocks
    for q in range(blocks):
        start = pl.multiple_of(block_of(q, blocks, where_ref[2]) * rows, rows)
        own = slice(q * rows, (q + 1) * rows)
        if len(x_refs) == 1:
            x_all[own] = x_refs[0][pl.ds(start, rows)]
            continue
        count = x_all.shape[1] // (CORES * width)
        for j in range(count):
            for core, x_ref in enumerate(x_refs):
                place = lax.rem(where_ref[1] + j, count) * CORES + (where_ref[2] ^ core)
                x_all[own, pl.ds(pl.multiple_of(place * width, width), width)] = x_ref[
                    pl.ds(start, rows), j * width : (j + 1) * width
                ]


def forward_kernel(groups, contract, width, count, where_ref, *refs):
    outs = len(groups)
    x_refs, weight_refs = refs[: -outs - 1 - count], refs[-outs - 1 - count : -outs - 1]
    out_refs, x_all = refs[-outs - 1 : -1], refs[-1]
    blocks = sum(len(group) for group in groups)
    assemble(width, blocks, where_ref, x_refs, x_all)
    columns = out_refs[0].shape[1] // count
    rows = x_all.shape[0] // blocks
    tile = tile_of(columns, 512)
    for at, weight_ref in enumerate(weight_refs):
        for n in range(0, columns, tile):
            part = weight_ref[n : n + tile, :] if contract else weight_ref[:, n : n + tile]
            total = dot(x_all[...], part, contract).astype(BF16)
            place = slice(at * columns + n, at * columns + n + tile)
            for out_ref, group in zip(out_refs, groups):
                for i, q in enumerate(group):
                    out_ref[i * rows : (i + 1) * rows, place] = total[q * rows : (q + 1) * rows]


def forward(where, x, weights, groups, contract, width):
    rows, blocks = x[0].shape[0], sum(len(group) for group in groups)
    depth, columns = weights[0].shape[contract], weights[0].shape[1 - contract]
    outs = [array(rows * len(group) // blocks, columns * len(weights)) for group in groups]
    return pl.pallas_call(
        functools.partial(forward_kernel, groups, contract, width, len(weights)),
        in_specs=[SMEM] + [VMEM] * (len(x) + len(weights)),
        out_specs=[VMEM] * len(outs),
        out_shape=outs,
        scratch_shapes=[pltpu.VMEM((rows, depth), BF16)],
        compiler_params=PARAMS,
        cost_estimate=cost(rows, depth, columns),
        name="forward_product",
    )(where, *x, *(pltpu.with_memory_space_constraint(part, pltpu.VMEM) for part in weights))


def streamed_kernel(groups, width, where_ref, scale_ref, *refs):
    outs = len(groups)
    x_refs, code_ref = refs[: -outs - 4], refs[-outs - 4]
    out_refs, (x_all, buffer, sems) = refs[-outs - 3 : -3], refs[-3:]
    slots, tile, depth = buffer.shape
    count = code_ref.shape[0] // tile
    blocks = sum(len(group) for group in groups)
    rows = x_all.shape[0] // blocks
    step = tile_of(depth, 512)

    def fetch(i):
        slot = lax.rem(i, slots)
        return pltpu.make_async_copy(
            code_ref.at[pl.ds(pl.multiple_of(i * tile, tile), tile)], buffer.at[slot], sems.at[slot]
        )

    for i in range(min(slots, count)):
        fetch(i).start()
    assemble(width, blocks, where_ref, x_refs, x_all)

    def body(i, carry):
        fetch(i).wait()
        slot = lax.rem(i, slots)
        total = None
        for k in range(0, depth, step):
            lines = []
            for r in range(tile // BLOCK):
                lines.append(
                    jnp.concatenate(
                        [
                            (
                                buffer[slot, r * BLOCK : (r + 1) * BLOCK, c : c + BLOCK].astype(F32)
                                * scale_ref[i * (tile // BLOCK) + r, c // BLOCK]
                            ).astype(BF16)
                            for c in range(k, k + step, BLOCK)
                        ],
                        axis=1,
                    )
                )
            term = dot(x_all[:, k : k + step], jnp.concatenate(lines, axis=0), 1)
            total = term if total is None else total + term
        total = total.astype(BF16)
        columns = pl.ds(pl.multiple_of(i * tile, tile), tile)
        for out_ref, group in zip(out_refs, groups):
            for at, q in enumerate(group):
                out_ref[at * rows : (at + 1) * rows, columns] = total[q * rows : (q + 1) * rows]

        @pl.when(i + slots < count)
        def _():
            fetch(i + slots).start()

        return carry

    lax.fori_loop(0, count, body, 0)


def forward_streamed(where, x, code, scale, groups, width):
    rows, blocks = x[0].shape[0], sum(len(group) for group in groups)
    columns, depth = code.shape
    tile, slots = tile_of(columns, 256), 3
    return pl.pallas_call(
        functools.partial(streamed_kernel, groups, width),
        in_specs=[SMEM] * 2 + [VMEM] * len(x) + [pl.BlockSpec(memory_space=pltpu.HBM)],
        out_specs=[VMEM] * len(groups),
        out_shape=[array(rows * len(group) // blocks, columns) for group in groups],
        scratch_shapes=[
            pltpu.VMEM((rows, depth), BF16),
            pltpu.VMEM((slots, tile, depth), BF16),
            pltpu.SemaphoreType.DMA((slots,)),
        ],
        compiler_params=pltpu.CompilerParams(vmem_limit_bytes=14 << 20),
        cost_estimate=cost(rows, depth, columns),
        name="forward_streamed",
    )(where, scale, *x, pltpu.with_memory_space_constraint(code, pltpu.HBM))


def grads_kernel(both, where_ref, *refs):
    *in_refs, out_ref = refs
    rows, width = out_ref.shape[0], out_ref.shape[1] // 2
    tile = tile_of(width, 512)

    def total(terms, n):
        values = [term[term.shape[0] - rows :, n : n + tile].astype(F32) for term in terms]
        return functools.reduce(lambda left, right: left + right, values)

    for n in range(0, width, tile):
        gate_pre = total(in_refs[:both], n)
        up_pre = total(in_refs[:both], width + n)
        hidden_grad = total(in_refs[both:], n)
        gate_sig = jax.nn.sigmoid(gate_pre)
        out_ref[:, n : n + tile] = (
            hidden_grad * up_pre * gate_sig * (1.0 + gate_pre * (1.0 - gate_sig))
        ).astype(BF16)
        out_ref[:, width + n : width + n + tile] = (hidden_grad * gate_pre * gate_sig).astype(BF16)


def grads(where, gate_up, hidden_terms, rows, width):
    return pl.pallas_call(
        functools.partial(grads_kernel, len(gate_up)),
        in_specs=[SMEM] + [VMEM] * (len(gate_up) + len(hidden_terms)),
        out_specs=VMEM,
        out_shape=array(rows, 2 * width),
        compiler_params=PARAMS,
        name="hidden_grads",
    )(where, *gate_up, *hidden_terms)


def backward_kernel(places, total_places, where_ref, *refs):
    outs = CORES if total_places else 1
    *grad_refs, gate_ref, up_ref = refs[: -3 - outs]
    *out_refs, gate_all, up_all, total_ref = refs[-3 - outs :]
    blocks, rows = len(grad_refs), grad_refs[0].shape[0]
    depth = gate_all.shape[1]
    for q, grad_ref in enumerate(grad_refs):
        start = pl.multiple_of(block_of(q, blocks, where_ref[2]) * rows, rows)
        gate_all[pl.ds(start, rows)] = grad_ref[:, :depth]
        up_all[pl.ds(start, rows)] = grad_ref[:, depth:]
    tile = total_ref.shape[1]
    for at, j in enumerate(places):
        place = lax.rem(where_ref[1] + j, total_places) if total_places else j
        part = pl.ds(pl.multiple_of(place * tile, tile), tile)
        total = dot(gate_all[...], gate_ref[part, :], 1) + dot(up_all[...], up_ref[part, :], 1)
        if total_places:
            width = tile // CORES
            total_ref[...] = total.astype(BF16)
            for out_ref, core in zip(out_refs, (where_ref[2], 1 - where_ref[2])):
                out_ref[:, at * width : (at + 1) * width] = total_ref[
                    :, pl.ds(pl.multiple_of(core * width, width), width)
                ]
        else:
            out_refs[0][:, at * tile : (at + 1) * tile] = total.astype(BF16)


def backward(where, grad_parts, gate_weight, up_weight, places, total_places):
    columns, depth = gate_weight.shape
    rows = grad_parts[0].shape[0] * len(grad_parts)
    outs = CORES if total_places else 1
    tile = columns // total_places if total_places else tile_of(columns, 512)
    places = places if total_places else range(columns // tile)
    return pl.pallas_call(
        functools.partial(backward_kernel, places, total_places),
        in_specs=[SMEM] + [VMEM] * (len(grad_parts) + 2),
        out_specs=[VMEM] * outs,
        out_shape=[array(rows, tile * len(places) // outs)] * outs,
        scratch_shapes=[pltpu.VMEM((rows, depth), BF16)] * 2 + [pltpu.VMEM((rows, tile), BF16)],
        compiler_params=PARAMS,
        cost_estimate=cost(rows, 2 * depth, tile * len(places)),
        name="backward_product",
    )(
        where,
        *grad_parts,
        pltpu.with_memory_space_constraint(gate_weight, pltpu.VMEM),
        pltpu.with_memory_space_constraint(up_weight, pltpu.VMEM),
    )


def pair_kernel(own_ref, other_ref, *out_refs):
    width = out_refs[0].shape[1]
    for j, out_ref in enumerate(out_refs):
        columns = slice(j * width, (j + 1) * width)
        out_ref[...] = (own_ref[:, columns].astype(F32) + other_ref[:, columns].astype(F32)).astype(
            BF16
        )


def pair_sums(own, other, count, width):
    rows = own.shape[0]
    return pl.pallas_call(
        pair_kernel,
        in_specs=[VMEM] * 2,
        out_specs=[VMEM] * count,
        out_shape=[array(rows, width)] * count,
        compiler_params=PARAMS,
        name="pair_sums",
    )(own, other)


def final_kernel(blocks, done, where_ref, *refs):
    done_refs, in_refs, out_ref = refs[:done], refs[done:-1], refs[-1]
    rows = in_refs[0].shape[0] // blocks
    width = out_ref.shape[1]
    at = 0
    for done_ref in done_refs:
        out_ref[at : at + done_ref.shape[0]] = done_ref[...]
        at += done_ref.shape[0]
    for q in range(blocks):
        total = None
        for ref in in_refs:
            value = ref[q * rows : (q + 1) * rows, ref.shape[1] - width :].astype(F32)
            total = value if total is None else total + value
        start = pl.multiple_of(at + (where_ref[0] ^ q) * rows, rows)
        out_ref[pl.ds(start, rows)] = total.astype(BF16)


def final_sum(where, done, terms, blocks, width):
    rows = terms[0].shape[0] + sum(part.shape[0] for part in done)
    return pl.pallas_call(
        functools.partial(final_kernel, blocks, len(done)),
        in_specs=[SMEM] + [VMEM] * (len(done) + len(terms)),
        out_specs=VMEM,
        out_shape=array(rows, width),
        compiler_params=PARAMS,
        name="final_sum",
    )(where, *done, *terms)


def local(
    n_tp, n_dp, inputs, cotangent, gate_code, gate_scale, up_code, up_scale, down_code, down_scale
):
    n_z = n_tp // CORES
    width = inputs.shape[1]
    hidden = gate_code.shape[1]
    steps = n_dp.bit_length() - 1
    by_blocks = width % BLOCK == 0
    tp = lax.axis_index("tp")
    where = jnp.stack([lax.axis_index("dp"), tp // CORES, tp % CORES]).astype(jnp.int32)

    def exchange(value, step):
        pairs = []
        for i in range(n_tp):
            bit = 1 << (step if i % CORES == 0 else steps - 1 - step)
            pairs += [(i * n_dp + k, i * n_dp + (k ^ bit)) for k in range(n_dp)]
        return lax.ppermute(value, ("tp", "dp"), pairs)

    def swap_cores(value):
        return lax.ppermute(value, "tp", [(i, i ^ 1) for i in range(n_tp)])

    def along(value, places):
        return lax.ppermute(
            value, "tp", [(i, (i + places * CORES) % n_tp) for i in range(n_tp)]
        )

    def between(value, pairs):
        return lax.ppermute(
            value,
            "tp",
            [(i * CORES + c, k * CORES + c) for i, k in pairs for c in range(CORES)],
        )

    hops = by_blocks and n_z == 4

    def set_out(piece):
        if not by_blocks:
            return [lax.all_gather(piece, "tp", axis=1, tiled=True)]
        if hops:
            return [along(piece, 2)]
        return [along(piece, n_z - j) for j in range(1, n_z)]

    def near(piece, got):
        return [*got, between(piece, [(0, 1), (1, 0), (2, 3), (3, 2)])] if hops else got

    def pass_on(piece, got):
        if not hops:
            return got
        return [*got, between(piece, [(1, 2), (2, 1)]), between(got[0], [(1, 0), (2, 3)])]

    def arrive(piece, got):
        if not by_blocks:
            return got
        own = join_four(where, (piece, *got)) if hops else join([piece, *got])
        return [own, swap_cores(own)]

    groups, stays = [[0]], [0]
    for step in reversed(range(steps)):
        groups.insert(0, [q | 1 << step for q in stays])
        stays = groups[0] + stays

    def send(parts, step=0):
        return [*parts, exchange(parts[step], step)]

    def take(parts, step=0):
        parts, at = list(parts), 0
        for later in range(step + 1, steps):
            height = parts[later].shape[0]
            came = parts[-1][at : at + height].astype(F32)
            parts[later] = (parts[later].astype(F32) + came).astype(BF16)
            at += height
        return parts

    def settle(parts):
        for step in range(1, steps):
            parts = send(take(parts, step - 1), step)
        return parts

    def terms_of(parts):
        return parts[steps:]

    def start_rows(value):
        return (
            {0: value, 1: exchange(value, 0)},
            {1 << step: exchange(value, step) for step in range(1, steps)},
        )

    def finish_rows(have, late):
        have = dict(have)
        for step in range(1, steps):
            for q in list(have):
                have[q | 1 << step] = exchange(have[q], step) if q else late[1 << step]
        return [have[q] for q in range(n_dp)]

    whole = [[2, 1, 3, 0] if hops else [*range(1, n_z), 0]]
    parts_of_z = [[2], [1, 3], [0]] if hops else whole

    def products(grad_parts, places):
        return backward(
            where, grad_parts, gate_weight, up_weight, places, n_z if by_blocks else 0
        )

    def swapped(partial):
        return [partial[0], swap_cores(partial[1])] if by_blocks else partial

    def sums_of(partial, places):
        away = [j for j in places if j]
        return pair_sums(*partial, len(away), width) if by_blocks and away else []

    def spread(sums, partial, places):
        if not by_blocks:
            return [lax.psum_scatter(partial[0], "tp", scatter_dimension=1, tiled=True)]
        terms = [along(part, j) for j, part in zip([j for j in places if j], sums)]
        return terms + (list(partial) if 0 in places else [])

    def scatter(partial, places):
        return spread(sums_of(partial, places), partial, places)

    rows = inputs.shape[0] // CHUNKS // n_dp

    def hold(values):
        nonlocal where
        values, where = lax.optimization_barrier((values, where))
        return values

    in_1, co_1, in_2, co_2 = prepare(where, inputs, cotangent, n_dp)
    got_in_1 = near(in_1, set_out(in_1))
    gate_weight = weight(gate_code, gate_scale, True)
    gate_weight, got_in_1, co_1 = hold((gate_weight, got_in_1, co_1))

    got_in_1 = pass_on(in_1, got_in_1)
    got_co_1 = near(co_1, set_out(co_1))
    up_weight = weight(up_code, up_scale, True)
    up_weight, got_in_1, got_co_1 = hold((up_weight, got_in_1, got_co_1))

    x = arrive(in_1, got_in_1)
    got_co_1 = pass_on(co_1, got_co_1)
    gate_up_1 = forward(where, x, [gate_weight, up_weight], groups, 0, width)
    gate_up_1, got_co_1, in_2 = hold((gate_up_1, got_co_1, in_2))

    gate_up_1 = send(gate_up_1)
    x = arrive(co_1, got_co_1)
    got_in_2 = near(in_2, set_out(in_2))
    hidden_1 = forward_streamed(where, x, down_code, down_scale, groups, width)
    hidden_1, gate_up_1, got_in_2, co_2 = hold((hidden_1, gate_up_1, got_in_2, co_2))

    hidden_1 = send(hidden_1)
    got_co_2 = near(co_2, set_out(co_2))
    got_in_2 = hold(pass_on(in_2, got_in_2))

    gate_up_1 = settle(gate_up_1)
    x = arrive(in_2, got_in_2)
    x, hidden_1, got_co_2 = hold((x, hidden_1, got_co_2))

    hidden_1 = settle(hidden_1)
    got_co_2 = pass_on(co_2, got_co_2)
    gate_up_2 = forward(where, x, [gate_weight, up_weight], groups, 0, width)
    gate_up_2, got_co_2, gate_up_1, hidden_1 = hold((gate_up_2, got_co_2, gate_up_1, hidden_1))

    gate_up_2 = send(gate_up_2)
    grad_1 = grads(where, terms_of(gate_up_1), terms_of(hidden_1), rows, hidden)
    x, grad_1 = hold((arrive(co_2, got_co_2), grad_1))

    early_1, late_1 = start_rows(grad_1)
    hidden_2 = forward_streamed(where, x, down_code, down_scale, groups, width)
    hidden_2 = hold(hidden_2)

    hidden_2 = send(hidden_2)
    early_1, gate_up_2 = hold((early_1, gate_up_2))

    parts_1 = finish_rows(early_1, late_1)
    parts_1, hidden_2 = hold((parts_1, hidden_2))

    hidden_2 = settle(hidden_2)
    gate_up_2 = settle(gate_up_2)
    partial_1 = products(parts_1, whole[0])
    hidden_2, gate_up_2, partial_1 = hold((hidden_2, gate_up_2, partial_1))

    partial_1 = swapped(partial_1)
    grad_2 = grads(where, terms_of(gate_up_2), terms_of(hidden_2), rows, hidden)
    early_2, late_2 = start_rows(grad_2)
    terms_1 = scatter(partial_1, whole[0])
    early_2, early = hold((early_2, terms_1[:1]))
    parts_2 = finish_rows(early_2, late_2)
    parts_2, later = hold((parts_2, terms_1[1:2]))
    terms_1 = [*early, *later, *terms_1[2:]]

    terms_2 = []
    partial, before = products(parts_2, parts_of_z[0]), parts_of_z[0]
    for places in parts_of_z[1:]:
        following = products(parts_2, places) if len(places) > 1 else None
        partial, following, terms_1 = hold((swapped(partial), following, terms_1))
        sums = hold(sums_of(partial, before))
        terms_2 += spread(sums, partial, before)
        partial = following or products(parts_2, places)
        before = places
    partial = swapped(partial)
    terms_2 += spread(sums_of(partial, before), partial, before)
    done = [final_sum(where, [], terms_1, n_dp, width)]
    return final_sum(where, done, terms_2, n_dp, width)


def solution(mesh):
    placed = (
        P("groups", ("dp", "tp")),
        P("groups", ("dp", "tp")),
        P("dp", "tp"),
        P("dp", "tp"),
        P("dp", "tp"),
        P("dp", "tp"),
        P("tp", "dp"),
        P("tp", "dp"),
    )
    return jax.shard_map(
        functools.partial(local, mesh.shape["tp"], mesh.shape["dp"]),
        mesh=mesh,
        in_specs=placed,
        out_specs=P("groups", ("dp", "tp")),
        check_vma=False,
    )
```

```python
import functools

import jax
import jax.numpy as jnp
from jax import lax
from jax.experimental import pallas as pl
from jax.experimental.pallas import tpu as pltpu
from jax.sharding import PartitionSpec as P

BLOCK = 128
CORES = 2
CHUNKS = 2
BF16 = jnp.bfloat16
F32 = jnp.float32
PARAMS = pltpu.CompilerParams(vmem_limit_bytes=8 << 20)
VMEM = pl.BlockSpec(memory_space=pltpu.VMEM)
SMEM = pl.BlockSpec(memory_space=pltpu.SMEM)


def tile_of(extent, most):
    best = BLOCK
    for size in range(BLOCK, most + 1, BLOCK):
        if extent % size == 0:
            best = size
    return best


def dot(left, right, contract):
    return lax.dot_general(
        left, right, (((1,), (contract,)), ((), ())), preferred_element_type=F32
    )


def cost(rows, depth, columns):
    return pl.CostEstimate(
        flops=1024, bytes_accessed=1024, transcendentals=0
    )


def array(rows, columns):
    return jax.ShapeDtypeStruct((rows, columns), BF16)


def reversed_bits(q, count):
    width = count.bit_length() - 1
    return sum(((q >> i) & 1) << (width - 1 - i) for i in range(width))


def block_of(q, count, core):
    return q + core * (reversed_bits(q, count) - q)


def weight_kernel(turned, code_ref, scale_ref, weight_ref, buffer, sems):
    slots, rows = buffer.shape[:2]
    count = code_ref.shape[0] // rows

    def fetch(i):
        slot = lax.rem(i, slots)
        return pltpu.make_async_copy(
            code_ref.at[pl.ds(pl.multiple_of(i * rows, rows), rows)], buffer.at[slot], sems.at[slot]
        )

    for i in range(min(slots, count)):
        fetch(i).start()

    def body(i, carry):
        fetch(i).wait()
        slot = lax.rem(i, slots)
        start = pl.multiple_of(i * rows, rows)
        for c in range(code_ref.shape[1] // BLOCK):
            columns = slice(c * BLOCK, (c + 1) * BLOCK)
            weight_ref[pl.ds(start, rows), columns] = (
                buffer[slot, :, columns].astype(F32) * (scale_ref[c, i] if turned else scale_ref[i, c])
            ).astype(BF16)

        @pl.when(i + slots < count)
        def _():
            fetch(i + slots).start()

        return carry

    lax.fori_loop(0, count, body, 0)


def weight(code, scale, turned):
    slots = 6
    scale = scale.T if turned else scale
    return pl.pallas_call(
        functools.partial(weight_kernel, turned),
        in_specs=[pl.BlockSpec(memory_space=pltpu.HBM), SMEM],
        out_specs=VMEM,
        out_shape=pltpu.VMEM(code.shape, BF16),
        scratch_shapes=[
            pltpu.VMEM((slots, BLOCK, code.shape[1]), BF16),
            pltpu.SemaphoreType.DMA((slots,)),
        ],
        compiler_params=pltpu.CompilerParams(vmem_limit_bytes=10 << 20),
        cost_estimate=pl.CostEstimate(
            flops=0, bytes_accessed=code.size // 4096, transcendentals=0
        ),
        name="scaled_weight",
    )(pltpu.with_memory_space_constraint(code, pltpu.HBM), scale)


def prep_kernel(rows, where_ref, inputs_ref, cotangent_ref, *refs):
    *out_refs, sem = refs
    count = inputs_ref.shape[0] // CHUNKS // rows
    copies = []
    for at, out_ref in enumerate(out_refs):
        for q in range(count):
            start = pl.multiple_of((at // 2 * count + (where_ref[0] ^ q)) * rows, rows)
            copies.append(
                pltpu.make_async_copy(
                    (inputs_ref, cotangent_ref)[at % 2].at[pl.ds(start, rows)],
                    out_ref.at[pl.ds(q * rows, rows)],
                    sem.at[len(copies)],
                )
            )
            copies[-1].start()
    for copy in copies:
        copy.wait()


def prepare(where, inputs, cotangent, n_dp):
    seq, width = inputs.shape
    return pl.pallas_call(
        functools.partial(prep_kernel, seq // CHUNKS // n_dp),
        in_specs=[SMEM] + [pl.BlockSpec(memory_space=pltpu.HBM)] * 2,
        out_specs=[VMEM] * (2 * CHUNKS),
        out_shape=[array(seq // CHUNKS, width)] * (2 * CHUNKS),
        scratch_shapes=[pltpu.SemaphoreType.DMA((2 * CHUNKS * n_dp,))],
        compiler_params=PARAMS,
        name="order_rows",
    )(
        where,
        pltpu.with_memory_space_constraint(inputs, pltpu.HBM),
        pltpu.with_memory_space_constraint(cotangent, pltpu.HBM),
    )


def join_kernel(*refs):
    *part_refs, out_ref = refs
    width = part_refs[0].shape[1]
    for j, part_ref in enumerate(part_refs):
        out_ref[:, j * width : (j + 1) * width] = part_ref[...]


def join(parts):
    rows, width = parts[0].shape
    return pl.pallas_call(
        join_kernel,
        in_specs=[VMEM] * len(parts),
        out_specs=VMEM,
        out_shape=array(rows, width * len(parts)),
        compiler_params=PARAMS,
        name="join",
    )(*parts)


def join_four_kernel(where_ref, own_ref, two_ref, near_ref, middle_ref, passed_ref, out_ref):
    width = own_ref.shape[1]
    place = where_ref[1]
    out_ref[:, :width] = own_ref[...]
    out_ref[:, 2 * width : 3 * width] = two_ref[...]
    odd = lax.rem(place, 2)
    out_ref[:, pl.ds(pl.multiple_of((1 + 2 * odd) * width, width), width)] = near_ref[...]
    rest = pl.ds(pl.multiple_of((3 - 2 * odd) * width, width), width)
    inner = jnp.logical_or(place == 1, place == 2)

    @pl.when(inner)
    def _():
        out_ref[:, rest] = middle_ref[...]

    @pl.when(jnp.logical_not(inner))
    def _():
        out_ref[:, rest] = passed_ref[...]


def join_four(where, parts):
    rows, width = parts[0].shape
    return pl.pallas_call(
        join_four_kernel,
        in_specs=[SMEM] + [VMEM] * len(parts),
        out_specs=VMEM,
        out_shape=array(rows, 4 * width),
        compiler_params=PARAMS,
        name="join",
    )(where, *parts)


def assemble(width, blocks, where_ref, x_refs, x_all):
    rows = x_all.shape[0] // blocks
    for q in range(blocks):
        start = pl.multiple_of(block_of(q, blocks, where_ref[2]) * rows, rows)
        own = slice(q * rows, (q + 1) * rows)
        if len(x_refs) == 1:
            x_all[own] = x_refs[0][pl.ds(start, rows)]
            continue
        count = x_all.shape[1] // (CORES * width)
        for j in range(count):
            for core, x_ref in enumerate(x_refs):
                place = lax.rem(where_ref[1] + j, count) * CORES + (where_ref[2] ^ core)
                x_all[own, pl.ds(pl.multiple_of(place * width, width), width)] = x_ref[
                    pl.ds(start, rows), j * width : (j + 1) * width
                ]


def forward_kernel(groups, contract, width, count, where_ref, *refs):
    outs = len(groups)
    x_refs, weight_refs = refs[: -outs - 1 - count], refs[-outs - 1 - count : -outs - 1]
    out_refs, x_all = refs[-outs - 1 : -1], refs[-1]
    blocks = sum(len(group) for group in groups)
    assemble(width, blocks, where_ref, x_refs, x_all)
    columns = out_refs[0].shape[1] // count
    rows = x_all.shape[0] // blocks
    tile = tile_of(columns, 512)
    for at, weight_ref in enumerate(weight_refs):
        for n in range(0, columns, tile):
            part = weight_ref[n : n + tile, :] if contract else weight_ref[:, n : n + tile]
            total = dot(x_all[...], part, contract).astype(BF16)
            place = slice(at * columns + n, at * columns + n + tile)
            for out_ref, group in zip(out_refs, groups):
                for i, q in enumerate(group):
                    out_ref[i * rows : (i + 1) * rows, place] = total[q * rows : (q + 1) * rows]


def forward(where, x, weights, groups, contract, width):
    rows, blocks = x[0].shape[0], sum(len(group) for group in groups)
    depth, columns = weights[0].shape[contract], weights[0].shape[1 - contract]
    outs = [array(rows * len(group) // blocks, columns * len(weights)) for group in groups]
    return pl.pallas_call(
        functools.partial(forward_kernel, groups, contract, width, len(weights)),
        in_specs=[SMEM] + [VMEM] * (len(x) + len(weights)),
        out_specs=[VMEM] * len(outs),
        out_shape=outs,
        scratch_shapes=[pltpu.VMEM((rows, depth), BF16)],
        compiler_params=PARAMS,
        cost_estimate=cost(rows, depth, columns),
        name="forward_product",
    )(where, *x, *(pltpu.with_memory_space_constraint(part, pltpu.VMEM) for part in weights))


def streamed_kernel(groups, width, where_ref, scale_ref, *refs):
    outs = len(groups)
    x_refs, code_ref = refs[: -outs - 4], refs[-outs - 4]
    out_refs, (x_all, buffer, sems) = refs[-outs - 3 : -3], refs[-3:]
    slots, tile, depth = buffer.shape
    count = code_ref.shape[0] // tile
    blocks = sum(len(group) for group in groups)
    rows = x_all.shape[0] // blocks
    step = tile_of(depth, 512)

    def fetch(i):
        slot = lax.rem(i, slots)
        return pltpu.make_async_copy(
            code_ref.at[pl.ds(pl.multiple_of(i * tile, tile), tile)], buffer.at[slot], sems.at[slot]
        )

    for i in range(min(slots, count)):
        fetch(i).start()
    assemble(width, blocks, where_ref, x_refs, x_all)

    def body(i, carry):
        fetch(i).wait()
        slot = lax.rem(i, slots)
        total = None
        for k in range(0, depth, step):
            lines = []
            for r in range(tile // BLOCK):
                lines.append(
                    jnp.concatenate(
                        [
                            (
                                buffer[slot, r * BLOCK : (r + 1) * BLOCK, c : c + BLOCK].astype(F32)
                                * scale_ref[i * (tile // BLOCK) + r, c // BLOCK]
                            ).astype(BF16)
                            for c in range(k, k + step, BLOCK)
                        ],
                        axis=1,
                    )
                )
            term = dot(x_all[:, k : k + step], jnp.concatenate(lines, axis=0), 1)
            total = term if total is None else total + term
        total = total.astype(BF16)
        columns = pl.ds(pl.multiple_of(i * tile, tile), tile)
        for out_ref, group in zip(out_refs, groups):
            for at, q in enumerate(group):
                out_ref[at * rows : (at + 1) * rows, columns] = total[q * rows : (q + 1) * rows]

        @pl.when(i + slots < count)
        def _():
            fetch(i + slots).start()

        return carry

    lax.fori_loop(0, count, body, 0)


def forward_streamed(where, x, code, scale, groups, width):
    rows, blocks = x[0].shape[0], sum(len(group) for group in groups)
    columns, depth = code.shape
    tile, slots = tile_of(columns, 256), 3
    return pl.pallas_call(
        functools.partial(streamed_kernel, groups, width),
        in_specs=[SMEM] * 2 + [VMEM] * len(x) + [pl.BlockSpec(memory_space=pltpu.HBM)],
        out_specs=[VMEM] * len(groups),
        out_shape=[array(rows * len(group) // blocks, columns) for group in groups],
        scratch_shapes=[
            pltpu.VMEM((rows, depth), BF16),
            pltpu.VMEM((slots, tile, depth), BF16),
            pltpu.SemaphoreType.DMA((slots,)),
        ],
        compiler_params=pltpu.CompilerParams(vmem_limit_bytes=14 << 20),
        cost_estimate=cost(rows, depth, columns),
        name="forward_streamed",
    )(where, scale, *x, pltpu.with_memory_space_constraint(code, pltpu.HBM))


def grads_kernel(both, where_ref, *refs):
    *in_refs, out_ref = refs
    rows, width = out_ref.shape[0], out_ref.shape[1] // 2
    tile = tile_of(width, 512)

    def total(terms, n):
        values = [term[term.shape[0] - rows :, n : n + tile].astype(F32) for term in terms]
        return functools.reduce(lambda left, right: left + right, values)

    for n in range(0, width, tile):
        gate_pre = total(in_refs[:both], n)
        up_pre = total(in_refs[:both], width + n)
        hidden_grad = total(in_refs[both:], n)
        gate_sig = jax.nn.sigmoid(gate_pre)
        out_ref[:, n : n + tile] = (
            hidden_grad * up_pre * gate_sig * (1.0 + gate_pre * (1.0 - gate_sig))
        ).astype(BF16)
        out_ref[:, width + n : width + n + tile] = (hidden_grad * gate_pre * gate_sig).astype(BF16)


def grads(where, gate_up, hidden_terms, rows, width):
    return pl.pallas_call(
        functools.partial(grads_kernel, len(gate_up)),
        in_specs=[SMEM] + [VMEM] * (len(gate_up) + len(hidden_terms)),
        out_specs=VMEM,
        out_shape=array(rows, 2 * width),
        compiler_params=PARAMS,
        name="hidden_grads",
    )(where, *gate_up, *hidden_terms)


def backward_kernel(places, total_places, where_ref, *refs):
    outs = CORES if total_places else 1
    *grad_refs, gate_ref, up_ref = refs[: -3 - outs]
    *out_refs, gate_all, up_all, total_ref = refs[-3 - outs :]
    blocks, rows = len(grad_refs), grad_refs[0].shape[0]
    depth = gate_all.shape[1]
    for q, grad_ref in enumerate(grad_refs):
        start = pl.multiple_of(block_of(q, blocks, where_ref[2]) * rows, rows)
        gate_all[pl.ds(start, rows)] = grad_ref[:, :depth]
        up_all[pl.ds(start, rows)] = grad_ref[:, depth:]
    tile = total_ref.shape[1]
    for at, j in enumerate(places):
        place = lax.rem(where_ref[1] + j, total_places) if total_places else j
        part = pl.ds(pl.multiple_of(place * tile, tile), tile)
        total = dot(gate_all[...], gate_ref[part, :], 1) + dot(up_all[...], up_ref[part, :], 1)
        if total_places:
            width = tile // CORES
            total_ref[...] = total.astype(BF16)
            for out_ref, core in zip(out_refs, (where_ref[2], 1 - where_ref[2])):
                out_ref[:, at * width : (at + 1) * width] = total_ref[
                    :, pl.ds(pl.multiple_of(core * width, width), width)
                ]
        else:
            out_refs[0][:, at * tile : (at + 1) * tile] = total.astype(BF16)


def backward(where, grad_parts, gate_weight, up_weight, places, total_places):
    columns, depth = gate_weight.shape
    rows = grad_parts[0].shape[0] * len(grad_parts)
    outs = CORES if total_places else 1
    tile = columns // total_places if total_places else tile_of(columns, 512)
    places = places if total_places else range(columns // tile)
    return pl.pallas_call(
        functools.partial(backward_kernel, places, total_places),
        in_specs=[SMEM] + [VMEM] * (len(grad_parts) + 2),
        out_specs=[VMEM] * outs,
        out_shape=[array(rows, tile * len(places) // outs)] * outs,
        scratch_shapes=[pltpu.VMEM((rows, depth), BF16)] * 2 + [pltpu.VMEM((rows, tile), BF16)],
        compiler_params=PARAMS,
        cost_estimate=cost(rows, 2 * depth, tile * len(places)),
        name="backward_product",
    )(
        where,
        *grad_parts,
        pltpu.with_memory_space_constraint(gate_weight, pltpu.VMEM),
        pltpu.with_memory_space_constraint(up_weight, pltpu.VMEM),
    )


def pair_kernel(own_ref, other_ref, *out_refs):
    width = out_refs[0].shape[1]
    for j, out_ref in enumerate(out_refs):
        columns = slice(j * width, (j + 1) * width)
        out_ref[...] = (own_ref[:, columns].astype(F32) + other_ref[:, columns].astype(F32)).astype(
            BF16
        )


def pair_sums(own, other, count, width):
    rows = own.shape[0]
    return pl.pallas_call(
        pair_kernel,
        in_specs=[VMEM] * 2,
        out_specs=[VMEM] * count,
        out_shape=[array(rows, width)] * count,
        compiler_params=PARAMS,
        name="pair_sums",
    )(own, other)


def final_kernel(blocks, done, where_ref, *refs):
    done_refs, in_refs, out_ref = refs[:done], refs[done:-1], refs[-1]
    rows = in_refs[0].shape[0] // blocks
    width = out_ref.shape[1]
    at = 0
    for done_ref in done_refs:
        out_ref[at : at + done_ref.shape[0]] = done_ref[...]
        at += done_ref.shape[0]
    for q in range(blocks):
        total = None
        for ref in in_refs:
            value = ref[q * rows : (q + 1) * rows, ref.shape[1] - width :].astype(F32)
            total = value if total is None else total + value
        start = pl.multiple_of(at + (where_ref[0] ^ q) * rows, rows)
        out_ref[pl.ds(start, rows)] = total.astype(BF16)


def final_sum(where, done, terms, blocks, width):
    rows = terms[0].shape[0] + sum(part.shape[0] for part in done)
    return pl.pallas_call(
        functools.partial(final_kernel, blocks, len(done)),
        in_specs=[SMEM] + [VMEM] * (len(done) + len(terms)),
        out_specs=VMEM,
        out_shape=array(rows, width),
        compiler_params=PARAMS,
        name="final_sum",
    )(where, *done, *terms)


def local(
    n_tp, n_dp, inputs, cotangent, gate_code, gate_scale, up_code, up_scale, down_code, down_scale
):
    n_z = n_tp // CORES
    width = inputs.shape[1]
    hidden = gate_code.shape[1]
    steps = n_dp.bit_length() - 1
    by_blocks = width % BLOCK == 0
    tp = lax.axis_index("tp")
    where = jnp.stack([lax.axis_index("dp"), tp // CORES, tp % CORES]).astype(jnp.int32)

    def exchange(value, step):
        pairs = []
        for i in range(n_tp):
            bit = 1 << (step if i % CORES == 0 else steps - 1 - step)
            pairs += [(i * n_dp + k, i * n_dp + (k ^ bit)) for k in range(n_dp)]
        return lax.ppermute(value, ("tp", "dp"), pairs)

    def swap_cores(value):
        return lax.ppermute(value, "tp", [(i, i ^ 1) for i in range(n_tp)])

    def along(value, places):
        return lax.ppermute(
            value, "tp", [(i, (i + places * CORES) % n_tp) for i in range(n_tp)]
        )

    def between(value, pairs):
        return lax.ppermute(
            value,
            "tp",
            [(i * CORES + c, k * CORES + c) for i, k in pairs for c in range(CORES)],
        )

    hops = by_blocks and n_z == 4

    def set_out(piece):
        if not by_blocks:
            return [lax.all_gather(piece, "tp", axis=1, tiled=True)]
        if hops:
            return [along(piece, 2)]
        return [along(piece, n_z - j) for j in range(1, n_z)]

    def near(piece, got):
        return [*got, between(piece, [(0, 1), (1, 0), (2, 3), (3, 2)])] if hops else got

    def pass_on(piece, got):
        if not hops:
            return got
        return [*got, between(piece, [(1, 2), (2, 1)]), between(got[0], [(1, 0), (2, 3)])]

    def arrive(piece, got):
        if not by_blocks:
            return got
        own = join_four(where, (piece, *got)) if hops else join([piece, *got])
        return [own, swap_cores(own)]

    groups, stays = [[0]], [0]
    for step in reversed(range(steps)):
        groups.insert(0, [q | 1 << step for q in stays])
        stays = groups[0] + stays

    def send(parts, step=0):
        return [*parts, exchange(parts[step], step)]

    def take(parts, step=0):
        parts, at = list(parts), 0
        for later in range(step + 1, steps):
            height = parts[later].shape[0]
            came = parts[-1][at : at + height].astype(F32)
            parts[later] = (parts[later].astype(F32) + came).astype(BF16)
            at += height
        return parts

    def settle(parts):
        for step in range(1, steps):
            parts = send(take(parts, step - 1), step)
        return parts

    def terms_of(parts):
        return parts[steps:]

    def start_rows(value):
        return (
            {0: value, 1: exchange(value, 0)},
            {1 << step: exchange(value, step) for step in range(1, steps)},
        )

    def finish_rows(have, late):
        have = dict(have)
        for step in range(1, steps):
            for q in list(have):
                have[q | 1 << step] = exchange(have[q], step) if q else late[1 << step]
        return [have[q] for q in range(n_dp)]

    whole = [[2, 1, 3, 0] if hops else [*range(1, n_z), 0]]
    parts_of_z = [[2], [1, 3], [0]] if hops else whole

    def products(grad_parts, places):
        return backward(
            where, grad_parts, gate_weight, up_weight, places, n_z if by_blocks else 0
        )

    def swapped(partial):
        return [partial[0], swap_cores(partial[1])] if by_blocks else partial

    def sums_of(partial, places):
        away = [j for j in places if j]
        return pair_sums(*partial, len(away), width) if by_blocks and away else []

    def spread(sums, partial, places):
        if not by_blocks:
            return [lax.psum_scatter(partial[0], "tp", scatter_dimension=1, tiled=True)]
        terms = [along(part, j) for j, part in zip([j for j in places if j], sums)]
        return terms + (list(partial) if 0 in places else [])

    def scatter(partial, places):
        return spread(sums_of(partial, places), partial, places)

    rows = inputs.shape[0] // CHUNKS // n_dp

    def hold(values):
        nonlocal where
        values, where = lax.optimization_barrier((values, where))
        return values

    in_1, co_1, in_2, co_2 = prepare(where, inputs, cotangent, n_dp)
    got_in_1 = near(in_1, set_out(in_1))
    gate_weight = weight(gate_code, gate_scale, True)
    gate_weight, got_in_1, co_1 = hold((gate_weight, got_in_1, co_1))

    got_in_1 = pass_on(in_1, got_in_1)
    got_co_1 = near(co_1, set_out(co_1))
    up_weight = weight(up_code, up_scale, True)
    up_weight, got_in_1, got_co_1 = hold((up_weight, got_in_1, got_co_1))

    x = arrive(in_1, got_in_1)
    got_co_1 = pass_on(co_1, got_co_1)
    gate_up_1 = forward(where, x, [gate_weight, up_weight], groups, 0, width)
    gate_up_1, got_co_1, in_2 = hold((gate_up_1, got_co_1, in_2))

    gate_up_1 = send(gate_up_1)
    x = arrive(co_1, got_co_1)
    got_in_2 = near(in_2, set_out(in_2))
    hidden_1 = forward_streamed(where, x, down_code, down_scale, groups, width)
    hidden_1, gate_up_1, got_in_2, co_2 = hold((hidden_1, gate_up_1, got_in_2, co_2))

    hidden_1 = send(hidden_1)
    got_co_2 = near(co_2, set_out(co_2))
    got_in_2 = hold(pass_on(in_2, got_in_2))

    gate_up_1 = settle(gate_up_1)
    x = arrive(in_2, got_in_2)
    x, hidden_1, got_co_2 = hold((x, hidden_1, got_co_2))

    hidden_1 = settle(hidden_1)
    got_co_2 = pass_on(co_2, got_co_2)
    gate_up_2 = forward(where, x, [gate_weight, up_weight], groups, 0, width)
    gate_up_2, got_co_2, gate_up_1, hidden_1 = hold((gate_up_2, got_co_2, gate_up_1, hidden_1))

    gate_up_2 = send(gate_up_2)
    grad_1 = grads(where, terms_of(gate_up_1), terms_of(hidden_1), rows, hidden)
    x, grad_1 = hold((arrive(co_2, got_co_2), grad_1))

    early_1, late_1 = start_rows(grad_1)
    hidden_2 = forward_streamed(where, x, down_code, down_scale, groups, width)
    hidden_2 = hold(hidden_2)

    hidden_2 = send(hidden_2)
    gate_up_2 = hold(gate_up_2)

    gate_up_2 = settle(gate_up_2)
    early_1, hidden_2 = hold((early_1, hidden_2))

    hidden_2 = settle(hidden_2)
    parts_1 = finish_rows(early_1, late_1)
    hidden_2, gate_up_2 = hold((hidden_2, gate_up_2))

    grad_2 = grads(where, terms_of(gate_up_2), terms_of(hidden_2), rows, hidden)
    early_2, late_2 = start_rows(grad_2)
    parts_1, grad_2 = hold((parts_1, grad_2))

    partial_1 = products(parts_1, whole[0])
    partial_1, early_2 = hold((partial_1, early_2))

    parts_2 = finish_rows(early_2, late_2)
    partial_1 = hold(swapped(partial_1))

    terms_1 = scatter(partial_1, whole[0])
    parts_2, early = hold((parts_2, terms_1[:1]))
    terms_1 = [*early, *terms_1[1:]]

    terms_2 = []
    partial, before = products(parts_2, parts_of_z[0]), parts_of_z[0]
    for places in parts_of_z[1:]:
        following = products(parts_2, places) if len(places) > 1 else None
        partial, following, terms_1 = hold((swapped(partial), following, terms_1))
        sums = hold(sums_of(partial, before))
        terms_2 += spread(sums, partial, before)
        partial = following or products(parts_2, places)
        before = places
    partial = swapped(partial)
    terms_2 += spread(sums_of(partial, before), partial, before)
    done = [final_sum(where, [], terms_1, n_dp, width)]
    return final_sum(where, done, terms_2, n_dp, width)


def solution(mesh):
    placed = (
        P("groups", ("dp", "tp")),
        P("groups", ("dp", "tp")),
        P("dp", "tp"),
        P("dp", "tp"),
        P("dp", "tp"),
        P("dp", "tp"),
        P("tp", "dp"),
        P("tp", "dp"),
    )
    return jax.shard_map(
        functools.partial(local, mesh.shape["tp"], mesh.shape["dp"]),
        mesh=mesh,
        in_specs=placed,
        out_specs=P("groups", ("dp", "tp")),
        check_vma=False,
    )
```

```python
import functools

import jax
import jax.numpy as jnp
from jax import lax
from jax.experimental import pallas as pl
from jax.experimental.pallas import tpu as pltpu
from jax.sharding import PartitionSpec as P

BLOCK = 128
CORES = 2
CHUNKS = 2
BF16 = jnp.bfloat16
F32 = jnp.float32
PARAMS = pltpu.CompilerParams(vmem_limit_bytes=8 << 20)
VMEM = pl.BlockSpec(memory_space=pltpu.VMEM)
SMEM = pl.BlockSpec(memory_space=pltpu.SMEM)


def tile_of(extent, most):
    best = BLOCK
    for size in range(BLOCK, most + 1, BLOCK):
        if extent % size == 0:
            best = size
    return best


def dot(left, right, contract):
    return lax.dot_general(
        left, right, (((1,), (contract,)), ((), ())), preferred_element_type=F32
    )


def cost(rows, depth, columns):
    return pl.CostEstimate(
        flops=1024, bytes_accessed=1024, transcendentals=0
    )


def array(rows, columns):
    return jax.ShapeDtypeStruct((rows, columns), BF16)


def reversed_bits(q, count):
    width = count.bit_length() - 1
    return sum(((q >> i) & 1) << (width - 1 - i) for i in range(width))


def block_of(q, count, core):
    return q + core * (reversed_bits(q, count) - q)


def weight_kernel(turned, code_ref, scale_ref, weight_ref, buffer, sems):
    slots, rows = buffer.shape[:2]
    count = code_ref.shape[0] // rows

    def fetch(i):
        slot = lax.rem(i, slots)
        return pltpu.make_async_copy(
            code_ref.at[pl.ds(pl.multiple_of(i * rows, rows), rows)], buffer.at[slot], sems.at[slot]
        )

    for i in range(min(slots, count)):
        fetch(i).start()

    def body(i, carry):
        fetch(i).wait()
        slot = lax.rem(i, slots)
        start = pl.multiple_of(i * rows, rows)
        for c in range(code_ref.shape[1] // BLOCK):
            columns = slice(c * BLOCK, (c + 1) * BLOCK)
            weight_ref[pl.ds(start, rows), columns] = (
                buffer[slot, :, columns].astype(F32) * (scale_ref[c, i] if turned else scale_ref[i, c])
            ).astype(BF16)

        @pl.when(i + slots < count)
        def _():
            fetch(i + slots).start()

        return carry

    lax.fori_loop(0, count, body, 0)


def weight(code, scale, turned):
    slots = 6
    scale = scale.T if turned else scale
    return pl.pallas_call(
        functools.partial(weight_kernel, turned),
        in_specs=[pl.BlockSpec(memory_space=pltpu.HBM), SMEM],
        out_specs=VMEM,
        out_shape=pltpu.VMEM(code.shape, BF16),
        scratch_shapes=[
            pltpu.VMEM((slots, BLOCK, code.shape[1]), BF16),
            pltpu.SemaphoreType.DMA((slots,)),
        ],
        compiler_params=pltpu.CompilerParams(vmem_limit_bytes=10 << 20),
        cost_estimate=pl.CostEstimate(
            flops=0, bytes_accessed=code.size // 4096, transcendentals=0
        ),
        name="scaled_weight",
    )(pltpu.with_memory_space_constraint(code, pltpu.HBM), scale)


def prep_kernel(rows, where_ref, inputs_ref, cotangent_ref, *refs):
    *out_refs, sem = refs
    count = inputs_ref.shape[0] // CHUNKS // rows
    copies = []
    for at, out_ref in enumerate(out_refs):
        for q in range(count):
            start = pl.multiple_of((at // 2 * count + (where_ref[0] ^ q)) * rows, rows)
            copies.append(
                pltpu.make_async_copy(
                    (inputs_ref, cotangent_ref)[at % 2].at[pl.ds(start, rows)],
                    out_ref.at[pl.ds(q * rows, rows)],
                    sem.at[len(copies)],
                )
            )
            copies[-1].start()
    for copy in copies:
        copy.wait()


def prepare(where, inputs, cotangent, n_dp):
    seq, width = inputs.shape
    return pl.pallas_call(
        functools.partial(prep_kernel, seq // CHUNKS // n_dp),
        in_specs=[SMEM] + [pl.BlockSpec(memory_space=pltpu.HBM)] * 2,
        out_specs=[VMEM] * (2 * CHUNKS),
        out_shape=[array(seq // CHUNKS, width)] * (2 * CHUNKS),
        scratch_shapes=[pltpu.SemaphoreType.DMA((2 * CHUNKS * n_dp,))],
        compiler_params=PARAMS,
        name="order_rows",
    )(
        where,
        pltpu.with_memory_space_constraint(inputs, pltpu.HBM),
        pltpu.with_memory_space_constraint(cotangent, pltpu.HBM),
    )


def join_kernel(*refs):
    *part_refs, out_ref = refs
    width = part_refs[0].shape[1]
    for j, part_ref in enumerate(part_refs):
        out_ref[:, j * width : (j + 1) * width] = part_ref[...]


def join(parts):
    rows, width = parts[0].shape
    return pl.pallas_call(
        join_kernel,
        in_specs=[VMEM] * len(parts),
        out_specs=VMEM,
        out_shape=array(rows, width * len(parts)),
        compiler_params=PARAMS,
        name="join",
    )(*parts)


def join_four_kernel(where_ref, own_ref, two_ref, near_ref, middle_ref, passed_ref, out_ref):
    width = own_ref.shape[1]
    place = where_ref[1]
    out_ref[:, :width] = own_ref[...]
    out_ref[:, 2 * width : 3 * width] = two_ref[...]
    odd = lax.rem(place, 2)
    out_ref[:, pl.ds(pl.multiple_of((1 + 2 * odd) * width, width), width)] = near_ref[...]
    rest = pl.ds(pl.multiple_of((3 - 2 * odd) * width, width), width)
    inner = jnp.logical_or(place == 1, place == 2)

    @pl.when(inner)
    def _():
        out_ref[:, rest] = middle_ref[...]

    @pl.when(jnp.logical_not(inner))
    def _():
        out_ref[:, rest] = passed_ref[...]


def join_four(where, parts):
    rows, width = parts[0].shape
    return pl.pallas_call(
        join_four_kernel,
        in_specs=[SMEM] + [VMEM] * len(parts),
        out_specs=VMEM,
        out_shape=array(rows, 4 * width),
        compiler_params=PARAMS,
        name="join",
    )(where, *parts)


def assemble(width, blocks, where_ref, x_refs, x_all):
    rows = x_all.shape[0] // blocks
    for q in range(blocks):
        start = pl.multiple_of(block_of(q, blocks, where_ref[2]) * rows, rows)
        own = slice(q * rows, (q + 1) * rows)
        if len(x_refs) == 1:
            x_all[own] = x_refs[0][pl.ds(start, rows)]
            continue
        count = x_all.shape[1] // (CORES * width)
        for j in range(count):
            for core, x_ref in enumerate(x_refs):
                place = lax.rem(where_ref[1] + j, count) * CORES + (where_ref[2] ^ core)
                x_all[own, pl.ds(pl.multiple_of(place * width, width), width)] = x_ref[
                    pl.ds(start, rows), j * width : (j + 1) * width
                ]


def forward_kernel(groups, contract, width, count, where_ref, *refs):
    outs = len(groups)
    x_refs, weight_refs = refs[: -outs - 1 - count], refs[-outs - 1 - count : -outs - 1]
    out_refs, x_all = refs[-outs - 1 : -1], refs[-1]
    blocks = sum(len(group) for group in groups)
    assemble(width, blocks, where_ref, x_refs, x_all)
    columns = out_refs[0].shape[1] // count
    rows = x_all.shape[0] // blocks
    tile = tile_of(columns, 512)
    for at, weight_ref in enumerate(weight_refs):
        for n in range(0, columns, tile):
            part = weight_ref[n : n + tile, :] if contract else weight_ref[:, n : n + tile]
            total = dot(x_all[...], part, contract).astype(BF16)
            place = slice(at * columns + n, at * columns + n + tile)
            for out_ref, group in zip(out_refs, groups):
                for i, q in enumerate(group):
                    out_ref[i * rows : (i + 1) * rows, place] = total[q * rows : (q + 1) * rows]


def forward(where, x, weights, groups, contract, width):
    rows, blocks = x[0].shape[0], sum(len(group) for group in groups)
    depth, columns = weights[0].shape[contract], weights[0].shape[1 - contract]
    outs = [array(rows * len(group) // blocks, columns * len(weights)) for group in groups]
    return pl.pallas_call(
        functools.partial(forward_kernel, groups, contract, width, len(weights)),
        in_specs=[SMEM] + [VMEM] * (len(x) + len(weights)),
        out_specs=[VMEM] * len(outs),
        out_shape=outs,
        scratch_shapes=[pltpu.VMEM((rows, depth), BF16)],
        compiler_params=PARAMS,
        cost_estimate=cost(rows, depth, columns),
        name="forward_product",
    )(where, *x, *(pltpu.with_memory_space_constraint(part, pltpu.VMEM) for part in weights))


def streamed_kernel(groups, width, where_ref, scale_ref, *refs):
    outs = len(groups)
    x_refs, code_ref = refs[: -outs - 4], refs[-outs - 4]
    out_refs, (x_all, buffer, sems) = refs[-outs - 3 : -3], refs[-3:]
    slots, tile, depth = buffer.shape
    count = code_ref.shape[0] // tile
    blocks = sum(len(group) for group in groups)
    rows = x_all.shape[0] // blocks
    step = tile_of(depth, 512)

    def fetch(i):
        slot = lax.rem(i, slots)
        return pltpu.make_async_copy(
            code_ref.at[pl.ds(pl.multiple_of(i * tile, tile), tile)], buffer.at[slot], sems.at[slot]
        )

    for i in range(min(slots, count)):
        fetch(i).start()
    assemble(width, blocks, where_ref, x_refs, x_all)

    def body(i, carry):
        fetch(i).wait()
        slot = lax.rem(i, slots)
        total = None
        for k in range(0, depth, step):
            lines = []
            for r in range(tile // BLOCK):
                lines.append(
                    jnp.concatenate(
                        [
                            (
                                buffer[slot, r * BLOCK : (r + 1) * BLOCK, c : c + BLOCK].astype(F32)
                                * scale_ref[i * (tile // BLOCK) + r, c // BLOCK]
                            ).astype(BF16)
                            for c in range(k, k + step, BLOCK)
                        ],
                        axis=1,
                    )
                )
            term = dot(x_all[:, k : k + step], jnp.concatenate(lines, axis=0), 1)
            total = term if total is None else total + term
        total = total.astype(BF16)
        columns = pl.ds(pl.multiple_of(i * tile, tile), tile)
        for out_ref, group in zip(out_refs, groups):
            for at, q in enumerate(group):
                out_ref[at * rows : (at + 1) * rows, columns] = total[q * rows : (q + 1) * rows]

        @pl.when(i + slots < count)
        def _():
            fetch(i + slots).start()

        return carry

    lax.fori_loop(0, count, body, 0)


def forward_streamed(where, x, code, scale, groups, width):
    rows, blocks = x[0].shape[0], sum(len(group) for group in groups)
    columns, depth = code.shape
    tile, slots = tile_of(columns, 256), 3
    return pl.pallas_call(
        functools.partial(streamed_kernel, groups, width),
        in_specs=[SMEM] * 2 + [VMEM] * len(x) + [pl.BlockSpec(memory_space=pltpu.HBM)],
        out_specs=[VMEM] * len(groups),
        out_shape=[array(rows * len(group) // blocks, columns) for group in groups],
        scratch_shapes=[
            pltpu.VMEM((rows, depth), BF16),
            pltpu.VMEM((slots, tile, depth), BF16),
            pltpu.SemaphoreType.DMA((slots,)),
        ],
        compiler_params=pltpu.CompilerParams(vmem_limit_bytes=14 << 20),
        cost_estimate=cost(rows, depth, columns),
        name="forward_streamed",
    )(where, scale, *x, pltpu.with_memory_space_constraint(code, pltpu.HBM))


def grads_kernel(both, where_ref, *refs):
    *in_refs, out_ref = refs
    rows, width = out_ref.shape[0], out_ref.shape[1] // 2
    tile = tile_of(width, 512)

    def total(terms, n):
        values = [term[term.shape[0] - rows :, n : n + tile].astype(F32) for term in terms]
        return functools.reduce(lambda left, right: left + right, values)

    for n in range(0, width, tile):
        gate_pre = total(in_refs[:both], n)
        up_pre = total(in_refs[:both], width + n)
        hidden_grad = total(in_refs[both:], n)
        gate_sig = jax.nn.sigmoid(gate_pre)
        out_ref[:, n : n + tile] = (
            hidden_grad * up_pre * gate_sig * (1.0 + gate_pre * (1.0 - gate_sig))
        ).astype(BF16)
        out_ref[:, width + n : width + n + tile] = (hidden_grad * gate_pre * gate_sig).astype(BF16)


def grads(where, gate_up, hidden_terms, rows, width):
    return pl.pallas_call(
        functools.partial(grads_kernel, len(gate_up)),
        in_specs=[SMEM] + [VMEM] * (len(gate_up) + len(hidden_terms)),
        out_specs=VMEM,
        out_shape=array(rows, 2 * width),
        compiler_params=PARAMS,
        name="hidden_grads",
    )(where, *gate_up, *hidden_terms)


def backward_kernel(places, total_places, where_ref, *refs):
    outs = CORES if total_places else 1
    *grad_refs, gate_ref, up_ref = refs[: -3 - outs]
    *out_refs, gate_all, up_all, total_ref = refs[-3 - outs :]
    blocks, rows = len(grad_refs), grad_refs[0].shape[0]
    depth = gate_all.shape[1]
    for q, grad_ref in enumerate(grad_refs):
        start = pl.multiple_of(block_of(q, blocks, where_ref[2]) * rows, rows)
        gate_all[pl.ds(start, rows)] = grad_ref[:, :depth]
        up_all[pl.ds(start, rows)] = grad_ref[:, depth:]
    tile = total_ref.shape[1]
    for at, j in enumerate(places):
        place = lax.rem(where_ref[1] + j, total_places) if total_places else j
        part = pl.ds(pl.multiple_of(place * tile, tile), tile)
        total = dot(gate_all[...], gate_ref[part, :], 1) + dot(up_all[...], up_ref[part, :], 1)
        if total_places:
            width = tile // CORES
            total_ref[...] = total.astype(BF16)
            for out_ref, core in zip(out_refs, (where_ref[2], 1 - where_ref[2])):
                out_ref[:, at * width : (at + 1) * width] = total_ref[
                    :, pl.ds(pl.multiple_of(core * width, width), width)
                ]
        else:
            out_refs[0][:, at * tile : (at + 1) * tile] = total.astype(BF16)


def backward(where, grad_parts, gate_weight, up_weight, places, total_places):
    columns, depth = gate_weight.shape
    rows = grad_parts[0].shape[0] * len(grad_parts)
    outs = CORES if total_places else 1
    tile = columns // total_places if total_places else tile_of(columns, 512)
    places = places if total_places else range(columns // tile)
    return pl.pallas_call(
        functools.partial(backward_kernel, places, total_places),
        in_specs=[SMEM] + [VMEM] * (len(grad_parts) + 2),
        out_specs=[VMEM] * outs,
        out_shape=[array(rows, tile * len(places) // outs)] * outs,
        scratch_shapes=[pltpu.VMEM((rows, depth), BF16)] * 2 + [pltpu.VMEM((rows, tile), BF16)],
        compiler_params=PARAMS,
        cost_estimate=cost(rows, 2 * depth, tile * len(places)),
        name="backward_product",
    )(
        where,
        *grad_parts,
        pltpu.with_memory_space_constraint(gate_weight, pltpu.VMEM),
        pltpu.with_memory_space_constraint(up_weight, pltpu.VMEM),
    )


def pair_kernel(own_ref, other_ref, *out_refs):
    width = out_refs[0].shape[1]
    for j, out_ref in enumerate(out_refs):
        columns = slice(j * width, (j + 1) * width)
        out_ref[...] = (own_ref[:, columns].astype(F32) + other_ref[:, columns].astype(F32)).astype(
            BF16
        )


def pair_sums(own, other, count, width):
    rows = own.shape[0]
    return pl.pallas_call(
        pair_kernel,
        in_specs=[VMEM] * 2,
        out_specs=[VMEM] * count,
        out_shape=[array(rows, width)] * count,
        compiler_params=PARAMS,
        name="pair_sums",
    )(own, other)


def final_kernel(blocks, done, where_ref, *refs):
    done_refs, in_refs, out_ref = refs[:done], refs[done:-1], refs[-1]
    rows = in_refs[0].shape[0] // blocks
    width = out_ref.shape[1]
    at = 0
    for done_ref in done_refs:
        out_ref[at : at + done_ref.shape[0]] = done_ref[...]
        at += done_ref.shape[0]
    for q in range(blocks):
        total = None
        for ref in in_refs:
            value = ref[q * rows : (q + 1) * rows, ref.shape[1] - width :].astype(F32)
            total = value if total is None else total + value
        start = pl.multiple_of(at + (where_ref[0] ^ q) * rows, rows)
        out_ref[pl.ds(start, rows)] = total.astype(BF16)


def final_sum(where, done, terms, blocks, width):
    rows = terms[0].shape[0] + sum(part.shape[0] for part in done)
    return pl.pallas_call(
        functools.partial(final_kernel, blocks, len(done)),
        in_specs=[SMEM] + [VMEM] * (len(done) + len(terms)),
        out_specs=VMEM,
        out_shape=array(rows, width),
        compiler_params=PARAMS,
        name="final_sum",
    )(where, *done, *terms)


def local(
    n_tp, n_dp, inputs, cotangent, gate_code, gate_scale, up_code, up_scale, down_code, down_scale
):
    n_z = n_tp // CORES
    width = inputs.shape[1]
    hidden = gate_code.shape[1]
    steps = n_dp.bit_length() - 1
    by_blocks = width % BLOCK == 0
    tp = lax.axis_index("tp")
    where = jnp.stack([lax.axis_index("dp"), tp // CORES, tp % CORES]).astype(jnp.int32)

    def exchange(value, step):
        pairs = []
        for i in range(n_tp):
            bit = 1 << (step if i % CORES == 0 else steps - 1 - step)
            pairs += [(i * n_dp + k, i * n_dp + (k ^ bit)) for k in range(n_dp)]
        return lax.ppermute(value, ("tp", "dp"), pairs)

    def swap_cores(value):
        return lax.ppermute(value, "tp", [(i, i ^ 1) for i in range(n_tp)])

    def along(value, places):
        return lax.ppermute(
            value, "tp", [(i, (i + places * CORES) % n_tp) for i in range(n_tp)]
        )

    def between(value, pairs):
        return lax.ppermute(
            value,
            "tp",
            [(i * CORES + c, k * CORES + c) for i, k in pairs for c in range(CORES)],
        )

    hops = by_blocks and n_z == 4

    def set_out(piece):
        if not by_blocks:
            return [lax.all_gather(piece, "tp", axis=1, tiled=True)]
        if hops:
            return [along(piece, 2)]
        return [along(piece, n_z - j) for j in range(1, n_z)]

    def near(piece, got):
        return [*got, between(piece, [(0, 1), (1, 0), (2, 3), (3, 2)])] if hops else got

    def pass_on(piece, got):
        if not hops:
            return got
        return [*got, between(piece, [(1, 2), (2, 1)]), between(got[0], [(1, 0), (2, 3)])]

    def arrive(piece, got):
        if not by_blocks:
            return got
        own = join_four(where, (piece, *got)) if hops else join([piece, *got])
        return [own, swap_cores(own)]

    groups, stays = [[0]], [0]
    for step in reversed(range(steps)):
        groups.insert(0, [q | 1 << step for q in stays])
        stays = groups[0] + stays

    def send(parts, step=0):
        return [*parts, exchange(parts[step], step)]

    def take(parts, step=0):
        parts, at = list(parts), 0
        for later in range(step + 1, steps):
            height = parts[later].shape[0]
            came = parts[-1][at : at + height].astype(F32)
            parts[later] = (parts[later].astype(F32) + came).astype(BF16)
            at += height
        return parts

    def settle(parts):
        for step in range(1, steps):
            parts = send(take(parts, step - 1), step)
        return parts

    def terms_of(parts):
        return parts[steps:]

    def start_rows(value):
        return (
            {0: value, 1: exchange(value, 0)},
            {1 << step: exchange(value, step) for step in range(1, steps)},
        )

    def finish_rows(have, late):
        have = dict(have)
        for step in range(1, steps):
            for q in list(have):
                have[q | 1 << step] = exchange(have[q], step) if q else late[1 << step]
        return [have[q] for q in range(n_dp)]

    whole = [[*range(1, n_z), 0]]
    parts_of_z = [[2], [1, 3], [0]] if hops else whole

    def products(grad_parts, places):
        return backward(
            where, grad_parts, gate_weight, up_weight, places, n_z if by_blocks else 0
        )

    def swapped(partial):
        return [partial[0], swap_cores(partial[1])] if by_blocks else partial

    def sums_of(partial, places):
        away = [j for j in places if j]
        return pair_sums(*partial, len(away), width) if by_blocks and away else []

    def spread(sums, partial, places):
        if not by_blocks:
            return [lax.psum_scatter(partial[0], "tp", scatter_dimension=1, tiled=True)]
        terms = [along(part, j) for j, part in zip([j for j in places if j], sums)]
        return terms + (list(partial) if 0 in places else [])

    def scatter(partial, places):
        return spread(sums_of(partial, places), partial, places)

    rows = inputs.shape[0] // CHUNKS // n_dp

    def hold(values):
        nonlocal where
        values, where = lax.optimization_barrier((values, where))
        return values

    in_1, co_1, in_2, co_2 = prepare(where, inputs, cotangent, n_dp)
    got_in_1 = near(in_1, set_out(in_1))
    gate_weight = weight(gate_code, gate_scale, True)
    gate_weight, got_in_1, co_1 = hold((gate_weight, got_in_1, co_1))

    got_in_1 = pass_on(in_1, got_in_1)
    got_co_1 = near(co_1, set_out(co_1))
    up_weight = weight(up_code, up_scale, True)
    up_weight, got_in_1, got_co_1 = hold((up_weight, got_in_1, got_co_1))

    x = arrive(in_1, got_in_1)
    got_co_1 = pass_on(co_1, got_co_1)
    gate_up_1 = forward(where, x, [gate_weight, up_weight], groups, 0, width)
    gate_up_1, got_co_1, in_2 = hold((gate_up_1, got_co_1, in_2))

    gate_up_1 = send(gate_up_1)
    x = arrive(co_1, got_co_1)
    got_in_2 = near(in_2, set_out(in_2))
    hidden_1 = forward_streamed(where, x, down_code, down_scale, groups, width)
    hidden_1, gate_up_1, got_in_2, co_2 = hold((hidden_1, gate_up_1, got_in_2, co_2))

    hidden_1 = send(hidden_1)
    got_co_2 = near(co_2, set_out(co_2))
    got_in_2 = hold(pass_on(in_2, got_in_2))

    gate_up_1 = settle(gate_up_1)
    x = arrive(in_2, got_in_2)
    x, hidden_1, got_co_2 = hold((x, hidden_1, got_co_2))

    hidden_1 = settle(hidden_1)
    got_co_2 = pass_on(co_2, got_co_2)
    gate_up_2 = forward(where, x, [gate_weight, up_weight], groups, 0, width)
    gate_up_2, got_co_2, gate_up_1, hidden_1 = hold((gate_up_2, got_co_2, gate_up_1, hidden_1))

    gate_up_2 = send(gate_up_2)
    grad_1 = grads(where, terms_of(gate_up_1), terms_of(hidden_1), rows, hidden)
    x, grad_1 = hold((arrive(co_2, got_co_2), grad_1))

    early_1, late_1 = start_rows(grad_1)
    hidden_2 = forward_streamed(where, x, down_code, down_scale, groups, width)
    hidden_2 = hold(hidden_2)

    hidden_2 = send(hidden_2)
    early_1, gate_up_2 = hold((early_1, gate_up_2))

    parts_1 = finish_rows(early_1, late_1)
    parts_1, hidden_2 = hold((parts_1, hidden_2))

    hidden_2 = settle(hidden_2)
    gate_up_2 = settle(gate_up_2)
    partial_1 = products(parts_1, whole[0])
    hidden_2, gate_up_2, partial_1 = hold((hidden_2, gate_up_2, partial_1))

    partial_1 = swapped(partial_1)
    grad_2 = grads(where, terms_of(gate_up_2), terms_of(hidden_2), rows, hidden)
    early_2, late_2 = start_rows(grad_2)
    terms_1 = scatter(partial_1, whole[0])
    early_2, early = hold((early_2, terms_1[:1]))
    parts_2 = finish_rows(early_2, late_2)
    parts_2, later = hold((parts_2, terms_1[1:2]))
    terms_1 = [*early, *later, *terms_1[2:]]

    terms_2 = []
    partial, before = products(parts_2, parts_of_z[0]), parts_of_z[0]
    for places in parts_of_z[1:]:
        following = products(parts_2, places) if len(places) > 1 else None
        partial, following, terms_1 = hold((swapped(partial), following, terms_1))
        sums = hold(sums_of(partial, before))
        terms_2 += spread(sums, partial, before)
        partial = following or products(parts_2, places)
        before = places
    partial = swapped(partial)
    terms_2 += spread(sums_of(partial, before), partial, before)
    done = [final_sum(where, [], terms_1, n_dp, width)]
    return final_sum(where, done, terms_2, n_dp, width)


def solution(mesh):
    placed = (
        P("groups", ("dp", "tp")),
        P("groups", ("dp", "tp")),
        P("dp", "tp"),
        P("dp", "tp"),
        P("dp", "tp"),
        P("dp", "tp"),
        P("tp", "dp"),
        P("tp", "dp"),
    )
    return jax.shard_map(
        functools.partial(local, mesh.shape["tp"], mesh.shape["dp"]),
        mesh=mesh,
        in_specs=placed,
        out_specs=P("groups", ("dp", "tp")),
        check_vma=False,
    )
```

```python
import functools

import jax
import jax.numpy as jnp
from jax import lax
from jax.experimental import pallas as pl
from jax.experimental.pallas import tpu as pltpu
from jax.sharding import PartitionSpec as P

BLOCK = 128
CORES = 2
CHUNKS = 2
BF16 = jnp.bfloat16
F32 = jnp.float32
PARAMS = pltpu.CompilerParams(vmem_limit_bytes=8 << 20)
VMEM = pl.BlockSpec(memory_space=pltpu.VMEM)
SMEM = pl.BlockSpec(memory_space=pltpu.SMEM)


def tile_of(extent, most):
    best = BLOCK
    for size in range(BLOCK, most + 1, BLOCK):
        if extent % size == 0:
            best = size
    return best


def dot(left, right, contract):
    return lax.dot_general(
        left, right, (((1,), (contract,)), ((), ())), preferred_element_type=F32
    )


def cost(rows, depth, columns):
    return pl.CostEstimate(
        flops=1024, bytes_accessed=1024, transcendentals=0
    )


def array(rows, columns):
    return jax.ShapeDtypeStruct((rows, columns), BF16)


def reversed_bits(q, count):
    width = count.bit_length() - 1
    return sum(((q >> i) & 1) << (width - 1 - i) for i in range(width))


def block_of(q, count, core):
    return q + core * (reversed_bits(q, count) - q)


def weight_kernel(turned, code_ref, scale_ref, weight_ref, buffer, sems):
    slots, rows = buffer.shape[:2]
    count = code_ref.shape[0] // rows

    def fetch(i):
        slot = lax.rem(i, slots)
        return pltpu.make_async_copy(
            code_ref.at[pl.ds(pl.multiple_of(i * rows, rows), rows)], buffer.at[slot], sems.at[slot]
        )

    for i in range(min(slots, count)):
        fetch(i).start()

    def body(i, carry):
        fetch(i).wait()
        slot = lax.rem(i, slots)
        start = pl.multiple_of(i * rows, rows)
        for c in range(code_ref.shape[1] // BLOCK):
            columns = slice(c * BLOCK, (c + 1) * BLOCK)
            weight_ref[pl.ds(start, rows), columns] = (
                buffer[slot, :, columns].astype(F32) * (scale_ref[c, i] if turned else scale_ref[i, c])
            ).astype(BF16)

        @pl.when(i + slots < count)
        def _():
            fetch(i + slots).start()

        return carry

    lax.fori_loop(0, count, body, 0)


def weight(code, scale, turned):
    slots = 6
    scale = scale.T if turned else scale
    return pl.pallas_call(
        functools.partial(weight_kernel, turned),
        in_specs=[pl.BlockSpec(memory_space=pltpu.HBM), SMEM],
        out_specs=VMEM,
        out_shape=pltpu.VMEM(code.shape, BF16),
        scratch_shapes=[
            pltpu.VMEM((slots, BLOCK, code.shape[1]), BF16),
            pltpu.SemaphoreType.DMA((slots,)),
        ],
        compiler_params=pltpu.CompilerParams(vmem_limit_bytes=10 << 20),
        cost_estimate=pl.CostEstimate(
            flops=0, bytes_accessed=code.size // 4096, transcendentals=0
        ),
        name="scaled_weight",
    )(pltpu.with_memory_space_constraint(code, pltpu.HBM), scale)


def prep_kernel(rows, where_ref, inputs_ref, cotangent_ref, *refs):
    *out_refs, sem = refs
    count = inputs_ref.shape[0] // CHUNKS // rows
    copies = []
    for at, out_ref in enumerate(out_refs):
        for q in range(count):
            start = pl.multiple_of((at // 2 * count + (where_ref[0] ^ q)) * rows, rows)
            copies.append(
                pltpu.make_async_copy(
                    (inputs_ref, cotangent_ref)[at % 2].at[pl.ds(start, rows)],
                    out_ref.at[pl.ds(q * rows, rows)],
                    sem.at[len(copies)],
                )
            )
            copies[-1].start()
    for copy in copies:
        copy.wait()


def prepare(where, inputs, cotangent, n_dp):
    seq, width = inputs.shape
    return pl.pallas_call(
        functools.partial(prep_kernel, seq // CHUNKS // n_dp),
        in_specs=[SMEM] + [pl.BlockSpec(memory_space=pltpu.HBM)] * 2,
        out_specs=[VMEM] * (2 * CHUNKS),
        out_shape=[array(seq // CHUNKS, width)] * (2 * CHUNKS),
        scratch_shapes=[pltpu.SemaphoreType.DMA((2 * CHUNKS * n_dp,))],
        compiler_params=PARAMS,
        name="order_rows",
    )(
        where,
        pltpu.with_memory_space_constraint(inputs, pltpu.HBM),
        pltpu.with_memory_space_constraint(cotangent, pltpu.HBM),
    )


def join_kernel(*refs):
    *part_refs, out_ref = refs
    width = part_refs[0].shape[1]
    for j, part_ref in enumerate(part_refs):
        out_ref[:, j * width : (j + 1) * width] = part_ref[...]


def join(parts):
    rows, width = parts[0].shape
    return pl.pallas_call(
        join_kernel,
        in_specs=[VMEM] * len(parts),
        out_specs=VMEM,
        out_shape=array(rows, width * len(parts)),
        compiler_params=PARAMS,
        name="join",
    )(*parts)


def join_four_kernel(where_ref, own_ref, two_ref, near_ref, middle_ref, passed_ref, out_ref):
    width = own_ref.shape[1]
    place = where_ref[1]
    out_ref[:, :width] = own_ref[...]
    out_ref[:, 2 * width : 3 * width] = two_ref[...]
    odd = lax.rem(place, 2)
    out_ref[:, pl.ds(pl.multiple_of((1 + 2 * odd) * width, width), width)] = near_ref[...]
    rest = pl.ds(pl.multiple_of((3 - 2 * odd) * width, width), width)
    inner = jnp.logical_or(place == 1, place == 2)

    @pl.when(inner)
    def _():
        out_ref[:, rest] = middle_ref[...]

    @pl.when(jnp.logical_not(inner))
    def _():
        out_ref[:, rest] = passed_ref[...]


def join_four(where, parts):
    rows, width = parts[0].shape
    return pl.pallas_call(
        join_four_kernel,
        in_specs=[SMEM] + [VMEM] * len(parts),
        out_specs=VMEM,
        out_shape=array(rows, 4 * width),
        compiler_params=PARAMS,
        name="join",
    )(where, *parts)


def assemble(width, blocks, where_ref, x_refs, x_all):
    rows = x_all.shape[0] // blocks
    for q in range(blocks):
        start = pl.multiple_of(block_of(q, blocks, where_ref[2]) * rows, rows)
        own = slice(q * rows, (q + 1) * rows)
        if len(x_refs) == 1:
            x_all[own] = x_refs[0][pl.ds(start, rows)]
            continue
        count = x_all.shape[1] // (CORES * width)
        for j in range(count):
            for core, x_ref in enumerate(x_refs):
                place = lax.rem(where_ref[1] + j, count) * CORES + (where_ref[2] ^ core)
                x_all[own, pl.ds(pl.multiple_of(place * width, width), width)] = x_ref[
                    pl.ds(start, rows), j * width : (j + 1) * width
                ]


def forward_kernel(groups, contract, width, count, where_ref, *refs):
    outs = len(groups)
    x_refs, weight_refs = refs[: -outs - 1 - count], refs[-outs - 1 - count : -outs - 1]
    out_refs, x_all = refs[-outs - 1 : -1], refs[-1]
    blocks = sum(len(group) for group in groups)
    assemble(width, blocks, where_ref, x_refs, x_all)
    columns = out_refs[0].shape[1] // count
    rows = x_all.shape[0] // blocks
    tile = tile_of(columns, 512)
    for at, weight_ref in enumerate(weight_refs):
        for n in range(0, columns, tile):
            part = weight_ref[n : n + tile, :] if contract else weight_ref[:, n : n + tile]
            total = dot(x_all[...], part, contract).astype(BF16)
            place = slice(at * columns + n, at * columns + n + tile)
            for out_ref, group in zip(out_refs, groups):
                for i, q in enumerate(group):
                    out_ref[i * rows : (i + 1) * rows, place] = total[q * rows : (q + 1) * rows]


def forward(where, x, weights, groups, contract, width):
    rows, blocks = x[0].shape[0], sum(len(group) for group in groups)
    depth, columns = weights[0].shape[contract], weights[0].shape[1 - contract]
    outs = [array(rows * len(group) // blocks, columns * len(weights)) for group in groups]
    return pl.pallas_call(
        functools.partial(forward_kernel, groups, contract, width, len(weights)),
        in_specs=[SMEM] + [VMEM] * (len(x) + len(weights)),
        out_specs=[VMEM] * len(outs),
        out_shape=outs,
        scratch_shapes=[pltpu.VMEM((rows, depth), BF16)],
        compiler_params=PARAMS,
        cost_estimate=cost(rows, depth, columns),
        name="forward_product",
    )(where, *x, *(pltpu.with_memory_space_constraint(part, pltpu.VMEM) for part in weights))


def streamed_kernel(groups, width, where_ref, scale_ref, *refs):
    outs = len(groups)
    x_refs, code_ref = refs[: -outs - 4], refs[-outs - 4]
    out_refs, (x_all, buffer, sems) = refs[-outs - 3 : -3], refs[-3:]
    slots, tile, depth = buffer.shape
    count = code_ref.shape[0] // tile
    blocks = sum(len(group) for group in groups)
    rows = x_all.shape[0] // blocks
    step = tile_of(depth, 512)

    def fetch(i):
        slot = lax.rem(i, slots)
        return pltpu.make_async_copy(
            code_ref.at[pl.ds(pl.multiple_of(i * tile, tile), tile)], buffer.at[slot], sems.at[slot]
        )

    for i in range(min(slots, count)):
        fetch(i).start()
    assemble(width, blocks, where_ref, x_refs, x_all)

    def body(i, carry):
        fetch(i).wait()
        slot = lax.rem(i, slots)
        total = None
        for k in range(0, depth, step):
            lines = []
            for r in range(tile // BLOCK):
                lines.append(
                    jnp.concatenate(
                        [
                            (
                                buffer[slot, r * BLOCK : (r + 1) * BLOCK, c : c + BLOCK].astype(F32)
                                * scale_ref[i * (tile // BLOCK) + r, c // BLOCK]
                            ).astype(BF16)
                            for c in range(k, k + step, BLOCK)
                        ],
                        axis=1,
                    )
                )
            term = dot(x_all[:, k : k + step], jnp.concatenate(lines, axis=0), 1)
            total = term if total is None else total + term
        total = total.astype(BF16)
        columns = pl.ds(pl.multiple_of(i * tile, tile), tile)
        for out_ref, group in zip(out_refs, groups):
            for at, q in enumerate(group):
                out_ref[at * rows : (at + 1) * rows, columns] = total[q * rows : (q + 1) * rows]

        @pl.when(i + slots < count)
        def _():
            fetch(i + slots).start()

        return carry

    lax.fori_loop(0, count, body, 0)


def forward_streamed(where, x, code, scale, groups, width):
    rows, blocks = x[0].shape[0], sum(len(group) for group in groups)
    columns, depth = code.shape
    tile, slots = tile_of(columns, 256), 3
    return pl.pallas_call(
        functools.partial(streamed_kernel, groups, width),
        in_specs=[SMEM] * 2 + [VMEM] * len(x) + [pl.BlockSpec(memory_space=pltpu.HBM)],
        out_specs=[VMEM] * len(groups),
        out_shape=[array(rows * len(group) // blocks, columns) for group in groups],
        scratch_shapes=[
            pltpu.VMEM((rows, depth), BF16),
            pltpu.VMEM((slots, tile, depth), BF16),
            pltpu.SemaphoreType.DMA((slots,)),
        ],
        compiler_params=pltpu.CompilerParams(vmem_limit_bytes=14 << 20),
        cost_estimate=cost(rows, depth, columns),
        name="forward_streamed",
    )(where, scale, *x, pltpu.with_memory_space_constraint(code, pltpu.HBM))


def grads_kernel(both, where_ref, *refs):
    *in_refs, out_ref = refs
    rows, width = out_ref.shape[0], out_ref.shape[1] // 2
    tile = tile_of(width, 512)

    def total(terms, n):
        values = [term[term.shape[0] - rows :, n : n + tile].astype(F32) for term in terms]
        return functools.reduce(lambda left, right: left + right, values)

    for n in range(0, width, tile):
        gate_pre = total(in_refs[:both], n)
        up_pre = total(in_refs[:both], width + n)
        hidden_grad = total(in_refs[both:], n)
        gate_sig = jax.nn.sigmoid(gate_pre)
        out_ref[:, n : n + tile] = (
            hidden_grad * up_pre * gate_sig * (1.0 + gate_pre * (1.0 - gate_sig))
        ).astype(BF16)
        out_ref[:, width + n : width + n + tile] = (hidden_grad * gate_pre * gate_sig).astype(BF16)


def grads(where, gate_up, hidden_terms, rows, width):
    return pl.pallas_call(
        functools.partial(grads_kernel, len(gate_up)),
        in_specs=[SMEM] + [VMEM] * (len(gate_up) + len(hidden_terms)),
        out_specs=VMEM,
        out_shape=array(rows, 2 * width),
        compiler_params=PARAMS,
        name="hidden_grads",
    )(where, *gate_up, *hidden_terms)


def backward_kernel(places, total_places, where_ref, *refs):
    outs = CORES if total_places else 1
    *grad_refs, gate_ref, up_ref = refs[: -3 - outs]
    *out_refs, gate_all, up_all, total_ref = refs[-3 - outs :]
    blocks, rows = len(grad_refs), grad_refs[0].shape[0]
    depth = gate_all.shape[1]
    for q, grad_ref in enumerate(grad_refs):
        start = pl.multiple_of(block_of(q, blocks, where_ref[2]) * rows, rows)
        gate_all[pl.ds(start, rows)] = grad_ref[:, :depth]
        up_all[pl.ds(start, rows)] = grad_ref[:, depth:]
    tile = total_ref.shape[1]
    for at, j in enumerate(places):
        place = lax.rem(where_ref[1] + j, total_places) if total_places else j
        part = pl.ds(pl.multiple_of(place * tile, tile), tile)
        total = dot(gate_all[...], gate_ref[part, :], 1) + dot(up_all[...], up_ref[part, :], 1)
        if total_places:
            width = tile // CORES
            total_ref[...] = total.astype(BF16)
            for out_ref, core in zip(out_refs, (where_ref[2], 1 - where_ref[2])):
                out_ref[:, at * width : (at + 1) * width] = total_ref[
                    :, pl.ds(pl.multiple_of(core * width, width), width)
                ]
        else:
            out_refs[0][:, at * tile : (at + 1) * tile] = total.astype(BF16)


def backward(where, grad_parts, gate_weight, up_weight, places, total_places):
    columns, depth = gate_weight.shape
    rows = grad_parts[0].shape[0] * len(grad_parts)
    outs = CORES if total_places else 1
    tile = columns // total_places if total_places else tile_of(columns, 512)
    places = places if total_places else range(columns // tile)
    return pl.pallas_call(
        functools.partial(backward_kernel, places, total_places),
        in_specs=[SMEM] + [VMEM] * (len(grad_parts) + 2),
        out_specs=[VMEM] * outs,
        out_shape=[array(rows, tile * len(places) // outs)] * outs,
        scratch_shapes=[pltpu.VMEM((rows, depth), BF16)] * 2 + [pltpu.VMEM((rows, tile), BF16)],
        compiler_params=PARAMS,
        cost_estimate=cost(rows, 2 * depth, tile * len(places)),
        name="backward_product",
    )(
        where,
        *grad_parts,
        pltpu.with_memory_space_constraint(gate_weight, pltpu.VMEM),
        pltpu.with_memory_space_constraint(up_weight, pltpu.VMEM),
    )


def pair_kernel(own_ref, other_ref, *out_refs):
    width = out_refs[0].shape[1]
    for j, out_ref in enumerate(out_refs):
        columns = slice(j * width, (j + 1) * width)
        out_ref[...] = (own_ref[:, columns].astype(F32) + other_ref[:, columns].astype(F32)).astype(
            BF16
        )


def pair_sums(own, other, count, width):
    rows = own.shape[0]
    return pl.pallas_call(
        pair_kernel,
        in_specs=[VMEM] * 2,
        out_specs=[VMEM] * count,
        out_shape=[array(rows, width)] * count,
        compiler_params=PARAMS,
        name="pair_sums",
    )(own, other)


def final_kernel(blocks, done, where_ref, *refs):
    done_refs, in_refs, out_ref = refs[:done], refs[done:-1], refs[-1]
    rows = in_refs[0].shape[0] // blocks
    width = out_ref.shape[1]
    at = 0
    for done_ref in done_refs:
        out_ref[at : at + done_ref.shape[0]] = done_ref[...]
        at += done_ref.shape[0]
    for q in range(blocks):
        total = None
        for ref in in_refs:
            value = ref[q * rows : (q + 1) * rows, ref.shape[1] - width :].astype(F32)
            total = value if total is None else total + value
        start = pl.multiple_of(at + (where_ref[0] ^ q) * rows, rows)
        out_ref[pl.ds(start, rows)] = total.astype(BF16)


def final_sum(where, done, terms, blocks, width):
    rows = terms[0].shape[0] + sum(part.shape[0] for part in done)
    return pl.pallas_call(
        functools.partial(final_kernel, blocks, len(done)),
        in_specs=[SMEM] + [VMEM] * (len(done) + len(terms)),
        out_specs=VMEM,
        out_shape=array(rows, width),
        compiler_params=PARAMS,
        name="final_sum",
    )(where, *done, *terms)


def local(
    n_tp, n_dp, inputs, cotangent, gate_code, gate_scale, up_code, up_scale, down_code, down_scale
):
    n_z = n_tp // CORES
    width = inputs.shape[1]
    hidden = gate_code.shape[1]
    steps = n_dp.bit_length() - 1
    by_blocks = width % BLOCK == 0
    tp = lax.axis_index("tp")
    where = jnp.stack([lax.axis_index("dp"), tp // CORES, tp % CORES]).astype(jnp.int32)

    def exchange(value, step):
        pairs = []
        for i in range(n_tp):
            bit = 1 << (step if i % CORES == 0 else steps - 1 - step)
            pairs += [(i * n_dp + k, i * n_dp + (k ^ bit)) for k in range(n_dp)]
        return lax.ppermute(value, ("tp", "dp"), pairs)

    def swap_cores(value):
        return lax.ppermute(value, "tp", [(i, i ^ 1) for i in range(n_tp)])

    def along(value, places):
        return lax.ppermute(
            value, "tp", [(i, (i + places * CORES) % n_tp) for i in range(n_tp)]
        )

    def between(value, pairs):
        return lax.ppermute(
            value,
            "tp",
            [(i * CORES + c, k * CORES + c) for i, k in pairs for c in range(CORES)],
        )

    hops = by_blocks and n_z == 4

    def set_out(piece):
        if not by_blocks:
            return [lax.all_gather(piece, "tp", axis=1, tiled=True)]
        if hops:
            return [along(piece, 2)]
        return [along(piece, n_z - j) for j in range(1, n_z)]

    def near(piece, got):
        return [*got, between(piece, [(0, 1), (1, 0), (2, 3), (3, 2)])] if hops else got

    def pass_on(piece, got):
        if not hops:
            return got
        return [*got, between(piece, [(1, 2), (2, 1)]), between(got[0], [(1, 0), (2, 3)])]

    def arrive(piece, got):
        if not by_blocks:
            return got
        own = join_four(where, (piece, *got)) if hops else join([piece, *got])
        return [own, swap_cores(own)]

    groups, stays = [[0]], [0]
    for step in reversed(range(steps)):
        groups.insert(0, [q | 1 << step for q in stays])
        stays = groups[0] + stays

    def send(parts, step=0):
        return [*parts, exchange(parts[step], step)]

    def take(parts, step=0):
        parts, at = list(parts), 0
        for later in range(step + 1, steps):
            height = parts[later].shape[0]
            came = parts[-1][at : at + height].astype(F32)
            parts[later] = (parts[later].astype(F32) + came).astype(BF16)
            at += height
        return parts

    def settle(parts):
        for step in range(1, steps):
            parts = send(take(parts, step - 1), step)
        return parts

    def terms_of(parts):
        return parts[steps:]

    def start_rows(value):
        return (
            {0: value, 1: exchange(value, 0)},
            {1 << step: exchange(value, step) for step in range(1, steps)},
        )

    def finish_rows(have, late):
        have = dict(have)
        for step in range(1, steps):
            for q in list(have):
                have[q | 1 << step] = exchange(have[q], step) if q else late[1 << step]
        return [have[q] for q in range(n_dp)]

    whole = [[2, 1, 3, 0] if hops else [*range(1, n_z), 0]]
    parts_of_z = [[2], [1, 3], [0]] if hops else whole

    def products(grad_parts, places):
        return backward(
            where, grad_parts, gate_weight, up_weight, places, n_z if by_blocks else 0
        )

    def swapped(partial):
        return [partial[0], swap_cores(partial[1])] if by_blocks else partial

    def sums_of(partial, places):
        away = [j for j in places if j]
        return pair_sums(*partial, len(away), width) if by_blocks and away else []

    def spread(sums, partial, places):
        if not by_blocks:
            return [lax.psum_scatter(partial[0], "tp", scatter_dimension=1, tiled=True)]
        terms = [along(part, j) for j, part in zip([j for j in places if j], sums)]
        return terms + (list(partial) if 0 in places else [])

    def scatter(partial, places):
        return spread(sums_of(partial, places), partial, places)

    rows = inputs.shape[0] // CHUNKS // n_dp

    def hold(values):
        nonlocal where
        values, where = lax.optimization_barrier((values, where))
        return values

    in_1, co_1, in_2, co_2 = prepare(where, inputs, cotangent, n_dp)
    got_in_1 = near(in_1, set_out(in_1))
    gate_weight = weight(gate_code, gate_scale, True)
    gate_weight, got_in_1, co_1 = hold((gate_weight, got_in_1, co_1))

    got_in_1 = pass_on(in_1, got_in_1)
    got_co_1 = near(co_1, set_out(co_1))
    up_weight = weight(up_code, up_scale, True)
    up_weight, got_in_1, got_co_1 = hold((up_weight, got_in_1, got_co_1))

    x = arrive(in_1, got_in_1)
    got_co_1 = pass_on(co_1, got_co_1)
    gate_up_1 = forward(where, x, [gate_weight, up_weight], groups, 0, width)
    gate_up_1, got_co_1, in_2 = hold((gate_up_1, got_co_1, in_2))

    gate_up_1 = send(gate_up_1)
    x = arrive(co_1, got_co_1)
    got_in_2 = near(in_2, set_out(in_2))
    hidden_1 = forward_streamed(where, x, down_code, down_scale, groups, width)
    hidden_1, gate_up_1, got_in_2, co_2 = hold((hidden_1, gate_up_1, got_in_2, co_2))

    hidden_1 = send(hidden_1)
    got_co_2 = near(co_2, set_out(co_2))
    got_in_2 = hold(pass_on(in_2, got_in_2))

    gate_up_1 = settle(gate_up_1)
    x = arrive(in_2, got_in_2)
    x, hidden_1, got_co_2 = hold((x, hidden_1, got_co_2))

    hidden_1 = settle(hidden_1)
    got_co_2 = pass_on(co_2, got_co_2)
    gate_up_2 = forward(where, x, [gate_weight, up_weight], groups, 0, width)
    gate_up_2, got_co_2, gate_up_1, hidden_1 = hold((gate_up_2, got_co_2, gate_up_1, hidden_1))

    gate_up_2 = send(gate_up_2)
    grad_1 = grads(where, terms_of(gate_up_1), terms_of(hidden_1), rows, hidden)
    x, grad_1 = hold((arrive(co_2, got_co_2), grad_1))

    early_1, late_1 = start_rows(grad_1)
    hidden_2 = forward_streamed(where, x, down_code, down_scale, groups, width)
    hidden_2 = hold(hidden_2)

    hidden_2 = send(hidden_2)
    gate_up_2 = hold(gate_up_2)
    gate_up_2 = settle(gate_up_2)
    early_1 = hold(early_1)

    parts_1 = finish_rows(early_1, late_1)
    parts_1, hidden_2 = hold((parts_1, hidden_2))

    hidden_2 = settle(hidden_2)
    partial_1 = products(parts_1, whole[0])
    hidden_2, gate_up_2, partial_1 = hold((hidden_2, gate_up_2, partial_1))

    partial_1 = swapped(partial_1)
    grad_2 = grads(where, terms_of(gate_up_2), terms_of(hidden_2), rows, hidden)
    early_2, late_2 = start_rows(grad_2)
    terms_1 = scatter(partial_1, whole[0])
    early_2, early = hold((early_2, terms_1[:1]))
    parts_2 = finish_rows(early_2, late_2)
    parts_2, later = hold((parts_2, terms_1[1:2]))
    terms_1 = [*early, *later, *terms_1[2:]]

    terms_2 = []
    partial, before = products(parts_2, parts_of_z[0]), parts_of_z[0]
    for places in parts_of_z[1:]:
        following = products(parts_2, places) if len(places) > 1 else None
        partial, following, terms_1 = hold((swapped(partial), following, terms_1))
        sums = hold(sums_of(partial, before))
        terms_2 += spread(sums, partial, before)
        partial = following or products(parts_2, places)
        before = places
    partial = swapped(partial)
    terms_2 += spread(sums_of(partial, before), partial, before)
    done = [final_sum(where, [], terms_1, n_dp, width)]
    return final_sum(where, done, terms_2, n_dp, width)


def solution(mesh):
    placed = (
        P("groups", ("dp", "tp")),
        P("groups", ("dp", "tp")),
        P("dp", "tp"),
        P("dp", "tp"),
        P("dp", "tp"),
        P("dp", "tp"),
        P("tp", "dp"),
        P("tp", "dp"),
    )
    return jax.shard_map(
        functools.partial(local, mesh.shape["tp"], mesh.shape["dp"]),
        mesh=mesh,
        in_specs=placed,
        out_specs=P("groups", ("dp", "tp")),
        check_vma=False,
    )
```
